32 devices in a mesh: seg: 8 (over y, x, core), cell: 4 (over z).
Axes of the slice: x: 2, y: 2, z: 4, core: 2. Of those that a mesh axis runs over, the one named last changes fastest.
Arguments:
- positions: float32 [128, 3, 512], P(('seg', 'cell')), may hold values from -6 to 6
- rest_shape: float32 [128, 3, 512], P(('seg', 'cell')), may hold values from -6 to 6
- modulus: float32 [128], P(('seg', 'cell')), may hold values from 0.5 to 2
- stiffness: bfloat16 [512, 512], replicated, may hold values from -0.25 to 0.25
- wall_points: float32 [128, 3, 512], P(('seg', 'cell')), may hold values from -6 to 6
- density: float32 [128, 3, 512], P(('seg', 'cell')), may hold values from -6 to 6
- wall_operator: float32 [512, 512], replicated, may hold values from -0.25 to 0.25
- seg_count: int32 [8], P('seg'), may hold values from 1 to 16, as said below
- neighbours: int32 [128, 4], P(('seg', 'cell')), may hold values from 0 to 127, as said below
- near_patches: int32 [128, 2], P(('seg', 'cell')), may hold values from 0 to 127, as said below
Outputs:
- new_positions: float32 [128, 3, 512], P(('seg', 'cell'))
- velocity: float32 [128, 3, 512], P(('seg', 'cell'))
- new_density: float32 [128, 3, 512], P(('seg', 'cell'))
The draws below stay inside these ranges and needn't reach their ends.
Inputs may be any that keep to these rules, and one draw needn't show every extreme that they name: `seg_count`: live cells of a segment take its slots 0 to count - 1; some segment has 16 live cells and some other has 1. `neighbours`: the first entry of cell c is c itself; every other entry is a live cell of the same segment or of a segment next to it. `near_patches`: every entry is a patch of the cell's own segment or of a segment next to it.
All inputs are finite; a program needn't handle non-finite values.
Results may differ from the reference program's by a relative error of at most 0.0037.
Values sent between devices are 32-bit elements; how exact they have to be, the bound alone decides.
No kernel may reach another device: no remote copies, remote signals or barrier semaphores. Data moves between devices by JAX's collectives and lax.ppermute only.
A program may use at most 64 MiB of HBM per device.

```python
import math
import jax
import jax.numpy as jnp
from jax import lax

P_SIZE = 512
Q = 512
NB = 4
NW = 2
STEPS = 2
SEGMENTS = 8
SEG_CELLS = 16
SEG_PATCH = 16
CELLS = 128
PATCHES = 128


def segment_counts(key):
    base_key = jax.random.fold_in(key, 11)
    counts = jax.random.randint(jax.random.fold_in(base_key, 1), (SEGMENTS,), 1, SEG_CELLS + 1)
    fullest = jax.random.randint(jax.random.fold_in(base_key, 2), (), 0, SEGMENTS)
    emptiest = (fullest + 1 + jax.random.randint(jax.random.fold_in(base_key, 3), (), 0, SEGMENTS - 1)) % SEGMENTS
    counts = counts.at[fullest].set(SEG_CELLS).at[emptiest].set(1)
    return counts.astype(jnp.int32)


def draw_seg_count(key, part):
    return segment_counts(key)


def draw_neighbours(key, part):
    counts = segment_counts(key)
    cell_numbers = jnp.arange(CELLS, dtype=jnp.int32)
    home_segment = cell_numbers // SEG_CELLS
    stepped = jax.random.randint(jax.random.fold_in(key, 21), (CELLS, NB - 1), -1, 2)
    target = jnp.clip(home_segment[:, None] + stepped, 0, SEGMENTS - 1)
    random_bits = jax.random.randint(jax.random.fold_in(key, 22), (CELLS, NB - 1), 0, 1 << 20)
    slot_index = random_bits % counts[target]
    others = target * SEG_CELLS + slot_index
    return jnp.concatenate([cell_numbers[:, None], others], axis=1).astype(jnp.int32)


def draw_near_patches(key, part):
    cell_numbers = jnp.arange(CELLS, dtype=jnp.int32)
    home_segment = cell_numbers // SEG_CELLS
    stepped = jax.random.randint(jax.random.fold_in(key, 31), (CELLS, NW), -1, 2)
    target = jnp.clip(home_segment[:, None] + stepped, 0, SEGMENTS - 1)
    random_bits = jax.random.randint(jax.random.fold_in(key, 32), (CELLS, NW), 0, 1 << 20)
    return (target * SEG_PATCH + random_bits % SEG_PATCH).astype(jnp.int32)


def block_scale(key, extent, cuts, smallest, high):
    factor_of, own = 1.0, jax.random.fold_in(key, 6)
    for position, blocks in cuts:
        steps = jnp.exp(jax.random.uniform(jax.random.fold_in(own, position), (blocks,), jnp.float32, smallest / len(cuts), high / len(cuts)))
        factor_of = factor_of * jnp.repeat(steps, extent[position] // blocks).reshape([-1 if axis == position else 1 for axis in range(len(extent))])
    return factor_of


def gaussian(key, shape, deviation, limit, shards=(), kind=jnp.bfloat16):
    values = deviation * jax.random.normal(key, shape, jnp.float32)
    if shards:
        values = values * block_scale(key, shape, shards, -0.22, 0.18)
    return jnp.clip(values, -limit, limit).astype(kind)


def setup_inputs(seed: int = 0) -> dict:
    seeds = jax.random.split(jax.random.key(seed), 11)
    positions = gaussian(seeds[0], (CELLS, 3, P_SIZE), 1.0, 6.0, ((0, 32),), jnp.float32)
    rest_shape = gaussian(seeds[1], (CELLS, 3, P_SIZE), 1.0, 6.0, ((0, 32),), jnp.float32)
    modulus = jnp.clip(jnp.exp(math.log(2.0) - 1.3862944 * jax.random.uniform(seeds[2], (CELLS,), jnp.float32) ** block_scale(seeds[2], (CELLS,), ((0, 32),), -0.2, 0.2)), 0.5, 2.0)
    stiffness = gaussian(seeds[3], (P_SIZE, P_SIZE), P_SIZE ** -0.5, 0.25)
    wall_points = gaussian(seeds[4], (PATCHES, 3, Q), 1.0, 6.0, ((0, 32),), jnp.float32)
    density = gaussian(seeds[5], (PATCHES, 3, Q), 1.0, 6.0, ((0, 32),), jnp.float32)
    wall_operator = gaussian(seeds[6], (Q, Q), Q ** -0.5, 0.25, (), jnp.float32)
    seg_count = draw_seg_count(jax.random.fold_in(seeds[10], 71), 0)
    neighbours = draw_neighbours(jax.random.fold_in(seeds[10], 71), 0)
    near_patches = draw_near_patches(jax.random.fold_in(seeds[10], 71), 0)
    return dict(positions=positions, rest_shape=rest_shape, modulus=modulus, stiffness=stiffness, wall_points=wall_points, density=density, wall_operator=wall_operator, seg_count=seg_count, neighbours=neighbours, near_patches=near_patches)


soften_square = 0.25
stokes_factor = 0.039788735772973836
relax_factor = 0.5
time_step = 0.5
highest = lax.Precision.HIGHEST

def stokeslet(targets, sources, strength):
    apart_one = targets[0][:, None] - sources[0][None, :]
    apart_two = targets[1][:, None] - sources[1][None, :]
    apart_three = targets[2][:, None] - sources[2][None, :]
    inverse = lax.rsqrt(apart_one * apart_one + apart_two * apart_two + apart_three * apart_three + soften_square)
    along_force = apart_one * strength[0][None, :] + apart_two * strength[1][None, :] + apart_three * strength[2][None, :]
    weight = along_force * inverse * inverse * inverse
    direct = jnp.dot(inverse, strength.T, precision=highest)
    moment = jnp.dot(weight, sources.T, precision=highest)
    totals = lax.optimization_barrier(jnp.sum(weight, axis=1))
    return stokes_factor * (direct.T + targets * totals[None, :] - moment.T)

def reference(positions, rest_shape, modulus, stiffness, wall_points, density, wall_operator, seg_count, neighbours, near_patches):
    cell_numbers = jnp.arange(CELLS, dtype=jnp.int32)
    slot_index = cell_numbers % SEG_CELLS
    owner_segment = cell_numbers // SEG_CELLS
    living = (slot_index < seg_count[owner_segment]).astype(jnp.float32)
    stiff_float = stiffness.astype(jnp.float32)
    velocity = jnp.zeros_like(positions)
    for repeat in range(STEPS):
        offset = lax.optimization_barrier((positions - rest_shape).astype(jnp.bfloat16)).astype(jnp.float32)
        pushed = jnp.einsum('ckj,pj->ckp', offset, stiff_float, precision=highest)
        forces = (living * modulus)[:, None, None] * pushed

        def cell_terms(target):
            summed = jnp.zeros((3, P_SIZE), jnp.float32)
            for listed in range(NB):
                source = neighbours[target, listed]
                summed = summed + stokeslet(positions[target], positions[source], forces[source])
            pieces = []
            for listed in range(NW):
                patch_index = near_patches[target, listed]
                summed = summed + stokeslet(positions[target], wall_points[patch_index], density[patch_index])
                pieces.append(stokeslet(wall_points[patch_index], positions[target], forces[target]))
            return (summed, jnp.stack(pieces))
        moving, pieces = lax.map(cell_terms, cell_numbers)
        wall_velocity = jax.ops.segment_sum(pieces.reshape(CELLS * NW, 3, Q), near_patches.reshape(-1), num_segments=PATCHES)
        layered = jnp.einsum('pkj,ij->pki', density, wall_operator, precision=highest)
        density = density - relax_factor * (wall_velocity + 0.5 * density + layered)
        velocity = living[:, None, None] * moving
        positions = positions + time_step * velocity
    return (positions, velocity, density)
```

```python
import functools

import jax
import jax.numpy as jnp
from jax import lax
from jax.experimental import pallas as pl
from jax.experimental.pallas import tpu as pltpu
from jax.sharding import PartitionSpec as P

STEPS = 2
soften_square = 0.25
stokes_factor = 0.039788735772973836
relax_factor = 0.5
time_step = 0.5
bf16 = jnp.bfloat16
f32 = jnp.float32
highest = lax.Precision.HIGHEST


def stack_rows(rows, points):
    place = lax.broadcasted_iota(jnp.int32, (8, points), 0)
    out = jnp.zeros((8, points), f32)
    for number, row in enumerate(rows):
        out = jnp.where(place == number, jnp.broadcast_to(row, (8, points)), out)
    return out


def parts_of(value):
    first = value.astype(bf16).astype(f32)
    rest = value - first
    second = rest.astype(bf16).astype(f32)
    third = (rest - second).astype(bf16).astype(f32)
    return first, second, third


def target_features(x):
    points = x.shape[1]
    ones = jnp.ones((1, points), f32)
    square = jnp.sum(x * x, axis=0, keepdims=True)
    high, middle, low = parts_of(stack_rows([x[0:1], x[1:2], x[2:3], ones, square], points))
    return jnp.concatenate([high, middle, high, low, high, middle], axis=0).astype(bf16)


def source_features(y):
    points = y.shape[1]
    ones = jnp.ones((1, points), f32)
    square = jnp.sum(y * y, axis=0, keepdims=True) + soften_square
    high, middle, low = parts_of(
        stack_rows([-2 * y[0:1], -2 * y[1:2], -2 * y[2:3], square, ones], points)
    )
    wide = jnp.concatenate([high, high, middle, high, low, middle], axis=0)
    return wide.T.astype(bf16)


def source_moments(y, f):
    points = y.shape[1]
    place = lax.broadcasted_iota(jnp.int32, (8, points), 0)
    lower = place < 4
    ones = jnp.ones((1, points), f32)
    spread = lambda row: jnp.broadcast_to(row, (8, points))
    twice = stack_rows([y[0:1], y[1:2], y[2:3], ones, y[0:1], y[1:2], y[2:3], ones], points)
    one = jnp.where(lower, spread(f[0:1]), spread(f[1:2])) * twice
    two = jnp.where(lower, spread(f[2:3]), 0.0) * twice
    along = -jnp.sum(f * y, axis=0, keepdims=True)
    square = jnp.sum(y * y, axis=0, keepdims=True)
    scaled = [along * y[k : k + 1] for k in range(3)]
    pushed = [square * f[k : k + 1] for k in range(3)]
    three = stack_rows(scaled + [jnp.zeros((1, points), f32)] + pushed, points)
    return jnp.concatenate(parts_of(jnp.concatenate([one, two, three], axis=0)), axis=0).astype(bf16)


def pair_sums(features, y, f):
    distance = jnp.dot(source_features(y), features, preferred_element_type=f32)
    inverse = lax.rsqrt(distance)
    cubed = (inverse * inverse * inverse).astype(bf16)
    return jnp.dot(source_moments(y, f), cubed, preferred_element_type=f32)


def combine(sums, x):
    sums = sums[0:24] + sums[24:48] + sums[48:72]
    cross = [sums[0:3], sums[4:7], sums[8:11]]
    total = jnp.concatenate([sums[3:4], sums[7:8], sums[11:12]], axis=0)
    trace = cross[0][0:1] + cross[1][1:2] + cross[2][2:3]
    square = jnp.sum(x * x, axis=0, keepdims=True) + soften_square
    weight = jnp.sum(x * total, axis=0, keepdims=True) - trace
    moment = x[0:1] * cross[0] + x[1:2] * cross[1] + x[2:3] * cross[2] + sums[16:19]
    turned = jnp.concatenate([jnp.sum(x * cross[m], axis=0, keepdims=True) for m in range(3)], axis=0)
    direct = square * total + sums[20:23] - 2 * turned
    return stokes_factor * (direct + x * weight - moment)


def step_kernel(
    groups, per_dev, split, info, neighbours, near, *refs
):
    if split:
        (low, own, high, low_s, own_s, high_s, stiffness, layered,
         out_pos, out_vel, out_den, dyn, stat, frc, meta, lists, counts, sems) = refs
    else:
        (low, own, high, stiffness, layered,
         out_dyn, dyn, stat, frc, meta, lists, counts, sems) = refs
        low_s, own_s, high_s = low, own, high
    points = dyn.shape[-1]
    n_list = neighbours.shape[1]
    n_near = near.shape[1]
    blocks = 3 * groups
    copies = []
    for side, (moving, fixed) in enumerate(((low, low_s), (own, own_s), (high, high_s))):
        span = pl.ds(side * groups, groups)
        copies.append(pltpu.make_async_copy(
            moving.at[:, pl.ds(0, per_dev)], dyn.at[span], sems.at[3 * side]))
        copies.append(pltpu.make_async_copy(
            fixed.at[:, pl.ds(per_dev, per_dev)], stat.at[span], sems.at[3 * side + 1]))
        copies.append(pltpu.make_async_copy(
            fixed.at[:, pl.ds(per_dev, per_dev), 6, pl.ds(0, 128)], meta.at[span], sems.at[3 * side + 2]))
    for copy in copies:
        copy.start()
    for copy in copies:
        copy.wait()
    segment = info[0]
    member = info[1]
    seg_cells = groups * per_dev

    def place(number):
        relative = number - (segment - 1) * seg_cells
        side = relative // seg_cells
        inside = relative % seg_cells
        turn = lax.rem(member - inside // per_dev + groups, groups)
        return side * groups + turn, inside % per_dev

    rows = blocks * per_dev * 8
    offset = (dyn[...] - stat[...]).reshape(rows, points).astype(bf16)
    frc[...] = lax.dot_general(
        offset, stiffness[...], (((1,), (1,)), ((), ())), preferred_element_type=f32
    ).reshape(frc.shape)

    for p in range(per_dev + 1):
        counts[p] = 0
    first_patch = segment * seg_cells + member * per_dev

    def scan(number, carry):
        block = number // per_dev
        local = number % per_dev
        alive = meta[block, local, 0] != 0.0
        for w in range(n_near):
            patch = meta[block, local, 1 + w].astype(jnp.int32) - first_patch
            mine = jnp.logical_and(alive, jnp.logical_and(patch >= 0, patch < per_dev))
            row = jnp.where(mine, patch, per_dev)
            filled = counts[row]
            lists[row, filled] = number
            counts[row] = filled + 1
        return carry

    lax.fori_loop(0, blocks * per_dev, scan, 0)

    def cell_source(block, local):
        return dyn[block, local, 0:3, :], frc[block, local, 0:3, :] * meta[block, local, 0]

    def centred(x):
        centre = jnp.mean(x, axis=1, keepdims=True)
        return x - centre, centre

    def do_cell(local, carry):
        alive = meta[groups, local, 0] != 0.0
        position = dyn[groups, local, 0:3, :]

        def moved():
            x, centre = centred(position)
            features = target_features(x)
            sums = jnp.zeros((72, points), f32)
            for n in range(n_list):
                y, f = cell_source(*place(neighbours[local, n]))
                sums = sums + pair_sums(features, y - centre, f)
            for n in range(n_near):
                block, other = place(near[local, n])
                y = stat[block, other, 3:6, :]
                f = dyn[block, other, 3:6, :]
                sums = sums + pair_sums(features, y - centre, f)
            return combine(sums, x)

        velocity = lax.cond(alive, moved, lambda: jnp.zeros((3, points), f32))
        if split:
            out_vel[local] = velocity
            out_pos[local] = position + time_step * velocity
        else:
            out_dyn[local, 0:3, :] = position + time_step * velocity
        return carry

    lax.fori_loop(0, per_dev, do_cell, 0)

    def do_patch(local, carry):
        x, centre = centred(stat[groups, local, 3:6, :])
        features = target_features(x)
        count = counts[local]

        def two(pair, sums):
            for part in range(2):
                entry = 2 * pair + part
                number = lists[local, jnp.minimum(entry, count - 1)]
                y, f = cell_source(number // per_dev, number % per_dev)
                f = jnp.where(entry < count, f, 0.0)
                sums = sums + pair_sums(features, y - centre, f)
            return sums

        sums = lax.fori_loop(0, (count + 1) // 2, two, jnp.zeros((72, points), f32))
        wall_velocity = combine(sums, x)
        density = dyn[groups, local, 3:6, :]
        density = density - relax_factor * (wall_velocity + 0.5 * density + layered[local])
        if split:
            out_den[local] = density
        else:
            out_dyn[local, 3:6, :] = density
        return carry

    lax.fori_loop(0, per_dev, do_patch, 0)
    if not split:
        out_dyn[:, 6:8, :] = jnp.zeros((per_dev, 2, points), f32)


def gather_cell(block):
    groups = lax.axis_size("cell")
    parts = [block]
    for shift in range(1, groups):
        parts.append(lax.ppermute(block, "cell", [(i, (i + shift) % groups) for i in range(groups)]))
    return jnp.stack(parts)


def sides(window):
    count = lax.axis_size("seg")
    forward = [(i, i + 1) for i in range(count - 1)]
    backward = [(target, source) for source, target in forward]
    return lax.ppermute(window, "seg", forward), lax.ppermute(window, "seg", backward)


def run_step(groups, per_dev, points, split, info, neighbours, near, arrays, stiffness, layered):
    smem = pl.BlockSpec(memory_space=pltpu.SMEM)
    vmem = pl.BlockSpec(memory_space=pltpu.VMEM)
    anywhere = pl.BlockSpec(memory_space=pl.ANY)
    if split:
        shapes = [jax.ShapeDtypeStruct((per_dev, 3, points), f32)] * 3
    else:
        shapes = [jax.ShapeDtypeStruct((per_dev, 8, points), f32)]
    window = (3 * groups, per_dev, 8, points)
    entries = 3 * groups * per_dev * near.shape[1]
    return pl.pallas_call(
        functools.partial(step_kernel, groups, per_dev, split),
        out_shape=shapes,
        in_specs=[smem] * 3 + [anywhere] * len(arrays) + [vmem] * 2,
        out_specs=[vmem] * len(shapes),
        scratch_shapes=[
            pltpu.VMEM(window, f32),
            pltpu.VMEM(window, f32),
            pltpu.VMEM(window, f32),
            pltpu.SMEM((3 * groups, per_dev, 128), f32),
            pltpu.SMEM((per_dev + 1, entries + 1), jnp.int32),
            pltpu.SMEM((per_dev + 1,), jnp.int32),
            pltpu.SemaphoreType.DMA((9,)),
        ],
        compiler_params=pltpu.CompilerParams(vmem_limit_bytes=48 * 1024 * 1024),
        name="stokes_step",
    )(info, neighbours, near, *arrays, stiffness, layered)


def body(
    positions, rest_shape, modulus, stiffness, wall_points, density,
    wall_operator, seg_count, neighbours, near_patches,
):
    per_dev, _, points = positions.shape
    groups = lax.axis_size("cell")
    segment = lax.axis_index("seg")
    member = lax.axis_index("cell")
    info = jnp.stack([segment, member]).astype(jnp.int32)
    slots = member * per_dev + jnp.arange(per_dev, dtype=jnp.int32)
    scaling = jnp.where(slots < seg_count[0], modulus, 0.0)
    table = jnp.concatenate([scaling[:, None], near_patches.astype(f32)], axis=1)
    table = jnp.pad(table, ((0, 0), (0, points - table.shape[1])))[:, None, :]
    blank = jnp.zeros((per_dev, 1, points), f32)
    moving = jnp.concatenate([positions, density, blank, blank], axis=1)
    fixed = jnp.concatenate([rest_shape, wall_points, table, blank], axis=1)

    def layer(density):
        return lax.dot_general(
            density, wall_operator, (((2,), (1,)), ((), ())), precision=highest
        )

    own = gather_cell(jnp.concatenate([moving, fixed], axis=0))
    low, high = sides(own)
    step = functools.partial(run_step, groups, per_dev, points)
    (moving,) = step(
        False, info, neighbours, near_patches, (low, own, high), stiffness, layer(density)
    )
    own_two = gather_cell(moving)
    low_two, high_two = sides(own_two)
    return tuple(step(
        True, info, neighbours, near_patches,
        (low_two, own_two, high_two, low, own, high), stiffness, layer(moving[:, 3:6]),
    ))


def solution(mesh):
    both = P(("seg", "cell"), None, None)
    placed = (
        both, both, P(("seg", "cell")), P(), both, both, P(), P("seg"),
        P(("seg", "cell"), None), P(("seg", "cell"), None),
    )
    return jax.shard_map(
        body, mesh=mesh, in_specs=placed, out_specs=(both, both, both), check_vma=False
    )
```

```python
import functools

import jax
import jax.numpy as jnp
from jax import lax
from jax.experimental import pallas as pl
from jax.experimental.pallas import tpu as pltpu
from jax.sharding import PartitionSpec as P

soften_square = 0.25
stokes_factor = 0.039788735772973836
relax_factor = 0.5
time_step = 0.5
bf16 = jnp.bfloat16
f32 = jnp.float32
highest = lax.Precision.HIGHEST
unroll = 4


def row_places(points):
    return lax.broadcasted_iota(jnp.int32, (8, points), 0)


def tall(row):
    return jnp.broadcast_to(row, (8, row.shape[1]))


def parts_of(value):
    first = value.astype(bf16).astype(f32)
    rest = value - first
    second = rest.astype(bf16).astype(f32)
    third = (rest - second).astype(bf16).astype(f32)
    return first, second, third


def target_features(x):
    points = x[0].shape[1]
    place = row_places(points)
    square = x[0] * x[0] + x[1] * x[1] + x[2] * x[2]
    rows = jnp.where(place == 3, 1.0, 0.0)
    for number, row in ((0, x[0]), (1, x[1]), (2, x[2]), (4, square)):
        rows = jnp.where(place == number, tall(row), rows)
    high, middle, low = parts_of(rows)
    return jnp.concatenate([high, middle, high, low, high, middle], axis=0).astype(bf16)


def pair_sums(features, y, f):
    points = y[0].shape[1]
    place = row_places(points)
    low_half = place < 4
    lane = place & 3
    square = tall(y[0] * y[0] + y[1] * y[1] + y[2] * y[2])
    along = tall(-(y[0] * f[0] + y[1] * f[1] + y[2] * f[2]))
    y = [tall(row) for row in y]
    f = [tall(row) for row in f]
    points_one = jnp.where(lane == 0, y[0], jnp.where(lane == 1, y[1], jnp.where(lane == 2, y[2], 1.0)))
    source = jnp.where(
        place < 3, -2 * points_one,
        jnp.where(place == 3, square + soften_square, jnp.where(place == 4, 1.0, 0.0)),
    )
    high, middle, low = parts_of(source)
    wide = jnp.concatenate([high, high, middle, high, low, middle], axis=0)
    distance = jnp.dot(wide.T.astype(bf16), features, preferred_element_type=f32)
    inverse = lax.rsqrt(distance)
    cubed = (inverse * inverse * inverse).astype(bf16)
    one = jnp.where(low_half, f[0], f[1]) * points_one
    two = jnp.where(low_half, f[2], along) * points_one
    three = jnp.where(lane == 0, f[0], jnp.where(lane == 1, f[1], f[2])) * square
    moments = jnp.concatenate(parts_of(jnp.concatenate([one, two, three], axis=0)), axis=0)
    sums = jnp.dot(moments.astype(bf16), cubed, preferred_element_type=f32)
    return sums[0:24] + sums[24:48] + sums[48:72]


def combine(sums, x):
    cross = [[sums[4 * m + k : 4 * m + k + 1] for k in range(3)] for m in range(3)]
    total = [sums[4 * m + 3 : 4 * m + 4] for m in range(3)]
    square = x[0] * x[0] + x[1] * x[1] + x[2] * x[2] + soften_square
    weight = x[0] * total[0] + x[1] * total[1] + x[2] * total[2] + sums[15:16]
    out = []
    for k in range(3):
        moment = x[0] * cross[0][k] + x[1] * cross[1][k] + x[2] * cross[2][k] + sums[12 + k : 13 + k]
        turned = x[0] * cross[k][0] + x[1] * cross[k][1] + x[2] * cross[k][2]
        direct = square * total[k] + sums[16 + k : 17 + k] - 2 * turned
        out.append(stokes_factor * (direct + x[k] * weight - moment))
    return out


def pack_kernel(info, modulus, count, near, positions, rest_shape, wall_points, density, out, sems):
    per_dev = positions.shape[1]
    copies = [
        pltpu.make_async_copy(array, out.at[pl.ds(3 * number, 3)], sems.at[number])
        for number, array in enumerate((positions, density, rest_shape, wall_points))
    ]
    for copy in copies:
        copy.start()
    shape = out.shape[1:]
    row = lax.broadcasted_iota(jnp.int32, shape, 0)
    lane = lax.broadcasted_iota(jnp.int32, shape, 1)
    table = jnp.zeros(shape, f32)
    for local in range(per_dev):
        alive = info[1] * per_dev + local < count[0]
        scale = jnp.where(alive, modulus[local], 0.0)
        entries = [scale] + [near[w, local].astype(f32) for w in range(near.shape[0])]
        for number, entry in enumerate(entries):
            table = jnp.where(jnp.logical_and(row == local, lane == number), entry, table)
    out[12] = table
    for copy in copies:
        copy.wait()


def step_kernel(groups, per_dev, split, info, neighbours, near, *refs):
    if split:
        (low, own, high, low_s, own_s, high_s, stiffness, layered,
         out_pos, out_vel, out_den, src, tgt, centres, feats, sums, meta, pairs, sems) = refs
    else:
        (low, own, high, stiffness, layered,
         out_dyn, src, tgt, centres, feats, sums, meta, pairs, sems) = refs
        low_s, own_s, high_s = low, own, high
    points = src.shape[-1]
    n_list = neighbours.shape[1]
    n_near = near.shape[0]
    blocks = 3 * groups
    dummy = 2 * blocks
    moving = (low, own, high)
    fixed = (low_s, own_s, high_s)
    copies = []
    for side in range(3):
        cells = pl.ds(side * groups, groups)
        walls = pl.ds(blocks + side * groups, groups)
        for number, (source, target) in enumerate((
            (moving[side].at[:, pl.ds(0, 3)], src.at[cells, pl.ds(0, 3)]),
            (fixed[side].at[:, pl.ds(9, 3)], src.at[walls, pl.ds(0, 3)]),
            (moving[side].at[:, pl.ds(3, 3)], src.at[walls, pl.ds(3, 3)]),
            (fixed[side].at[:, 12, :, pl.ds(0, 128)], meta.at[cells]),
        )):
            copies.append(pltpu.make_async_copy(source, target, sems.at[4 * side + number]))
    for copy in copies:
        copy.start()
    src[dummy] = jnp.zeros(src.shape[1:], f32)

    tiles = []
    for side in range(3):
        for block in range(groups):
            for k in range(3):
                tiles.append(moving[side][block, k] - fixed[side][block, 6 + k])
    offset = jnp.concatenate(tiles, axis=0).astype(bf16)
    pushed = lax.dot_general(
        offset, stiffness[...], (((1,), (1,)), ((), ())), preferred_element_type=f32
    )
    row = 0
    for side in range(3):
        for block in range(groups):
            scale = jnp.broadcast_to(fixed[side][block, 12][:, 0:1], (per_dev, points))
            for k in range(3):
                src[side * groups + block, 3 + k] = scale * pushed[row : row + per_dev]
                row += per_dev

    for kind in range(2):
        for k in range(3):
            tile = (own[0, k], own_s[0, 9 + k])[kind]
            centre = jnp.mean(tile, axis=1, keepdims=True)
            centres[kind, k] = jnp.broadcast_to(centre, tile.shape)
            tgt[kind, k] = tile - centre
    for kind in range(2):
        for local in range(per_dev):
            x = [tgt[kind, k, local : local + 1, :] for k in range(3)]
            feats[kind * per_dev + local] = target_features(x)
    sums[...] = jnp.zeros(sums.shape, f32)
    for copy in copies:
        copy.wait()

    segment = info[0]
    member = info[1]
    seg_cells = groups * per_dev

    def place(number):
        relative = number - (segment - 1) * seg_cells
        side = relative // seg_cells
        inside = relative % seg_cells
        turn = lax.rem(member - inside // per_dev + groups, groups)
        return side * groups + turn, inside % per_dev

    def encode(target, block, local):
        return (target * (2 * blocks + 1) + block) * per_dev + local

    filled = jnp.int32(0)
    for local in range(per_dev):
        alive = (meta[groups, local, 0] != 0.0).astype(jnp.int32)
        for n in range(n_list):
            block, other = place(neighbours[local, n])
            pairs[filled] = encode(local, block, other)
            filled = filled + alive
        for n in range(n_near):
            block, other = place(near[n, local])
            pairs[filled] = encode(local, block + blocks, other)
            filled = filled + alive
    first_patch = segment * seg_cells + member * per_dev

    def scan(block, filled):
        for local in range(per_dev):
            alive = meta[block, local, 0] != 0.0
            for w in range(n_near):
                patch = meta[block, local, 1 + w].astype(jnp.int32) - first_patch
                mine = jnp.logical_and(alive, jnp.logical_and(patch >= 0, patch < per_dev))
                pairs[filled] = encode(per_dev + patch, block, local)
                filled = filled + mine.astype(jnp.int32)
        return filled

    filled = lax.fori_loop(0, blocks, scan, filled)
    for extra in range(unroll - 1):
        pairs[filled + extra] = encode(0, dummy, 0)

    def some(step, carry):
        for part in range(unroll):
            code = pairs[step * unroll + part]
            local = code % per_dev
            block = (code // per_dev) % (2 * blocks + 1)
            target = code // (per_dev * (2 * blocks + 1))
            kind = target // per_dev
            slot = target % per_dev
            y = [
                src[block, k, pl.ds(local, 1), :] - centres[kind, k, pl.ds(slot, 1), :]
                for k in range(3)
            ]
            f = [src[block, 3 + k, pl.ds(local, 1), :] for k in range(3)]
            sums[target] += pair_sums(feats[target], y, f)
        return carry

    lax.fori_loop(0, (filled + unroll - 1) // unroll, some, 0)

    for local in range(per_dev):
        slot = slice(local, local + 1)
        velocity = combine(sums[local], [tgt[0, k, slot, :] for k in range(3)])
        wall_velocity = combine(sums[per_dev + local], [tgt[1, k, slot, :] for k in range(3)])
        for k in range(3):
            position = own[0, k, slot, :] + time_step * velocity[k]
            density = own[0, 3 + k, slot, :]
            density = density - relax_factor * (
                wall_velocity[k] + 0.5 * density + layered[k, slot, :]
            )
            if split:
                out_pos[k, slot, :] = position
                out_vel[k, slot, :] = velocity[k]
                out_den[k, slot, :] = density
            else:
                out_dyn[k, slot, :] = position
                out_dyn[3 + k, slot, :] = density


def gather_cell(block):
    groups = lax.axis_size("cell")
    parts = [block]
    for shift in range(1, groups):
        parts.append(lax.ppermute(block, "cell", [(i, (i + shift) % groups) for i in range(groups)]))
    return jnp.stack(parts)


def sides(window):
    count = lax.axis_size("seg")
    forward = [(i, i + 1) for i in range(count - 1)]
    backward = [(target, source) for source, target in forward]
    return lax.ppermute(window, "seg", forward), lax.ppermute(window, "seg", backward)


smem = pl.BlockSpec(memory_space=pltpu.SMEM)
vmem = pl.BlockSpec(memory_space=pltpu.VMEM)
anywhere = pl.BlockSpec(memory_space=pl.ANY)


def pack(info, modulus, seg_count, near, arrays):
    _, per_dev, points = arrays[0].shape
    return pl.pallas_call(
        pack_kernel,
        out_shape=jax.ShapeDtypeStruct((13, per_dev, points), f32),
        in_specs=[smem] * 4 + [anywhere] * 4,
        out_specs=vmem,
        scratch_shapes=[pltpu.SemaphoreType.DMA((4,))],
        name="pack",
    )(info, modulus, seg_count, near, *arrays)


def run_step(groups, per_dev, points, split, info, neighbours, near, arrays, stiffness, layered):
    if split:
        shapes = [jax.ShapeDtypeStruct((3, per_dev, points), f32)] * 3
    else:
        shapes = [jax.ShapeDtypeStruct((6, per_dev, points), f32)]
    blocks = 3 * groups
    entries = blocks * per_dev * near.shape[0] + per_dev * (neighbours.shape[1] + near.shape[0])
    return pl.pallas_call(
        functools.partial(step_kernel, groups, per_dev, split),
        out_shape=shapes,
        in_specs=[smem] * 3 + [vmem] * (len(arrays) + 2),
        out_specs=[vmem] * len(shapes),
        scratch_shapes=[
            pltpu.VMEM((2 * blocks + 1, 6, per_dev, points), f32),
            pltpu.VMEM((2, 3, per_dev, points), f32),
            pltpu.VMEM((2, 3, per_dev, points), f32),
            pltpu.VMEM((2 * per_dev, 48, points), bf16),
            pltpu.VMEM((2 * per_dev, 24, points), f32),
            pltpu.SMEM((blocks, per_dev, 128), f32),
            pltpu.SMEM((entries + unroll,), jnp.int32),
            pltpu.SemaphoreType.DMA((12,)),
        ],
        compiler_params=pltpu.CompilerParams(vmem_limit_bytes=40 * 1024 * 1024),
        name="stokes_step",
    )(info, neighbours, near, *arrays, stiffness, layered)


def body(
    positions, rest_shape, modulus, stiffness, wall_points, density,
    wall_operator, seg_count, neighbours, near_patches,
):
    per_dev, _, points = positions.shape
    groups = lax.axis_size("cell")
    info = jnp.stack([lax.axis_index("seg"), lax.axis_index("cell")]).astype(jnp.int32)
    near = near_patches.T
    turn = lambda array: jnp.transpose(array, (1, 0, 2))
    positions, rest_shape, wall_points, density = map(
        turn, (positions, rest_shape, wall_points, density)
    )

    def layer(density):
        return lax.dot_general(
            density, wall_operator, (((2,), (1,)), ((), ())), precision=highest
        )

    step = functools.partial(run_step, groups, per_dev, points)
    own = gather_cell(pack(info, modulus, seg_count, near, (positions, rest_shape, wall_points, density)))
    low, high = sides(own)
    (moving,) = step(
        False, info, neighbours, near, (low, own, high), stiffness, layer(density)
    )
    own_two = gather_cell(moving)
    low_two, high_two = sides(own_two)
    outs = step(
        True, info, neighbours, near,
        (low_two, own_two, high_two, low, own, high), stiffness, layer(moving[3:6]),
    )
    return tuple(map(turn, outs))


def solution(mesh):
    both = P(("seg", "cell"), None, None)
    placed = (
        both, both, P(("seg", "cell")), P(), both, both, P(), P("seg"),
        P(("seg", "cell"), None), P(("seg", "cell"), None),
    )
    return jax.shard_map(
        body, mesh=mesh, in_specs=placed, out_specs=(both, both, both), check_vma=False
    )
```

```python
import functools

import jax
import jax.numpy as jnp
from jax import lax
from jax.experimental import pallas as pl
from jax.experimental.pallas import tpu as pltpu
from jax.sharding import PartitionSpec as P

soften_square = 0.25
stokes_factor = 0.039788735772973836
relax_factor = 0.5
time_step = 0.5
bf16 = jnp.bfloat16
f32 = jnp.float32
highest = lax.Precision.HIGHEST
unroll = 4
STEPS = 2


def row_places(points):
    return lax.broadcasted_iota(jnp.int32, (8, points), 0)


def tall(row):
    return jnp.broadcast_to(row, (8, row.shape[1]))


def parts_of(value):
    first = value.astype(bf16).astype(f32)
    rest = value - first
    second = rest.astype(bf16).astype(f32)
    third = (rest - second).astype(bf16).astype(f32)
    return first, second, third


def target_features(x):
    points = x[0].shape[1]
    place = row_places(points)
    square = x[0] * x[0] + x[1] * x[1] + x[2] * x[2]
    rows = jnp.where(place == 3, 1.0, 0.0)
    for number, row in ((0, x[0]), (1, x[1]), (2, x[2]), (4, square)):
        rows = jnp.where(place == number, tall(row), rows)
    high, middle, low = parts_of(rows)
    return jnp.concatenate([high, middle, high, low, high, middle], axis=0).astype(bf16)


def source_rows(y, f):
    place = row_places(y[0].shape[1])
    low_half = place < 4
    lane = place & 3
    square = tall(y[0] * y[0] + y[1] * y[1] + y[2] * y[2])
    along = tall(-(y[0] * f[0] + y[1] * f[1] + y[2] * f[2]))
    y = [tall(row) for row in y]
    f = [tall(row) for row in f]
    points_one = jnp.where(lane == 0, y[0], jnp.where(lane == 1, y[1], jnp.where(lane == 2, y[2], 1.0)))
    source = jnp.where(
        place < 3, -2 * points_one,
        jnp.where(place == 3, square + soften_square, jnp.where(place == 4, 1.0, 0.0)),
    )
    high, middle, low = parts_of(source)
    wide = jnp.concatenate([high, high, middle, high, low, middle], axis=0).astype(bf16)
    one = jnp.where(low_half, f[0], f[1]) * points_one
    two = jnp.where(low_half, f[2], along) * points_one
    three = jnp.where(lane == 0, f[0], jnp.where(lane == 1, f[1], f[2])) * square
    moments = jnp.concatenate(parts_of(jnp.concatenate([one, two, three], axis=0)), axis=0)
    return wide.T, moments.astype(bf16)


def sums_of_pairs(fetch, count):
    held = []

    def distance(unit):
        pair, half = divmod(unit, 2)
        if half == 0:
            y, f, features = fetch(pair)
            held.append((*source_rows(y, f), features))
        wide, _, features = held[pair]
        rows = wide.shape[0] // 2
        return jnp.dot(wide[half * rows : (half + 1) * rows], features, preferred_element_type=f32)

    def moment_sums(unit, distance):
        pair, half = divmod(unit, 2)
        inverse = lax.rsqrt(distance)
        cubed = (inverse * inverse * inverse).astype(bf16)
        moments = held[pair][1]
        rows = moments.shape[1] // 2
        return jnp.dot(
            moments[:, half * rows : (half + 1) * rows], cubed, preferred_element_type=f32
        )

    ready = [distance(0), distance(1)]
    out = []
    for unit in range(2 * count):
        if unit + 2 < 2 * count:
            ready.append(distance(unit + 2))
        sums = moment_sums(unit, ready[unit])
        if unit % 2 == 0:
            first = sums
        else:
            sums = first + sums
            out.append(sums[0:24] + sums[24:48] + sums[48:72])
    return out


def combine(sums, x):
    cross = [[sums[4 * m + k : 4 * m + k + 1] for k in range(3)] for m in range(3)]
    total = [sums[4 * m + 3 : 4 * m + 4] for m in range(3)]
    square = x[0] * x[0] + x[1] * x[1] + x[2] * x[2] + soften_square
    weight = x[0] * total[0] + x[1] * total[1] + x[2] * total[2] + sums[15:16]
    out = []
    for k in range(3):
        moment = x[0] * cross[0][k] + x[1] * cross[1][k] + x[2] * cross[2][k] + sums[12 + k : 13 + k]
        turned = x[0] * cross[k][0] + x[1] * cross[k][1] + x[2] * cross[k][2]
        direct = square * total[k] + sums[16 + k : 17 + k] - 2 * turned
        out.append(stokes_factor * (direct + x[k] * weight - moment))
    return out


def pack_kernel(info, modulus, count, near, positions, rest_shape, wall_points, density, out, sems):
    per_dev = positions.shape[1]
    copies = [
        pltpu.make_async_copy(array, out.at[pl.ds(3 * number, 3)], sems.at[number])
        for number, array in enumerate((positions, density, rest_shape, wall_points))
    ]
    for copy in copies:
        copy.start()
    shape = out.shape[1:]
    row = lax.broadcasted_iota(jnp.int32, shape, 0)
    lane = lax.broadcasted_iota(jnp.int32, shape, 1)
    table = jnp.zeros(shape, f32)
    for local in range(per_dev):
        alive = info[1] * per_dev + local < count[0]
        scale = jnp.where(alive, modulus[local], 0.0)
        entries = [scale] + [near[w, local].astype(f32) for w in range(near.shape[0])]
        for number, entry in enumerate(entries):
            table = jnp.where(jnp.logical_and(row == local, lane == number), entry, table)
    out[12] = table
    for copy in copies:
        copy.wait()


def encode(target, block, local):
    return (target * 256 + block) * 16 + local


def pair_loop(filled, pairs, src, centres, feats, sums, per_dev, dummy):
    for extra in range(unroll - 1):
        pairs[filled + extra] = encode(0, dummy, 0)

    def some(step, carry):
        targets = []

        def fetch(part):
            code = pairs[step * unroll + part]
            local = code & 15
            block = (code >> 4) & 255
            target = code >> 12
            targets.append(target)
            kind = lax.div(target, per_dev)
            slot = lax.rem(target, per_dev)
            y = [
                src[block, k, pl.ds(local, 1), :] - centres[kind, k, pl.ds(slot, 1), :]
                for k in range(3)
            ]
            f = [src[block, 3 + k, pl.ds(local, 1), :] for k in range(3)]
            return y, f, feats[target]

        found = sums_of_pairs(fetch, unroll)
        for target, value in zip(targets, found):
            sums[target] += value
        return carry

    lax.fori_loop(0, lax.div(filled + unroll - 1, unroll), some, 0)


def pairs_kernel(stage, last, groups, per_dev, info, neighbours, near, stiffness, *refs):
    (own, own_s), refs = refs[:2], refs[2:]
    if stage == 0:
        windows, (out_tgt, feats, sums), refs = [(own, own_s)], refs[:3], refs[3:]
        centres = out_tgt.at[1]
    elif stage == 1:
        windows, (tgt, feats, sums_in, sums), refs = [refs[:2]], refs[2:6], refs[6:]
        centres = tgt.at[1]
    else:
        windows, (tgt, feats, sums_in, layered), refs = [refs[:2], refs[2:4]], refs[4:8], refs[8:]
        centres = tgt.at[1]
        outs, refs = refs[: 3 if last else 1], refs[3 if last else 1 :]
    if stage == 2:
        src, meta, pairs, sems, sums = refs
    else:
        src, meta, pairs, sems = refs
    points = src.shape[-1]
    n_list = neighbours.shape[1]
    n_near = near.shape[0]
    each = windows[0][0].shape[0]
    blocks = each * len(windows)
    dummy = 2 * blocks
    copies = [pltpu.make_async_copy(
        own_s.at[pl.ds(0, 1), 12, :, pl.ds(0, 128)], meta.at[pl.ds(blocks, 1)], sems.at[0])]
    for side, (moving, fixed) in enumerate(windows):
        cells = pl.ds(side * each, each)
        copies.append(pltpu.make_async_copy(
            fixed.at[:, 12, :, pl.ds(0, 128)], meta.at[cells], sems.at[1 + side]))
    for copy in copies:
        copy.start()

    src[dummy] = jnp.zeros(src.shape[1:], f32)
    tiles = []
    for side, (moving, fixed) in enumerate(windows):
        for block in range(each):
            number = side * each + block
            for k in range(3):
                tiles.append(moving[block, k] - fixed[block, 6 + k])
                src[number, k] = moving[block, k]
                src[blocks + number, k] = fixed[block, 9 + k]
                src[blocks + number, 3 + k] = moving[block, 3 + k]
    offset = jnp.concatenate(tiles, axis=0).astype(bf16)
    pushed = lax.dot_general(
        offset, stiffness[...], (((1,), (1,)), ((), ())), preferred_element_type=f32
    )
    row = 0
    for side, (moving, fixed) in enumerate(windows):
        for block in range(each):
            scale = jnp.broadcast_to(fixed[block, 12][:, 0:1], (per_dev, points))
            for k in range(3):
                src[side * each + block, 3 + k] = scale * pushed[row : row + per_dev]
                row += per_dev

    if stage == 0:
        for kind in range(2):
            for k in range(3):
                tile = (own[0, k], own_s[0, 9 + k])[kind]
                centre = jnp.mean(tile, axis=1, keepdims=True)
                out_tgt[1, kind, k] = jnp.broadcast_to(centre, tile.shape)
                out_tgt[0, kind, k] = tile - centre
        for kind in range(2):
            for local in range(per_dev):
                x = [out_tgt[0, kind, k, local : local + 1, :] for k in range(3)]
                feats[kind * per_dev + local] = target_features(x)
        sums[...] = jnp.zeros(sums.shape, f32)
    else:
        sums[...] = sums_in[...]
    for copy in copies:
        copy.wait()

    segment = info[0]
    member = info[1]
    seg_cells = groups * per_dev

    def place(number):
        relative = number - (segment - 1) * seg_cells
        side = lax.div(relative, seg_cells)
        inside = lax.rem(relative, seg_cells)
        turn = lax.rem(member - lax.div(inside, per_dev) + groups, groups)
        if stage == 0:
            here, block = jnp.logical_and(side == 1, turn == 0), 0
        elif stage == 1:
            here, block = jnp.logical_and(side == 1, turn != 0), turn
        else:
            here, block = side != 1, lax.div(side, 2) * groups + turn
        return here, block, lax.rem(inside, per_dev)

    filled = jnp.int32(0)
    for local in range(per_dev):
        alive = meta[blocks, local, 0] != 0.0
        for entries, count, shift in ((neighbours, n_list, 0), (near, n_near, blocks)):
            for n in range(count):
                entry = entries[n, local] if shift else entries[local, n]
                here, block, other = place(entry)
                pairs[filled] = encode(local, block + shift, other)
                filled = filled + jnp.logical_and(alive, here).astype(jnp.int32)
    first_patch = segment * seg_cells + member * per_dev

    def scan(block, filled):
        for local in range(per_dev):
            alive = meta[block, local, 0] != 0.0
            for w in range(n_near):
                patch = meta[block, local, 1 + w].astype(jnp.int32) - first_patch
                mine = jnp.logical_and(alive, jnp.logical_and(patch >= 0, patch < per_dev))
                pairs[filled] = encode(per_dev + patch, block, local)
                filled = filled + mine.astype(jnp.int32)
        return filled

    filled = lax.fori_loop(1 if stage == 1 else 0, blocks, scan, filled)
    pair_loop(filled, pairs, src, centres, feats, sums, per_dev, dummy)
    if stage < 2:
        return

    for local in range(per_dev):
        slot = slice(local, local + 1)
        velocity = combine(sums[local], [tgt[0, 0, k, slot, :] for k in range(3)])
        wall_velocity = combine(sums[per_dev + local], [tgt[0, 1, k, slot, :] for k in range(3)])
        for k in range(3):
            position = own[0, k, slot, :] + time_step * velocity[k]
            density = own[0, 3 + k, slot, :]
            density = density - relax_factor * (
                wall_velocity[k] + 0.5 * density + layered[k, slot, :]
            )
            if last:
                outs[0][k, slot, :] = position
                outs[1][k, slot, :] = velocity[k]
                outs[2][k, slot, :] = density
            else:
                outs[0][k, slot, :] = position
                outs[0][3 + k, slot, :] = density


def gather_cell(block):
    groups = lax.axis_size("cell")
    parts = [block]
    for shift in range(1, groups):
        parts.append(lax.ppermute(block, "cell", [(i, (i + shift) % groups) for i in range(groups)]))
    return jnp.stack(parts)


def sides(window):
    count = lax.axis_size("seg")
    forward = [(i, i + 1) for i in range(count - 1)]
    backward = [(target, source) for source, target in forward]
    return lax.ppermute(window, "seg", forward), lax.ppermute(window, "seg", backward)


smem = pl.BlockSpec(memory_space=pltpu.SMEM)
vmem = pl.BlockSpec(memory_space=pltpu.VMEM)
anywhere = pl.BlockSpec(memory_space=pl.ANY)


def pack(info, modulus, seg_count, near, arrays):
    _, per_dev, points = arrays[0].shape
    return pl.pallas_call(
        pack_kernel,
        out_shape=jax.ShapeDtypeStruct((13, per_dev, points), f32),
        in_specs=[smem] * 4 + [anywhere] * 4,
        out_specs=vmem,
        scratch_shapes=[pltpu.SemaphoreType.DMA((4,))],
        name="pack",
    )(info, modulus, seg_count, near, *arrays)


def run_stage(stage, last, groups, per_dev, points, scalars, stiffness, own, arrays):
    _, neighbours, near = scalars
    blocks = (1, groups, 2 * groups)[stage]
    entries = blocks * per_dev * near.shape[0] + per_dev * (neighbours.shape[1] + near.shape[0])
    carried = [
        jax.ShapeDtypeStruct((2, 2, 3, per_dev, points), f32),
        jax.ShapeDtypeStruct((2 * per_dev, 48, points), bf16),
        jax.ShapeDtypeStruct((2 * per_dev, 24, points), f32),
    ]
    if stage == 0:
        shapes = carried
    elif stage == 1:
        shapes = carried[2:]
    elif last:
        shapes = [jax.ShapeDtypeStruct((3, per_dev, points), f32)] * 3
    else:
        shapes = [jax.ShapeDtypeStruct((6, per_dev, points), f32)]
    scratch = [
        pltpu.VMEM((2 * blocks + 1, 6, per_dev, points), f32),
        pltpu.SMEM((blocks + 1, per_dev, 128), f32),
        pltpu.SMEM((entries + unroll,), jnp.int32),
        pltpu.SemaphoreType.DMA((3,)),
    ]
    if stage == 2:
        scratch.append(pltpu.VMEM(carried[2].shape, f32))
    pair_count = 8 if stage < 2 else 24
    return pl.pallas_call(
        functools.partial(pairs_kernel, stage, last, groups, per_dev),
        out_shape=shapes,
        in_specs=[smem] * 3 + [vmem] * (3 + len(arrays)),
        out_specs=[vmem] * len(shapes),
        scratch_shapes=scratch,
        cost_estimate=pl.CostEstimate(
            flops=pair_count * 2 * points * points * 512, transcendentals=0,
            bytes_accessed=1 << 20,
        ),
        compiler_params=pltpu.CompilerParams(vmem_limit_bytes=32 * 1024 * 1024),
        name=("own_pairs", "segment_pairs", "outer_pairs")[stage],
    )(*scalars, stiffness, *own, *arrays)


def body(
    positions, rest_shape, modulus, stiffness, wall_points, density,
    wall_operator, seg_count, neighbours, near_patches,
):
    per_dev, _, points = positions.shape
    groups = lax.axis_size("cell")
    info = jnp.stack([lax.axis_index("seg"), lax.axis_index("cell")]).astype(jnp.int32)
    near = near_patches.T
    turn = lambda array: jnp.transpose(array, (1, 0, 2))
    positions, rest_shape, wall_points, density = map(
        turn, (positions, rest_shape, wall_points, density)
    )

    def layer(density):
        return lax.dot_general(
            density, wall_operator, (((2,), (1,)), ((), ())), precision=highest
        )

    scalars = (info, neighbours, near)
    fixed = pack(info, modulus, seg_count, near, (positions, rest_shape, wall_points, density))
    moving = fixed
    window_s = None
    for repeat in range(STEPS):
        last = repeat == STEPS - 1
        stage = functools.partial(run_stage, groups=groups, per_dev=per_dev, points=points,
                                  last=last, scalars=scalars, stiffness=stiffness,
                                  own=(moving[None], fixed[None]))
        layered = layer(moving[3:6])
        window = gather_cell(moving)
        tgt, feats, sums = stage(0, arrays=())
        low, high = sides(window)
        if window_s is None:
            window_s, low_s, high_s = window, low, high
        (sums,) = stage(1, arrays=(window, window_s, tgt, feats, sums))
        outs = stage(2, arrays=(low, low_s, high, high_s, tgt, feats, sums, layered))
        moving = outs[0]
    return tuple(map(turn, outs))


def solution(mesh):
    both = P(("seg", "cell"), None, None)
    placed = (
        both, both, P(("seg", "cell")), P(), both, both, P(), P("seg"),
        P(("seg", "cell"), None), P(("seg", "cell"), None),
    )
    return jax.shard_map(
        body, mesh=mesh, in_specs=placed, out_specs=(both, both, both), check_vma=False
    )
```

```python
import functools

import jax
import jax.numpy as jnp
from jax import lax
from jax.experimental import pallas as pl
from jax.experimental.pallas import tpu as pltpu
from jax.sharding import PartitionSpec as P

soften_square = 0.25
stokes_factor = 0.039788735772973836
relax_factor = 0.5
time_step = 0.5
bf16 = jnp.bfloat16
f32 = jnp.float32
highest = lax.Precision.HIGHEST
STEPS = 2


def row_places(points):
    return lax.broadcasted_iota(jnp.int32, (8, points), 0)


def tall(row):
    return jnp.broadcast_to(row, (8, row.shape[1]))


def parts_of(value):
    first = value.astype(bf16).astype(f32)
    rest = value - first
    second = rest.astype(bf16).astype(f32)
    third = (rest - second).astype(bf16).astype(f32)
    return first, second, third


def target_features(x):
    points = x[0].shape[1]
    place = row_places(points)
    square = x[0] * x[0] + x[1] * x[1] + x[2] * x[2]
    rows = jnp.where(place == 3, 1.0, 0.0)
    for number, row in ((0, x[0]), (1, x[1]), (2, x[2]), (4, square)):
        rows = jnp.where(place == number, tall(row), rows)
    high, middle, low = parts_of(rows)
    return jnp.concatenate([high, middle, high, low, high, middle], axis=0).astype(bf16)


def source_rows(y, f):
    place = row_places(y[0].shape[1])
    low_half = place < 4
    lane = place & 3
    square = tall(y[0] * y[0] + y[1] * y[1] + y[2] * y[2])
    along = tall(-(y[0] * f[0] + y[1] * f[1] + y[2] * f[2]))
    y = [tall(row) for row in y]
    f = [tall(row) for row in f]
    points_one = jnp.where(lane == 0, y[0], jnp.where(lane == 1, y[1], jnp.where(lane == 2, y[2], 1.0)))
    source = jnp.where(
        place < 3, -2 * points_one,
        jnp.where(place == 3, square + soften_square, jnp.where(place == 4, 1.0, 0.0)),
    )
    high, middle, low = parts_of(source)
    wide = jnp.concatenate([high, high, middle, high, low, middle], axis=0).astype(bf16)
    one = jnp.where(low_half, f[0], f[1]) * points_one
    two = jnp.where(low_half, f[2], along) * points_one
    three = jnp.where(lane == 0, f[0], jnp.where(lane == 1, f[1], f[2])) * square
    moments = jnp.concatenate(parts_of(jnp.concatenate([one, two, three], axis=0)), axis=0)
    return wide.T, moments.astype(bf16)


def sums_of_pairs(fetch, count):
    held = []

    def distance(unit):
        pair, half = divmod(unit, 2)
        if half == 0:
            y, f, features = fetch(pair)
            held.append((*source_rows(y, f), features))
        wide, _, features = held[pair]
        rows = wide.shape[0] // 2
        return jnp.dot(wide[half * rows : (half + 1) * rows], features, preferred_element_type=f32)

    def moment_sums(unit, distance):
        pair, half = divmod(unit, 2)
        inverse = lax.rsqrt(distance)
        cubed = (inverse * inverse * inverse).astype(bf16)
        moments = held[pair][1]
        rows = moments.shape[1] // 2
        return jnp.dot(
            moments[:, half * rows : (half + 1) * rows], cubed, preferred_element_type=f32
        )

    ready = [distance(0), distance(1)]
    out = []
    for unit in range(2 * count):
        if unit + 2 < 2 * count:
            ready.append(distance(unit + 2))
        sums = moment_sums(unit, ready[unit])
        if unit % 2 == 0:
            first = sums
        else:
            sums = first + sums
            out.append(sums[0:24] + sums[24:48] + sums[48:72])
    return out


def combine(sums, x):
    cross = [[sums[4 * m + k : 4 * m + k + 1] for k in range(3)] for m in range(3)]
    total = [sums[4 * m + 3 : 4 * m + 4] for m in range(3)]
    square = x[0] * x[0] + x[1] * x[1] + x[2] * x[2] + soften_square
    weight = x[0] * total[0] + x[1] * total[1] + x[2] * total[2] + sums[15:16]
    out = []
    for k in range(3):
        moment = x[0] * cross[0][k] + x[1] * cross[1][k] + x[2] * cross[2][k] + sums[12 + k : 13 + k]
        turned = x[0] * cross[k][0] + x[1] * cross[k][1] + x[2] * cross[k][2]
        direct = square * total[k] + sums[16 + k : 17 + k] - 2 * turned
        out.append(stokes_factor * (direct + x[k] * weight - moment))
    return out


def pack_kernel(*refs):
    modulus, count, near, positions, rest_shape, wall_points, density, out, sems = refs[:9]
    held = refs[9:]
    per_dev = positions.shape[1]
    copies = [
        pltpu.make_async_copy(array, target, sems.at[number])
        for number, (array, target) in enumerate(zip((modulus, count, near), held))
    ]
    for number, array in enumerate((positions, density, rest_shape, wall_points)):
        copies.append(pltpu.make_async_copy(array, out.at[pl.ds(3 * number, 3)], sems.at[3 + number]))
    for copy in copies:
        copy.start()
    for copy in copies:
        copy.wait()
    modulus, count, near = held
    shape = out.shape[1:]
    row = lax.broadcasted_iota(jnp.int32, shape, 0)
    lane = lax.broadcasted_iota(jnp.int32, shape, 1)
    table = jnp.zeros(shape, f32)
    first = lax.axis_index("cell") * per_dev
    for local in range(per_dev):
        scale = jnp.where(first + local < count[0], modulus[local], 0.0)
        entries = [scale] + [near[w, local].astype(f32) for w in range(near.shape[0])]
        for number, entry in enumerate(entries):
            table = jnp.where(jnp.logical_and(row == local, lane == number), entry, table)
    out[12] = table


def join_kernel(*refs):
    for number, part in enumerate(refs[:-1]):
        refs[-1][number] = part[...]


def encode(target, block, local):
    return (target * 256 + block) * 16 + local


def pair_loop(filled, pairs, src, centres, feats, sums, per_dev, dummy):
    for extra in range(2):
        pairs[filled + extra] = encode(0, dummy, 0)

    def some(first, count):
        targets = []

        def fetch(part):
            code = pairs[first + part]
            local = code & 15
            block = (code >> 4) & 255
            target = code >> 12
            targets.append(target)
            kind = lax.div(target, per_dev)
            slot = lax.rem(target, per_dev)
            y = [
                src[block, k, pl.ds(local, 1), :] - centres[kind, k, pl.ds(slot, 1), :]
                for k in range(3)
            ]
            f = [src[block, 3 + k, pl.ds(local, 1), :] for k in range(3)]
            return y, f, feats[target]

        found = sums_of_pairs(fetch, count)
        for target, value in zip(targets, found):
            sums[target] += value

    whole = lax.div(filled + 1, 4)

    def four(step, carry):
        some(step * 4, 4)
        return carry

    lax.fori_loop(0, whole, four, 0)

    @pl.when(whole * 4 < filled)
    def _():
        some(whole * 4, 2)


def list_pairs(stage, groups, per_dev, blocks, neighbours, near, meta, pairs):
    n_list = neighbours.shape[1]
    n_near = near.shape[0]
    segment = lax.axis_index("seg")
    member = lax.axis_index("cell")
    seg_cells = groups * per_dev

    def place(number):
        relative = number - (segment - 1) * seg_cells
        side = lax.div(relative, seg_cells)
        inside = lax.rem(relative, seg_cells)
        turn = lax.rem(member - lax.div(inside, per_dev) + groups, groups)
        if stage == 0:
            here, block = jnp.logical_and(side == 1, turn == 0), 0
        elif stage == 1:
            here, block = jnp.logical_and(side == 1, turn != 0), turn
        else:
            here, block = side != 1, lax.div(side, 2) * groups + turn
        return here, block, lax.rem(inside, per_dev)

    filled = jnp.int32(0)
    for local in range(per_dev):
        alive = meta[blocks, local, 0] != 0.0
        for n in range(n_list + n_near):
            shift = blocks if n >= n_list else 0
            here, block, other = place(near[n - n_list, local] if shift else neighbours[local, n])
            pairs[filled] = encode(local, block + shift, other)
            filled = filled + jnp.logical_and(alive, here).astype(jnp.int32)
    first_patch = segment * seg_cells + member * per_dev

    def scan(block, filled):
        for local in range(per_dev):
            alive = meta[block, local, 0] != 0.0
            for w in range(n_near):
                patch = meta[block, local, 1 + w].astype(jnp.int32) - first_patch
                mine = jnp.logical_and(alive, jnp.logical_and(patch >= 0, patch < per_dev))
                pairs[filled] = encode(per_dev + patch, block, local)
                filled = filled + mine.astype(jnp.int32)
        return filled

    return lax.fori_loop(1 if stage == 1 else 0, blocks, scan, filled)


def pairs_kernel(stage, first, last, groups, per_dev, *refs):
    if first:
        (neighbours, near), refs = refs[:2], refs[2:]
    else:
        pairs, refs = refs[0], refs[1:]
    (stiffness, own, own_s), refs = refs[:3], refs[3:]
    if stage == 0:
        windows, (out_tgt, feats, sums), refs = [(own, own_s)], refs[:3], refs[3:]
        centres = out_tgt.at[1]
    elif stage == 1:
        windows, (tgt, feats, sums_in, sums), refs = [refs[:2]], refs[2:6], refs[6:]
        centres = tgt.at[1]
    else:
        windows, (tgt, feats, sums_in, layered), refs = [refs[:2], refs[2:4]], refs[4:8], refs[8:]
        centres = tgt.at[1]
        outs, refs = refs[: 3 if last else 1], refs[3 if last else 1 :]
    if first:
        pairs, refs = refs[0], refs[1:]
        meta, sems = refs[-2:]
    src = refs[0]
    if stage == 2:
        sums = refs[1]
    points = src.shape[-1]
    each = windows[0][0].shape[0]
    blocks = each * len(windows)
    dummy = 2 * blocks
    copies = []
    if first:
        copies.append(pltpu.make_async_copy(
            own_s.at[pl.ds(0, 1), 12, :, pl.ds(0, 128)], meta.at[pl.ds(blocks, 1)], sems.at[0]))
        for side, (moving, fixed) in enumerate(windows):
            cells = pl.ds(side * each, each)
            copies.append(pltpu.make_async_copy(
                fixed.at[:, 12, :, pl.ds(0, 128)], meta.at[cells], sems.at[1 + side]))
    for copy in copies:
        copy.start()

    src[dummy] = jnp.zeros(src.shape[1:], f32)
    tiles = []
    for side, (moving, fixed) in enumerate(windows):
        for block in range(each):
            number = side * each + block
            for k in range(3):
                tiles.append(moving[block, k] - fixed[block, 6 + k])
                src[number, k] = moving[block, k]
                src[blocks + number, k] = fixed[block, 9 + k]
                src[blocks + number, 3 + k] = moving[block, 3 + k]
    offset = jnp.concatenate(tiles, axis=0).astype(bf16)
    pushed = lax.dot_general(
        offset, stiffness[...], (((1,), (1,)), ((), ())), preferred_element_type=f32
    )
    row = 0
    for side, (moving, fixed) in enumerate(windows):
        for block in range(each):
            scale = jnp.broadcast_to(fixed[block, 12][:, 0:1], (per_dev, points))
            for k in range(3):
                src[side * each + block, 3 + k] = scale * pushed[row : row + per_dev]
                row += per_dev

    if stage == 0:
        for kind in range(2):
            for k in range(3):
                tile = (own[0, k], own_s[0, 9 + k])[kind]
                centre = jnp.mean(tile, axis=1, keepdims=True)
                out_tgt[1, kind, k] = jnp.broadcast_to(centre, tile.shape)
                out_tgt[0, kind, k] = tile - centre
        for kind in range(2):
            for local in range(per_dev):
                x = [out_tgt[0, kind, k, local : local + 1, :] for k in range(3)]
                feats[kind * per_dev + local] = target_features(x)
        sums[...] = jnp.zeros(sums.shape, f32)
    else:
        sums[...] = sums_in[...]
    for copy in copies:
        copy.wait()
    if first:
        filled = list_pairs(stage, groups, per_dev, blocks, neighbours, near, meta, pairs)
        pairs[pairs.shape[0] - 1] = filled
    else:
        filled = pairs[pairs.shape[0] - 1]
    pair_loop(filled, pairs, src, centres, feats, sums, per_dev, dummy)
    if stage < 2:
        return

    for local in range(per_dev):
        slot = slice(local, local + 1)
        velocity = combine(sums[local], [tgt[0, 0, k, slot, :] for k in range(3)])
        wall_velocity = combine(sums[per_dev + local], [tgt[0, 1, k, slot, :] for k in range(3)])
        for k in range(3):
            position = own[0, k, slot, :] + time_step * velocity[k]
            density = own[0, 3 + k, slot, :]
            density = density - relax_factor * (
                wall_velocity[k] + 0.5 * density + layered[k, slot, :]
            )
            if last:
                outs[0][k, slot, :] = position
                outs[1][k, slot, :] = velocity[k]
                outs[2][k, slot, :] = density
            else:
                outs[0][k, slot, :] = position
                outs[0][3 + k, slot, :] = density


def cell_blocks(block):
    groups = lax.axis_size("cell")
    return [block] + [
        lax.ppermute(block, "cell", [(i, (i + shift) % groups) for i in range(groups)])
        for shift in range(1, groups)
    ]


def sides(window):
    count = lax.axis_size("seg")
    forward = [(i, i + 1) for i in range(count - 1)]
    backward = [(target, source) for source, target in forward]
    return lax.ppermute(window, "seg", forward), lax.ppermute(window, "seg", backward)


smem = pl.BlockSpec(memory_space=pltpu.SMEM)
vmem = pl.BlockSpec(memory_space=pltpu.VMEM)
anywhere = pl.BlockSpec(memory_space=pl.ANY)


def pack(modulus, seg_count, near, arrays):
    _, per_dev, points = arrays[0].shape
    return pl.pallas_call(
        pack_kernel,
        out_shape=jax.ShapeDtypeStruct((13, per_dev, points), f32),
        in_specs=[anywhere] * 7,
        out_specs=vmem,
        scratch_shapes=[
            pltpu.SemaphoreType.DMA((7,)),
            pltpu.SMEM(modulus.shape, f32),
            pltpu.SMEM(seg_count.shape, jnp.int32),
            pltpu.SMEM(near.shape, jnp.int32),
        ],
        name="pack",
    )(modulus, seg_count, near, *arrays)


def join(parts):
    return pl.pallas_call(
        join_kernel,
        out_shape=jax.ShapeDtypeStruct((len(parts), *parts[0].shape), f32),
        in_specs=[vmem] * len(parts),
        out_specs=vmem,
        name="join",
    )(*parts)


def run_stage(stage, first, last, groups, per_dev, points, lists, entries, stiffness, own, arrays):
    blocks = (1, groups, 2 * groups)[stage]
    carried = [
        jax.ShapeDtypeStruct((2, 2, 3, per_dev, points), f32),
        jax.ShapeDtypeStruct((2 * per_dev, 48, points), bf16),
        jax.ShapeDtypeStruct((2 * per_dev, 24, points), f32),
    ]
    if stage == 0:
        shapes = carried
    elif stage == 1:
        shapes = carried[2:]
    elif last:
        shapes = [jax.ShapeDtypeStruct((3, per_dev, points), f32)] * 3
    else:
        shapes = [jax.ShapeDtypeStruct((6, per_dev, points), f32)]
    scratch = [pltpu.VMEM((2 * blocks + 1, 6, per_dev, points), f32)]
    if stage == 2:
        scratch.append(pltpu.VMEM(carried[2].shape, f32))
    out_specs = [vmem] * len(shapes)
    if first:
        shapes = shapes + [jax.ShapeDtypeStruct((entries + 4,), jnp.int32)]
        out_specs = out_specs + [smem]
        scratch += [
            pltpu.SMEM((blocks + 1, per_dev, 128), f32),
            pltpu.SemaphoreType.DMA((3,)),
        ]
    pair_count = 8 if stage < 2 else 24
    return pl.pallas_call(
        functools.partial(pairs_kernel, stage, first, last, groups, per_dev),
        out_shape=shapes,
        in_specs=[smem] * len(lists) + [vmem] * (3 + len(arrays)),
        out_specs=out_specs,
        scratch_shapes=scratch,
        cost_estimate=pl.CostEstimate(
            flops=pair_count * 2 * points * points * 512, transcendentals=0,
            bytes_accessed=1 << 20,
        ),
        compiler_params=pltpu.CompilerParams(vmem_limit_bytes=32 * 1024 * 1024),
        name=("own_pairs", "segment_pairs", "outer_pairs")[stage],
    )(*lists, stiffness, *own, *arrays)


def body(
    positions, rest_shape, modulus, stiffness, wall_points, density,
    wall_operator, seg_count, neighbours, near_patches,
):
    per_dev, _, points = positions.shape
    groups = lax.axis_size("cell")
    near = near_patches.T
    turn = lambda array: jnp.transpose(array, (1, 0, 2))
    positions, rest_shape, wall_points, density = map(
        turn, (positions, rest_shape, wall_points, density)
    )

    def layer(density):
        return lax.dot_general(
            density, wall_operator, (((2,), (1,)), ((), ())), precision=highest
        )

    fixed = pack(modulus, seg_count, near, (positions, rest_shape, wall_points, density))
    moving = fixed
    lists = [(neighbours, near)] * 3
    windows = ()
    for repeat in range(STEPS):
        first = repeat == 0
        last = repeat == STEPS - 1
        stage = functools.partial(
            run_stage, groups=groups, per_dev=per_dev, points=points, first=first, last=last,
            stiffness=stiffness, own=(moving[None], fixed[None]),
            entries=3 * groups * per_dev * near.size // per_dev + neighbours.size + near.size,
        )
        parts = cell_blocks(moving)
        layered = layer(moving[3:6])
        tgt, feats, sums, *listed = stage(0, lists=lists[0], arrays=())
        parts, sums, layered = lax.optimization_barrier((parts, sums, layered))
        window = join(parts)
        low, high = sides(window)
        if first:
            windows = (window, low, high)
        sums, *more = stage(1, lists=lists[1], arrays=(window, windows[0], tgt, feats, sums))
        outs = stage(
            2, lists=lists[2],
            arrays=(low, windows[1], high, windows[2], tgt, feats, sums, layered),
        )
        if first:
            lists = [listed, more, outs[-1:]]
        moving = outs[0]
    return tuple(map(turn, outs))


def solution(mesh):
    both = P(("seg", "cell"), None, None)
    placed = (
        both, both, P(("seg", "cell")), P(), both, both, P(), P("seg"),
        P(("seg", "cell"), None), P(("seg", "cell"), None),
    )
    return jax.shard_map(
        body, mesh=mesh, in_specs=placed, out_specs=(both, both, both), check_vma=False
    )
```

```python
import functools

import jax
import jax.numpy as jnp
from jax import lax
from jax.experimental import pallas as pl
from jax.experimental.pallas import tpu as pltpu
from jax.sharding import PartitionSpec as P

soften_square = 0.25
stokes_factor = 0.039788735772973836
relax_factor = 0.5
time_step = 0.5
bf16 = jnp.bfloat16
f32 = jnp.float32
highest = lax.Precision.HIGHEST
STEPS = 2


def row_places(points):
    return lax.broadcasted_iota(jnp.int32, (8, points), 0)


def tall(row):
    return jnp.broadcast_to(row, (8, row.shape[1]))


def parts_of(value):
    first = value.astype(bf16).astype(f32)
    rest = value - first
    second = rest.astype(bf16).astype(f32)
    third = (rest - second).astype(bf16).astype(f32)
    return first, second, third


def target_features(x):
    points = x[0].shape[1]
    place = row_places(points)
    square = x[0] * x[0] + x[1] * x[1] + x[2] * x[2]
    rows = jnp.where(place == 3, 1.0, 0.0)
    for number, row in ((0, x[0]), (1, x[1]), (2, x[2]), (4, square)):
        rows = jnp.where(place == number, tall(row), rows)
    high, middle, low = parts_of(rows)
    return jnp.concatenate([high, middle, high, low, high, middle], axis=0).astype(bf16)


def source_rows(y, f):
    place = row_places(y[0].shape[1])
    low_half = place < 4
    lane = place & 3
    square = tall(y[0] * y[0] + y[1] * y[1] + y[2] * y[2])
    along = tall(-(y[0] * f[0] + y[1] * f[1] + y[2] * f[2]))
    y = [tall(row) for row in y]
    f = [tall(row) for row in f]
    points_one = jnp.where(lane == 0, y[0], jnp.where(lane == 1, y[1], jnp.where(lane == 2, y[2], 1.0)))
    source = jnp.where(
        place < 3, -2 * points_one,
        jnp.where(place == 3, square + soften_square, jnp.where(place == 4, 1.0, 0.0)),
    )
    high, middle, low = parts_of(source)
    wide = jnp.concatenate([high, high, middle, high, low, middle], axis=0).astype(bf16)
    one = jnp.where(low_half, f[0], f[1]) * points_one
    two = jnp.where(low_half, f[2], along) * points_one
    three = jnp.where(lane == 0, f[0], jnp.where(lane == 1, f[1], f[2])) * square
    moments = jnp.concatenate(parts_of(jnp.concatenate([one, two, three], axis=0)), axis=0)
    return wide.T, moments.astype(bf16)


def sums_of_pairs(fetch, count):
    held = []

    def distance(unit):
        pair, half = divmod(unit, 2)
        if half == 0:
            y, f, features = fetch(pair)
            held.append((*source_rows(y, f), features))
        wide, _, features = held[pair]
        rows = wide.shape[0] // 2
        return jnp.dot(wide[half * rows : (half + 1) * rows], features, preferred_element_type=f32)

    def moment_sums(unit, distance):
        pair, half = divmod(unit, 2)
        inverse = lax.rsqrt(distance)
        cubed = (inverse * inverse * inverse).astype(bf16)
        moments = held[pair][1]
        rows = moments.shape[1] // 2
        return jnp.dot(
            moments[:, half * rows : (half + 1) * rows], cubed, preferred_element_type=f32
        )

    ready = [distance(0), distance(1)]
    out = []
    for unit in range(2 * count):
        if unit + 2 < 2 * count:
            ready.append(distance(unit + 2))
        sums = moment_sums(unit, ready[unit])
        if unit % 2 == 0:
            first = sums
        else:
            sums = first + sums
            out.append(sums[0:24] + sums[24:48] + sums[48:72])
    return out


def combine(sums, x):
    cross = [[sums[4 * m + k : 4 * m + k + 1] for k in range(3)] for m in range(3)]
    total = [sums[4 * m + 3 : 4 * m + 4] for m in range(3)]
    square = x[0] * x[0] + x[1] * x[1] + x[2] * x[2] + soften_square
    weight = x[0] * total[0] + x[1] * total[1] + x[2] * total[2] + sums[15:16]
    out = []
    for k in range(3):
        moment = x[0] * cross[0][k] + x[1] * cross[1][k] + x[2] * cross[2][k] + sums[12 + k : 13 + k]
        turned = x[0] * cross[k][0] + x[1] * cross[k][1] + x[2] * cross[k][2]
        direct = square * total[k] + sums[16 + k : 17 + k] - 2 * turned
        out.append(stokes_factor * (direct + x[k] * weight - moment))
    return out


def pack_kernel(*refs):
    modulus, count, near, positions, rest_shape, wall_points, density, out, sems = refs[:9]
    held = refs[9:]
    per_dev = positions.shape[1]
    copies = [
        pltpu.make_async_copy(array, target, sems.at[number])
        for number, (array, target) in enumerate(zip((modulus, count, near), held))
    ]
    for number, array in enumerate((positions, density, rest_shape, wall_points)):
        copies.append(pltpu.make_async_copy(array, out.at[pl.ds(3 * number, 3)], sems.at[3 + number]))
    for copy in copies:
        copy.start()
    for copy in copies:
        copy.wait()
    modulus, count, near = held
    shape = out.shape[1:]
    row = lax.broadcasted_iota(jnp.int32, shape, 0)
    lane = lax.broadcasted_iota(jnp.int32, shape, 1)
    table = jnp.zeros(shape, f32)
    first = lax.axis_index("cell") * per_dev
    for local in range(per_dev):
        scale = jnp.where(first + local < count[0], modulus[local], 0.0)
        entries = [scale] + [near[w, local].astype(f32) for w in range(near.shape[0])]
        for number, entry in enumerate(entries):
            table = jnp.where(jnp.logical_and(row == local, lane == number), entry, table)
    out[12] = table


def join_kernel(*refs):
    for number, part in enumerate(refs[:-1]):
        refs[-1][number] = part[...]


def encode(target, block, local):
    return (target * 256 + block) * 16 + local


def pair_loop(filled, pairs, src, centres, feats, sums, per_dev, dummy):
    for extra in range(2):
        pairs[filled + extra] = encode(0, dummy, 0)

    def some(first, count):
        targets = []

        def fetch(part):
            code = pairs[first + part]
            local = code & 15
            block = (code >> 4) & 255
            target = code >> 12
            targets.append(target)
            kind = lax.div(target, per_dev)
            slot = lax.rem(target, per_dev)
            y = [
                src[block, k, pl.ds(local, 1), :] - centres[kind, k, pl.ds(slot, 1), :]
                for k in range(3)
            ]
            f = [src[block, 3 + k, pl.ds(local, 1), :] for k in range(3)]
            return y, f, feats[target]

        found = sums_of_pairs(fetch, count)
        for target, value in zip(targets, found):
            sums[target] += value

    whole = lax.div(filled + 1, 4)

    def four(step, carry):
        some(step * 4, 4)
        return carry

    lax.fori_loop(0, whole, four, 0)

    @pl.when(whole * 4 < filled)
    def _():
        some(whole * 4, 2)


def list_pairs(stage, groups, per_dev, blocks, neighbours, near, meta, pairs):
    n_list = neighbours.shape[1]
    n_near = near.shape[0]
    segment = lax.axis_index("seg")
    member = lax.axis_index("cell")
    seg_cells = groups * per_dev

    def place(number):
        relative = number - (segment - 1) * seg_cells
        side = lax.div(relative, seg_cells)
        inside = lax.rem(relative, seg_cells)
        turn = lax.rem(member - lax.div(inside, per_dev) + groups, groups)
        if stage == 0:
            here, block = jnp.logical_and(side == 1, turn == 0), 0
        elif stage == 1:
            here, block = jnp.logical_and(side == 1, turn != 0), turn
        else:
            here, block = side != 1, lax.div(side, 2) * groups + turn
        return here, block, lax.rem(inside, per_dev)

    filled = jnp.int32(0)
    for local in range(per_dev):
        alive = meta[blocks, local, 0] != 0.0
        for n in range(n_list + n_near):
            shift = blocks if n >= n_list else 0
            here, block, other = place(near[n - n_list, local] if shift else neighbours[local, n])
            pairs[filled] = encode(local, block + shift, other)
            filled = filled + jnp.logical_and(alive, here).astype(jnp.int32)
    first_patch = segment * seg_cells + member * per_dev

    def scan(block, filled):
        for local in range(per_dev):
            alive = meta[block, local, 0] != 0.0
            for w in range(n_near):
                patch = meta[block, local, 1 + w].astype(jnp.int32) - first_patch
                mine = jnp.logical_and(alive, jnp.logical_and(patch >= 0, patch < per_dev))
                pairs[filled] = encode(per_dev + patch, block, local)
                filled = filled + mine.astype(jnp.int32)
        return filled

    return lax.fori_loop(1 if stage == 1 else 0, blocks, scan, filled)


def pairs_kernel(stage, first, last, groups, per_dev, *refs):
    if first:
        (neighbours, near), refs = refs[:2], refs[2:]
    else:
        pairs, refs = refs[0], refs[1:]
    (stiffness, own, own_s), refs = refs[:3], refs[3:]
    if stage == 0:
        windows, (out_tgt, feats, sums), refs = [(own, own_s)], refs[:3], refs[3:]
        centres = out_tgt.at[1]
    elif stage == 1:
        windows, (tgt, feats, sums_in, sums), refs = [refs[:2]], refs[2:6], refs[6:]
        centres = tgt.at[1]
    else:
        windows, (tgt, feats, sums_in, layered), refs = [refs[:2], refs[2:4]], refs[4:8], refs[8:]
        centres = tgt.at[1]
        outs, refs = refs[: 3 if last else 1], refs[3 if last else 1 :]
    if first:
        pairs, refs = refs[0], refs[1:]
        meta, sems = refs[-2:]
    src = refs[0]
    if stage == 2:
        sums = refs[1]
    points = src.shape[-1]
    each = windows[0][0].shape[0]
    blocks = each * len(windows)
    dummy = 2 * blocks
    copies = []
    if first:
        copies.append(pltpu.make_async_copy(
            own_s.at[pl.ds(0, 1), 12, :, pl.ds(0, 128)], meta.at[pl.ds(blocks, 1)], sems.at[0]))
        for side, (moving, fixed) in enumerate(windows):
            cells = pl.ds(side * each, each)
            copies.append(pltpu.make_async_copy(
                fixed.at[:, 12, :, pl.ds(0, 128)], meta.at[cells], sems.at[1 + side]))
    for copy in copies:
        copy.start()

    src[dummy] = jnp.zeros(src.shape[1:], f32)
    tiles = []
    for side, (moving, fixed) in enumerate(windows):
        for block in range(each):
            number = side * each + block
            for k in range(3):
                tiles.append(moving[block, k] - fixed[block, 6 + k])
                src[number, k] = moving[block, k]
                src[blocks + number, k] = fixed[block, 9 + k]
                src[blocks + number, 3 + k] = moving[block, 3 + k]
    offset = jnp.concatenate(tiles, axis=0).astype(bf16)
    pushed = lax.dot_general(
        offset, stiffness[...], (((1,), (1,)), ((), ())), preferred_element_type=f32
    )
    row = 0
    for side, (moving, fixed) in enumerate(windows):
        for block in range(each):
            scale = jnp.broadcast_to(fixed[block, 12][:, 0:1], (per_dev, points))
            for k in range(3):
                src[side * each + block, 3 + k] = scale * pushed[row : row + per_dev]
                row += per_dev

    if stage == 0:
        for kind in range(2):
            for k in range(3):
                tile = (own[0, k], own_s[0, 9 + k])[kind]
                centre = jnp.mean(tile, axis=1, keepdims=True)
                out_tgt[1, kind, k] = jnp.broadcast_to(centre, tile.shape)
                out_tgt[0, kind, k] = tile - centre
        for kind in range(2):
            for local in range(per_dev):
                x = [out_tgt[0, kind, k, local : local + 1, :] for k in range(3)]
                feats[kind * per_dev + local] = target_features(x)
        sums[...] = jnp.zeros(sums.shape, f32)
    else:
        sums[...] = sums_in[...]
    for copy in copies:
        copy.wait()
    if first:
        filled = list_pairs(stage, groups, per_dev, blocks, neighbours, near, meta, pairs)
        pairs[pairs.shape[0] - 1] = filled
    else:
        filled = pairs[pairs.shape[0] - 1]
    pair_loop(filled, pairs, src, centres, feats, sums, per_dev, dummy)
    if stage < 2:
        return

    for local in range(per_dev):
        slot = slice(local, local + 1)
        velocity = combine(sums[local], [tgt[0, 0, k, slot, :] for k in range(3)])
        wall_velocity = combine(sums[per_dev + local], [tgt[0, 1, k, slot, :] for k in range(3)])
        for k in range(3):
            position = own[0, k, slot, :] + time_step * velocity[k]
            density = own[0, 3 + k, slot, :]
            density = density - relax_factor * (
                wall_velocity[k] + 0.5 * density + layered[k, slot, :]
            )
            if last:
                outs[0][k, slot, :] = position
                outs[1][k, slot, :] = velocity[k]
                outs[2][k, slot, :] = density
            else:
                outs[0][k, slot, :] = position
                outs[0][3 + k, slot, :] = density


def cell_blocks(block):
    groups = lax.axis_size("cell")
    return [block] + [
        lax.ppermute(block, "cell", [(i, (i + shift) % groups) for i in range(groups)])
        for shift in range(1, groups)
    ]


def sides(window):
    count = lax.axis_size("seg")
    forward = [(i, i + 1) for i in range(count - 1)]
    backward = [(target, source) for source, target in forward]
    return lax.ppermute(window, "seg", forward), lax.ppermute(window, "seg", backward)


smem = pl.BlockSpec(memory_space=pltpu.SMEM)
vmem = pl.BlockSpec(memory_space=pltpu.VMEM)
anywhere = pl.BlockSpec(memory_space=pl.ANY)


def pack(modulus, seg_count, near, arrays):
    _, per_dev, points = arrays[0].shape
    return pl.pallas_call(
        pack_kernel,
        out_shape=jax.ShapeDtypeStruct((13, per_dev, points), f32),
        in_specs=[anywhere] * 7,
        out_specs=vmem,
        scratch_shapes=[
            pltpu.SemaphoreType.DMA((7,)),
            pltpu.SMEM(modulus.shape, f32),
            pltpu.SMEM(seg_count.shape, jnp.int32),
            pltpu.SMEM(near.shape, jnp.int32),
        ],
        compiler_params=pltpu.CompilerParams(vmem_limit_bytes=4 * 1024 * 1024),
        name="pack",
    )(modulus, seg_count, near, *arrays)


def join(parts):
    return pl.pallas_call(
        join_kernel,
        out_shape=jax.ShapeDtypeStruct((len(parts), *parts[0].shape), f32),
        in_specs=[vmem] * len(parts),
        out_specs=vmem,
        compiler_params=pltpu.CompilerParams(vmem_limit_bytes=4 * 1024 * 1024),
        name="join",
    )(*parts)


def run_stage(stage, first, last, groups, per_dev, points, lists, entries, stiffness, own, arrays):
    blocks = (1, groups, 2 * groups)[stage]
    carried = [
        jax.ShapeDtypeStruct((2, 2, 3, per_dev, points), f32),
        jax.ShapeDtypeStruct((2 * per_dev, 48, points), bf16),
        jax.ShapeDtypeStruct((2 * per_dev, 24, points), f32),
    ]
    if stage == 0:
        shapes = carried
    elif stage == 1:
        shapes = carried[2:]
    elif last:
        shapes = [jax.ShapeDtypeStruct((3, per_dev, points), f32)] * 3
    else:
        shapes = [jax.ShapeDtypeStruct((6, per_dev, points), f32)]
    scratch = [pltpu.VMEM((2 * blocks + 1, 6, per_dev, points), f32)]
    if stage == 2:
        scratch.append(pltpu.VMEM(carried[2].shape, f32))
    out_specs = [vmem] * len(shapes)
    if first:
        shapes = shapes + [jax.ShapeDtypeStruct((entries + 4,), jnp.int32)]
        out_specs = out_specs + [smem]
        scratch += [
            pltpu.SMEM((blocks + 1, per_dev, 128), f32),
            pltpu.SemaphoreType.DMA((3,)),
        ]
    pair_count = 8 if stage < 2 else 24
    return pl.pallas_call(
        functools.partial(pairs_kernel, stage, first, last, groups, per_dev),
        out_shape=shapes,
        in_specs=[smem] * len(lists) + [vmem] * (3 + len(arrays)),
        out_specs=out_specs,
        scratch_shapes=scratch,
        cost_estimate=pl.CostEstimate(
            flops=pair_count * 2 * points * points * 512, transcendentals=0,
            bytes_accessed=1 << 20,
        ),
        compiler_params=pltpu.CompilerParams(vmem_limit_bytes=16 * 1024 * 1024),
        name=("own_pairs", "segment_pairs", "outer_pairs")[stage],
    )(*lists, stiffness, *own, *arrays)


def body(
    positions, rest_shape, modulus, stiffness, wall_points, density,
    wall_operator, seg_count, neighbours, near_patches,
):
    per_dev, _, points = positions.shape
    groups = lax.axis_size("cell")
    near = near_patches.T
    turn = lambda array: jnp.transpose(array, (1, 0, 2))
    positions, rest_shape, wall_points, density = map(
        turn, (positions, rest_shape, wall_points, density)
    )

    def layer(density):
        return lax.dot_general(
            density, wall_operator, (((2,), (1,)), ((), ())), precision=highest
        )

    fixed = pack(modulus, seg_count, near, (positions, rest_shape, wall_points, density))
    moving = fixed
    lists = [(neighbours, near)] * 3
    windows = ()
    for repeat in range(STEPS):
        first = repeat == 0
        last = repeat == STEPS - 1
        stage = functools.partial(
            run_stage, groups=groups, per_dev=per_dev, points=points, first=first, last=last,
            stiffness=stiffness, own=(moving[None], fixed[None]),
            entries=3 * groups * per_dev * near.size // per_dev + neighbours.size + near.size,
        )
        parts = cell_blocks(moving)
        layered = layer(moving[3:6])
        tgt, feats, sums, *listed = stage(0, lists=lists[0], arrays=())
        parts, sums, layered = lax.optimization_barrier((parts, sums, layered))
        window = join(parts)
        low, high = sides(window)
        if first:
            windows = (window, low, high)
        sums, *more = stage(1, lists=lists[1], arrays=(window, windows[0], tgt, feats, sums))
        outs = stage(
            2, lists=lists[2],
            arrays=(low, windows[1], high, windows[2], tgt, feats, sums, layered),
        )
        if first:
            lists = [listed, more, outs[-1:]]
        moving = outs[0]
    return tuple(map(turn, outs))


def solution(mesh):
    both = P(("seg", "cell"), None, None)
    placed = (
        both, both, P(("seg", "cell")), P(), both, both, P(), P("seg"),
        P(("seg", "cell"), None), P(("seg", "cell"), None),
    )
    return jax.shard_map(
        body, mesh=mesh, in_specs=placed, out_specs=(both, both, both), check_vma=False
    )
```

```python
import functools

import jax
import jax.numpy as jnp
from jax import lax
from jax.experimental import pallas as pl
from jax.experimental.pallas import tpu as pltpu
from jax.sharding import PartitionSpec as P

soften_square = 0.25
stokes_factor = 0.039788735772973836
relax_factor = 0.5
time_step = 0.5
bf16 = jnp.bfloat16
f32 = jnp.float32
STEPS = 2


def row_places(points):
    return lax.broadcasted_iota(jnp.int32, (8, points), 0)


def tall(row):
    return jnp.broadcast_to(row, (8, row.shape[1]))


def parts_of(value):
    first = value.astype(bf16).astype(f32)
    rest = value - first
    second = rest.astype(bf16).astype(f32)
    third = (rest - second).astype(bf16).astype(f32)
    return first, second, third


def target_features(x):
    points = x[0].shape[1]
    place = row_places(points)
    square = x[0] * x[0] + x[1] * x[1] + x[2] * x[2]
    rows = jnp.where(place == 3, 1.0, 0.0)
    for number, row in ((0, x[0]), (1, x[1]), (2, x[2]), (4, square)):
        rows = jnp.where(place == number, tall(row), rows)
    high, middle, low = parts_of(rows)
    return jnp.concatenate([high, middle, high, low, high, middle], axis=0).astype(bf16)


def source_rows(y, f):
    place = row_places(y[0].shape[1])
    low_half = place < 4
    lane = place & 3
    square = tall(y[0] * y[0] + y[1] * y[1] + y[2] * y[2])
    along = tall(-(y[0] * f[0] + y[1] * f[1] + y[2] * f[2]))
    y = [tall(row) for row in y]
    f = [tall(row) for row in f]
    points_one = jnp.where(lane == 0, y[0], jnp.where(lane == 1, y[1], jnp.where(lane == 2, y[2], 1.0)))
    source = jnp.where(
        place < 3, -2 * points_one,
        jnp.where(place == 3, square + soften_square, jnp.where(place == 4, 1.0, 0.0)),
    )
    high, middle, low = parts_of(source)
    wide = jnp.concatenate([high, high, middle, high, low, middle], axis=0).astype(bf16)
    one = jnp.where(low_half, f[0], f[1]) * points_one
    two = jnp.where(low_half, f[2], along) * points_one
    three = jnp.where(lane == 0, f[0], jnp.where(lane == 1, f[1], f[2])) * square
    moments = jnp.concatenate(parts_of(jnp.concatenate([one, two, three], axis=0)), axis=0)
    return wide.T, moments.astype(bf16)


def sums_of_pairs(fetch, count):
    held = []

    def distance(unit):
        pair, half = divmod(unit, 2)
        if half == 0:
            y, f, features = fetch(pair)
            held.append((*source_rows(y, f), features))
        wide, _, features = held[pair]
        rows = wide.shape[0] // 2
        return jnp.dot(wide[half * rows : (half + 1) * rows], features, preferred_element_type=f32)

    def moment_sums(unit, distance):
        pair, half = divmod(unit, 2)
        inverse = lax.rsqrt(distance)
        cubed = (inverse * inverse * inverse).astype(bf16)
        moments = held[pair][1]
        rows = moments.shape[1] // 2
        return jnp.dot(
            moments[:, half * rows : (half + 1) * rows], cubed, preferred_element_type=f32
        )

    ready = [distance(0), distance(1)]
    out = []
    for unit in range(2 * count):
        if unit + 2 < 2 * count:
            ready.append(distance(unit + 2))
        sums = moment_sums(unit, ready[unit])
        if unit % 2 == 0:
            first = sums
        else:
            sums = first + sums
            out.append(sums[0:24] + sums[24:48] + sums[48:72])
    return out


def combine(sums, x):
    cross = [[sums[4 * m + k : 4 * m + k + 1] for k in range(3)] for m in range(3)]
    total = [sums[4 * m + 3 : 4 * m + 4] for m in range(3)]
    square = x[0] * x[0] + x[1] * x[1] + x[2] * x[2] + soften_square
    weight = x[0] * total[0] + x[1] * total[1] + x[2] * total[2] + sums[15:16]
    out = []
    for k in range(3):
        moment = x[0] * cross[0][k] + x[1] * cross[1][k] + x[2] * cross[2][k] + sums[12 + k : 13 + k]
        turned = x[0] * cross[k][0] + x[1] * cross[k][1] + x[2] * cross[k][2]
        direct = square * total[k] + sums[16 + k : 17 + k] - 2 * turned
        out.append(stokes_factor * (direct + x[k] * weight - moment))
    return out


def pack_kernel(*refs):
    modulus, count, near, positions, rest_shape, wall_points, density, out, sems = refs[:9]
    held = refs[9:]
    per_dev = positions.shape[1]
    copies = [
        pltpu.make_async_copy(array, target, sems.at[number])
        for number, (array, target) in enumerate(zip((modulus, count, near), held))
    ]
    for number, array in enumerate((positions, density, rest_shape, wall_points)):
        copies.append(pltpu.make_async_copy(array, out.at[pl.ds(3 * number, 3)], sems.at[3 + number]))
    for copy in copies:
        copy.start()
    for copy in copies:
        copy.wait()
    modulus, count, near = held
    shape = out.shape[1:]
    row = lax.broadcasted_iota(jnp.int32, shape, 0)
    lane = lax.broadcasted_iota(jnp.int32, shape, 1)
    table = jnp.zeros(shape, f32)
    first = lax.axis_index("cell") * per_dev
    for local in range(per_dev):
        alive = first + local < count[0]
        entries = [jnp.where(alive, modulus[local], 0.0)]
        entries += [jnp.where(alive, near[w, local] + 1, 0).astype(f32) for w in range(near.shape[0])]
        for number, entry in enumerate(entries):
            table = jnp.where(jnp.logical_and(row == local, lane == number), entry, table)
    out[12] = table


def join_kernel(*refs):
    for number, part in enumerate(refs[:-1]):
        refs[-1][number] = part[...]


def encode(target, block, local):
    return (target * 256 + block) * 16 + local


def pair_loop(filled, pairs, src, centres, feats, sums, per_dev, dummy):
    for extra in range(2):
        pairs[filled + extra] = encode(0, dummy, 0)

    def some(first, count):
        targets = []

        def fetch(part):
            code = pairs[first + part]
            local = code & 15
            block = (code >> 4) & 255
            target = code >> 12
            targets.append(target)
            kind = lax.div(target, per_dev)
            slot = lax.rem(target, per_dev)
            y = [
                src[block, k, pl.ds(local, 1), :] - centres[kind, k, pl.ds(slot, 1), :]
                for k in range(3)
            ]
            f = [src[block, 3 + k, pl.ds(local, 1), :] for k in range(3)]
            return y, f, feats[target]

        found = sums_of_pairs(fetch, count)
        for target, value in zip(targets, found):
            sums[target] += value

    whole = lax.div(filled + 1, 4)

    def four(step, carry):
        some(step * 4, 4)
        return carry

    lax.fori_loop(0, whole, four, 0)

    @pl.when(whole * 4 < filled)
    def _():
        some(whole * 4, 2)


def pair_partner(index, shift, groups):
    if groups & (groups - 1) == 0:
        return index ^ shift
    return (index + shift) % groups


def slot_of(member, other, groups):
    if groups & (groups - 1) == 0:
        return member ^ other
    return lax.rem(member - other + groups, groups)


def list_own(groups, per_dev, neighbours, near, meta, lists):
    n_list = neighbours.shape[1]
    n_near = near.shape[0]
    segment = lax.axis_index("seg")
    member = lax.axis_index("cell")
    seg_cells = groups * per_dev
    start = (segment - 1) * seg_cells
    close_side = 2 - 2 * lax.rem(segment, 2)
    filled = [jnp.int32(0)] * 3
    for local in range(per_dev):
        alive = meta[0, local, 0] != 0.0
        for n in range(n_list + n_near):
            wall = n >= n_list
            relative = (near[n - n_list, local] if wall else neighbours[local, n]) - start
            side = lax.div(relative, seg_cells)
            inside = lax.rem(relative, seg_cells)
            turn = slot_of(member, lax.div(inside, per_dev), groups)
            middle = side == 1
            close = side == close_side
            own = jnp.logical_and(middle, turn == 0)
            where = (
                own,
                jnp.logical_or(jnp.logical_and(middle, turn != 0), close),
                jnp.logical_not(jnp.logical_or(middle, close)),
            )
            blocks = (0, turn + jnp.where(middle, 0, groups), turn)
            for stage, count in enumerate((1, 2 * groups, groups)):
                block = blocks[stage] + (count if wall else 0)
                lists[stage][filled[stage]] = encode(local, block, lax.rem(inside, per_dev))
                here = jnp.logical_and(alive, where[stage])
                filled[stage] = filled[stage] + here.astype(jnp.int32)
    return filled


def list_patches(groups, per_dev, first_block, blocks, n_near, meta, pairs, filled):
    seg_cells = groups * per_dev
    first = lax.axis_index("seg") * seg_cells + lax.axis_index("cell") * per_dev + 1

    def scan(block, filled):
        for local in range(per_dev):
            for w in range(n_near):
                patch = meta[block, local, 1 + w].astype(jnp.int32) - first
                mine = jnp.logical_and(patch >= 0, patch < per_dev)
                pairs[filled] = encode(per_dev + patch, block, local)
                filled = filled + mine.astype(jnp.int32)
        return filled

    return lax.fori_loop(first_block, blocks, scan, filled)


def two_parts(value):
    high = value.astype(bf16)
    return high, (value - high.astype(f32)).astype(bf16)


def layer(density, operator):
    _, per_dev, points = density.shape
    rows = jnp.concatenate([density[k] for k in range(3)] + [jnp.zeros((per_dev, points), f32)], axis=0)
    high, low = two_parts(rows)
    operator_high, operator_low = two_parts(operator[...])
    turned = functools.partial(
        lax.dot_general, dimension_numbers=(((1,), (1,)), ((), ())), preferred_element_type=f32
    )
    count = rows.shape[0]
    main = turned(jnp.concatenate([high, low], axis=0), operator_high)
    total = main[:count] + main[count:] + turned(high, operator_low)
    return [total[k * per_dev : (k + 1) * per_dev] for k in range(3)]


def pairs_kernel(stage, first, last, groups, per_dev, n_near, *refs):
    if first and stage == 0:
        (neighbours, near), refs = refs[:2], refs[2:]
    else:
        listed, refs = refs[0], refs[1:]
    (stiffness, own, own_s), refs = refs[:3], refs[3:]
    if stage == 0:
        windows = [(own, own_s)]
        (operator, out_tgt, feats, sums, out_layer), refs = refs[:5], refs[5:]
        centres = out_tgt.at[1]
        lists, refs = refs[: 3 if first else 0], refs[3 if first else 0 :]
    elif stage == 1:
        windows, (tgt, feats, sums_in, sums), refs = [refs[:2], refs[2:4]], refs[4:8], refs[8:]
        centres = tgt.at[1]
    else:
        windows, (tgt, feats, sums_in, layered), refs = [refs[:2]], refs[2:6], refs[6:]
        centres = tgt.at[1]
        outs, refs = refs[: 3 if last else 1], refs[3 if last else 1 :]
    if not first:
        pairs = listed
    elif stage == 0:
        pairs = lists[0]
    else:
        pairs, refs = refs[0], refs[1:]
    if first:
        meta, sems = refs[-2:]
    src = refs[0]
    if stage == 2:
        sums = refs[1]
    points = src.shape[-1]
    each = windows[0][0].shape[0]
    blocks = each * len(windows)
    dummy = 2 * blocks
    copies = []
    if first:
        for side, (moving, fixed) in enumerate(windows):
            cells = pl.ds(side * each, each)
            copies.append(pltpu.make_async_copy(
                fixed.at[:, 12, :, pl.ds(0, 128)], meta.at[cells], sems.at[side]))
    for copy in copies:
        copy.start()

    src[dummy] = jnp.zeros(src.shape[1:], f32)
    tiles = []
    for side, (moving, fixed) in enumerate(windows):
        for block in range(each):
            number = side * each + block
            for k in range(3):
                tiles.append(moving[block, k] - fixed[block, 6 + k])
                src[number, k] = moving[block, k]
                src[blocks + number, k] = fixed[block, 9 + k]
                src[blocks + number, 3 + k] = moving[block, 3 + k]
    offset = jnp.concatenate(tiles, axis=0).astype(bf16)
    pushed = lax.dot_general(
        offset, stiffness[...], (((1,), (1,)), ((), ())), preferred_element_type=f32
    )
    row = 0
    for side, (moving, fixed) in enumerate(windows):
        for block in range(each):
            scale = jnp.broadcast_to(fixed[block, 12][:, 0:1], (per_dev, points))
            for k in range(3):
                src[side * each + block, 3 + k] = scale * pushed[row : row + per_dev]
                row += per_dev

    if stage == 0:
        for kind in range(2):
            for k in range(3):
                tile = (own[0, k], own_s[0, 9 + k])[kind]
                centre = jnp.mean(tile, axis=1, keepdims=True)
                out_tgt[1, kind, k] = jnp.broadcast_to(centre, tile.shape)
                out_tgt[0, kind, k] = tile - centre
        for kind in range(2):
            for local in range(per_dev):
                x = [out_tgt[0, kind, k, local : local + 1, :] for k in range(3)]
                feats[kind * per_dev + local] = target_features(x)
        sums[...] = jnp.zeros(sums.shape, f32)
        for k, tile in enumerate(layer(own[0, 3:6], operator)):
            out_layer[k] = tile
    else:
        sums[...] = sums_in[...]
    for copy in copies:
        copy.wait()
    end = pairs.shape[0] - 1
    if not first:
        filled = pairs[end]
    else:
        if stage == 0:
            filled, *others = list_own(groups, per_dev, neighbours, near, meta, lists)
            for other, count in zip(lists[1:], others):
                other[end] = count
        else:
            filled = listed[end]

            def take(number, carry):
                pairs[number] = listed[number]
                return carry

            lax.fori_loop(0, filled, take, 0)
        filled = list_patches(
            groups, per_dev, 1 if stage == 1 else 0, blocks, n_near, meta, pairs, filled
        )
        pairs[end] = filled
    pair_loop(filled, pairs, src, centres, feats, sums, per_dev, dummy)
    if stage < 2:
        return

    for local in range(per_dev):
        slot = slice(local, local + 1)
        velocity = combine(sums[local], [tgt[0, 0, k, slot, :] for k in range(3)])
        wall_velocity = combine(sums[per_dev + local], [tgt[0, 1, k, slot, :] for k in range(3)])
        for k in range(3):
            position = own[0, k, slot, :] + time_step * velocity[k]
            density = own[0, 3 + k, slot, :]
            density = density - relax_factor * (
                wall_velocity[k] + 0.5 * density + layered[k, slot, :]
            )
            if last:
                outs[0][k, slot, :] = position
                outs[1][k, slot, :] = velocity[k]
                outs[2][k, slot, :] = density
            else:
                outs[0][k, slot, :] = position
                outs[0][3 + k, slot, :] = density


def cell_blocks(block):
    groups = lax.axis_size("cell")
    return [block] + [
        lax.ppermute(
            block, "cell", [(i, pair_partner(i, shift, groups)) for i in range(groups)]
        )
        for shift in range(1, groups)
    ]


def beside(window):
    count = lax.axis_size("seg")
    close = [(i, i ^ 1) for i in range(count) if i ^ 1 < count]
    other = [(i, i + 1 if i % 2 else i - 1) for i in range(count)]
    other = [(i, j) for i, j in other if 0 <= j < count]
    return lax.ppermute(window, "seg", close), lax.ppermute(window, "seg", other)


smem = pl.BlockSpec(memory_space=pltpu.SMEM)
vmem = pl.BlockSpec(memory_space=pltpu.VMEM)
anywhere = pl.BlockSpec(memory_space=pl.ANY)


def pack(modulus, seg_count, near, arrays):
    _, per_dev, points = arrays[0].shape
    return pl.pallas_call(
        pack_kernel,
        out_shape=jax.ShapeDtypeStruct((13, per_dev, points), f32),
        in_specs=[pl.BlockSpec(memory_space=pltpu.HBM)] * 7,
        out_specs=vmem,
        scratch_shapes=[
            pltpu.SemaphoreType.DMA((7,)),
            pltpu.SMEM(modulus.shape, f32),
            pltpu.SMEM(seg_count.shape, jnp.int32),
            pltpu.SMEM(near.shape, jnp.int32),
        ],
        compiler_params=pltpu.CompilerParams(vmem_limit_bytes=4 * 1024 * 1024),
        name="pack",
    )(modulus, seg_count, near, *arrays)


def join(parts):
    return pl.pallas_call(
        join_kernel,
        out_shape=jax.ShapeDtypeStruct((len(parts), *parts[0].shape), f32),
        in_specs=[vmem] * len(parts),
        out_specs=vmem,
        compiler_params=pltpu.CompilerParams(vmem_limit_bytes=4 * 1024 * 1024),
        name="join",
    )(*parts)


def run_stage(stage, first, last, groups, per_dev, n_near, points, lists, entries, stiffness, own, arrays):
    blocks = (1, 2 * groups, groups)[stage]
    carried = [
        jax.ShapeDtypeStruct((2, 2, 3, per_dev, points), f32),
        jax.ShapeDtypeStruct((2 * per_dev, 48, points), bf16),
        jax.ShapeDtypeStruct((2 * per_dev, 24, points), f32),
    ]
    if stage == 0:
        shapes = carried + [jax.ShapeDtypeStruct((3, per_dev, points), f32)]
    elif stage == 1:
        shapes = carried[2:]
    elif last:
        shapes = [jax.ShapeDtypeStruct((3, per_dev, points), f32)] * 3
    else:
        shapes = [jax.ShapeDtypeStruct((6, per_dev, points), f32)]
    scratch = [pltpu.VMEM((2 * blocks + 1, 6, per_dev, points), f32)]
    if stage == 2:
        scratch.append(pltpu.VMEM(carried[2].shape, f32))
    out_specs = [vmem] * len(shapes)
    if first:
        count = 1 if stage else 3
        shapes = shapes + [jax.ShapeDtypeStruct((entries + 4,), jnp.int32)] * count
        out_specs = out_specs + [smem] * count
        scratch += [
            pltpu.SMEM((blocks, per_dev, 128), f32),
            pltpu.SemaphoreType.DMA((2,)),
        ]
    pair_count = (6, 20, 10)[stage]
    return pl.pallas_call(
        functools.partial(pairs_kernel, stage, first, last, groups, per_dev, n_near),
        out_shape=shapes,
        in_specs=[smem] * len(lists) + [vmem] * (3 + len(arrays)),
        out_specs=out_specs,
        scratch_shapes=scratch,
        cost_estimate=pl.CostEstimate(
            flops=pair_count * 2 * points * points * 512, transcendentals=0,
            bytes_accessed=1 << 20,
        ),
        compiler_params=pltpu.CompilerParams(vmem_limit_bytes=16 * 1024 * 1024),
        name=("own_pairs", "segment_pairs", "outer_pairs")[stage],
    )(*lists, stiffness, *own, *arrays)


def body(
    positions, rest_shape, modulus, stiffness, wall_points, density,
    wall_operator, seg_count, neighbours, near_patches,
):
    per_dev, _, points = positions.shape
    groups = lax.axis_size("cell")
    near = near_patches.T
    turn = lambda array: jnp.transpose(array, (1, 0, 2))
    positions, rest_shape, wall_points, density = map(
        turn, (positions, rest_shape, wall_points, density)
    )

    fixed = pack(modulus, seg_count, near, (positions, rest_shape, wall_points, density))
    moving = fixed
    lists = [(neighbours, near)]
    n_near = near.shape[0]
    entries = neighbours.size + near.size + 3 * groups * near.size
    windows = ()
    for repeat in range(STEPS):
        first = repeat == 0
        last = repeat == STEPS - 1
        stage = functools.partial(
            run_stage, groups=groups, per_dev=per_dev, n_near=n_near, points=points, first=first,
            last=last, stiffness=stiffness, own=(moving[None], fixed[None]), entries=entries,
        )
        parts = cell_blocks(moving)
        tgt, feats, sums, layered, *listed = stage(0, lists=lists[0], arrays=(wall_operator,))
        if first:
            lists = [listed[:1], listed[1:2], listed[2:]]
        parts, sums = lax.optimization_barrier((parts, sums))
        window = join(parts)
        close, other = beside(window)
        if first:
            windows = (window, close, other)
        sums, *listed = stage(
            1, lists=lists[1],
            arrays=(window, windows[0], close, windows[1], tgt, feats, sums),
        )
        outs = stage(2, lists=lists[2], arrays=(other, windows[2], tgt, feats, sums, layered))
        if first:
            lists = [lists[0], listed, outs[1:]]
        moving = outs[0]
    return tuple(map(turn, outs))


def solution(mesh):
    both = P(("seg", "cell"), None, None)
    placed = (
        both, both, P(("seg", "cell")), P(), both, both, P(), P("seg"),
        P(("seg", "cell"), None), P(("seg", "cell"), None),
    )
    return jax.shard_map(
        body, mesh=mesh, in_specs=placed, out_specs=(both, both, both), check_vma=False
    )
```

```python
import functools

import jax
import jax.numpy as jnp
from jax import lax
from jax.experimental import pallas as pl
from jax.experimental.pallas import tpu as pltpu
from jax.sharding import PartitionSpec as P

soften_square = 0.25
stokes_factor = 0.039788735772973836
relax_factor = 0.5
time_step = 0.5
own_most = 8
bf16 = jnp.bfloat16
f32 = jnp.float32
STEPS = 2


def row_places(points):
    return lax.broadcasted_iota(jnp.int32, (8, points), 0)


def tall(row):
    return jnp.broadcast_to(row, (8, row.shape[1]))


def parts_of(value):
    first = value.astype(bf16).astype(f32)
    rest = value - first
    second = rest.astype(bf16).astype(f32)
    third = (rest - second).astype(bf16).astype(f32)
    return first, second, third


def target_features(x):
    points = x[0].shape[1]
    place = row_places(points)
    square = x[0] * x[0] + x[1] * x[1] + x[2] * x[2]
    rows = jnp.where(place == 3, 1.0, 0.0)
    for number, row in ((0, x[0]), (1, x[1]), (2, x[2]), (4, square)):
        rows = jnp.where(place == number, tall(row), rows)
    high, middle, low = parts_of(rows)
    return jnp.concatenate([high, middle, high, low, high, middle], axis=0).astype(bf16)


def source_rows(y, f):
    place = row_places(y[0].shape[1])
    low_half = place < 4
    lane = place & 3
    square = tall(y[0] * y[0] + y[1] * y[1] + y[2] * y[2])
    along = tall(-(y[0] * f[0] + y[1] * f[1] + y[2] * f[2]))
    y = [tall(row) for row in y]
    f = [tall(row) for row in f]
    points_one = jnp.where(lane == 0, y[0], jnp.where(lane == 1, y[1], jnp.where(lane == 2, y[2], 1.0)))
    source = jnp.where(
        place < 3, -2 * points_one,
        jnp.where(place == 3, square + soften_square, jnp.where(place == 4, 1.0, 0.0)),
    )
    high, middle, low = parts_of(source)
    wide = jnp.concatenate([high, high, middle, high, low, middle], axis=0).astype(bf16)
    one = jnp.where(low_half, f[0], f[1]) * points_one
    two = jnp.where(low_half, f[2], along) * points_one
    three = jnp.where(lane == 0, f[0], jnp.where(lane == 1, f[1], f[2])) * square
    moments = jnp.concatenate(parts_of(jnp.concatenate([one, two, three], axis=0)), axis=0)
    return wide.T, moments.astype(bf16)


def sums_of_pairs(fetch, count):
    held = []

    def distance(unit):
        pair, half = divmod(unit, 2)
        if half == 0:
            y, f, features = fetch(pair)
            held.append((*source_rows(y, f), features))
        wide, _, features = held[pair]
        rows = wide.shape[0] // 2
        return jnp.dot(wide[half * rows : (half + 1) * rows], features, preferred_element_type=f32)

    def moment_sums(unit, distance):
        pair, half = divmod(unit, 2)
        inverse = lax.rsqrt(distance)
        cubed = (inverse * inverse * inverse).astype(bf16)
        moments = held[pair][1]
        rows = moments.shape[1] // 2
        return jnp.dot(
            moments[:, half * rows : (half + 1) * rows], cubed, preferred_element_type=f32
        )

    ready = [distance(0), distance(1)]
    out = []
    for unit in range(2 * count):
        if unit + 2 < 2 * count:
            ready.append(distance(unit + 2))
        sums = moment_sums(unit, ready[unit])
        if unit % 2 == 0:
            first = sums
        else:
            sums = first + sums
            out.append(sums[0:24] + sums[24:48] + sums[48:72])
    return out


def combine(sums, x):
    cross = [[sums[4 * m + k : 4 * m + k + 1] for k in range(3)] for m in range(3)]
    total = [sums[4 * m + 3 : 4 * m + 4] for m in range(3)]
    square = x[0] * x[0] + x[1] * x[1] + x[2] * x[2] + soften_square
    weight = x[0] * total[0] + x[1] * total[1] + x[2] * total[2] + sums[15:16]
    out = []
    for k in range(3):
        moment = x[0] * cross[0][k] + x[1] * cross[1][k] + x[2] * cross[2][k] + sums[12 + k : 13 + k]
        turned = x[0] * cross[k][0] + x[1] * cross[k][1] + x[2] * cross[k][2]
        direct = square * total[k] + sums[16 + k : 17 + k] - 2 * turned
        out.append(stokes_factor * (direct + x[k] * weight - moment))
    return out


def pack_kernel(*refs):
    modulus, count, near, positions, rest_shape, wall_points, density, out, sems = refs[:9]
    held = refs[9:]
    per_dev = positions.shape[1]
    copies = [
        pltpu.make_async_copy(array, target, sems.at[number])
        for number, (array, target) in enumerate(zip((modulus, count, near), held))
    ]
    for number, array in enumerate((positions, density, rest_shape, wall_points)):
        copies.append(pltpu.make_async_copy(array, out.at[pl.ds(3 * number, 3)], sems.at[3 + number]))
    for copy in copies:
        copy.start()
    for copy in copies:
        copy.wait()
    modulus, count, near = held
    shape = out.shape[1:]
    row = lax.broadcasted_iota(jnp.int32, shape, 0)
    lane = lax.broadcasted_iota(jnp.int32, shape, 1)
    table = jnp.zeros(shape, f32)
    first = lax.axis_index("cell") * per_dev
    for local in range(per_dev):
        alive = first + local < count[0]
        entries = [jnp.where(alive, modulus[local], 0.0)]
        entries += [jnp.where(alive, near[w, local] + 1, 0).astype(f32) for w in range(near.shape[0])]
        for number, entry in enumerate(entries):
            table = jnp.where(jnp.logical_and(row == local, lane == number), entry, table)
    out[12] = table


def join_kernel(*refs):
    for number, part in enumerate(refs[:-1]):
        refs[-1][number] = part[...]


def encode(target, block, local):
    return (target * 256 + block) * 16 + local


def pair_loop(filled, pairs, src, centres, feats, sums, per_dev, dummy):
    for extra in range(2):
        pairs[filled + extra] = encode(0, dummy, 0)

    def some(first, count):
        targets = []

        def fetch(part):
            code = pairs[first + part]
            local = code & 15
            block = (code >> 4) & 255
            target = code >> 12
            targets.append(target)
            kind = lax.div(target, per_dev)
            slot = lax.rem(target, per_dev)
            y = [
                src[block, k, pl.ds(local, 1), :] - centres[kind, k, pl.ds(slot, 1), :]
                for k in range(3)
            ]
            f = [src[block, 3 + k, pl.ds(local, 1), :] for k in range(3)]
            return y, f, feats[target]

        found = sums_of_pairs(fetch, count)
        for target, value in zip(targets, found):
            sums[target] += value

    whole = lax.div(filled + 1, 4)

    def four(step, carry):
        some(step * 4, 4)
        return carry

    lax.fori_loop(0, whole, four, 0)

    @pl.when(whole * 4 < filled)
    def _():
        some(whole * 4, 2)


def pair_partner(index, shift, groups):
    if groups & (groups - 1) == 0:
        return index ^ shift
    return (index + shift) % groups


def slot_of(member, other, groups):
    if groups & (groups - 1) == 0:
        return member ^ other
    return lax.rem(member - other + groups, groups)


def list_own(groups, per_dev, neighbours, near, meta, lists):
    n_list = neighbours.shape[1]
    n_near = near.shape[0]
    segment = lax.axis_index("seg")
    member = lax.axis_index("cell")
    seg_cells = groups * per_dev
    start = (segment - 1) * seg_cells
    close_side = 2 - 2 * lax.rem(segment, 2)
    filled = [jnp.int32(0)] * 3
    for local in range(per_dev):
        alive = meta[0, local, 0] != 0.0
        for n in range(n_list + n_near):
            wall = n >= n_list
            relative = (near[n - n_list, local] if wall else neighbours[local, n]) - start
            side = lax.div(relative, seg_cells)
            inside = lax.rem(relative, seg_cells)
            turn = slot_of(member, lax.div(inside, per_dev), groups)
            middle = side == 1
            close = side == close_side
            early = jnp.logical_and(jnp.logical_and(middle, turn == 0), filled[0] < own_most)
            inner = jnp.logical_or(middle, close)
            where = (
                early,
                jnp.logical_and(inner, jnp.logical_not(early)),
                jnp.logical_not(inner),
            )
            blocks = (0, turn + jnp.where(middle, 0, groups), turn)
            for stage, count in enumerate((1, 2 * groups, groups)):
                block = blocks[stage] + (count if wall else 0)
                lists[stage][filled[stage]] = encode(local, block, lax.rem(inside, per_dev))
                here = jnp.logical_and(alive, where[stage])
                filled[stage] = filled[stage] + here.astype(jnp.int32)
    return filled


def list_patches(groups, per_dev, blocks, n_near, meta, pairs, filled):
    seg_cells = groups * per_dev
    first = lax.axis_index("seg") * seg_cells + lax.axis_index("cell") * per_dev + 1

    def scan(block, filled):
        for local in range(per_dev):
            for w in range(n_near):
                patch = meta[block, local, 1 + w].astype(jnp.int32) - first
                mine = jnp.logical_and(patch >= 0, patch < per_dev)
                pairs[filled] = encode(per_dev + patch, block, local)
                filled = filled + mine.astype(jnp.int32)
        return filled

    return lax.fori_loop(0, blocks, scan, filled)


def two_parts(value):
    high = value.astype(bf16)
    return high, (value - high.astype(f32)).astype(bf16)


def layer(density, operator):
    _, per_dev, points = density.shape
    rows = jnp.concatenate([density[k] for k in range(3)] + [jnp.zeros((per_dev, points), f32)], axis=0)
    high, low = two_parts(rows)
    operator_high, operator_low = two_parts(operator[...])
    turned = functools.partial(
        lax.dot_general, dimension_numbers=(((1,), (1,)), ((), ())), preferred_element_type=f32
    )
    count = rows.shape[0]
    main = turned(jnp.concatenate([high, low], axis=0), operator_high)
    total = main[:count] + main[count:] + turned(high, operator_low)
    return [total[k * per_dev : (k + 1) * per_dev] for k in range(3)]


def fill_forces(windows, stiffness, src):
    tiles = []
    for moving, fixed in windows:
        for block in range(moving.shape[0]):
            for k in range(3):
                tiles.append(moving[block, k] - fixed[block, 6 + k])
    per_dev, points = tiles[0].shape
    rows = len(tiles) * per_dev
    if rows % 16:
        tiles.append(jnp.zeros((16 - rows % 16, points), f32))
    offset = jnp.concatenate(tiles, axis=0).astype(bf16)
    pushed = lax.dot_general(
        offset, stiffness[...], (((1,), (1,)), ((), ())), preferred_element_type=f32
    )
    row = 0
    number = 0
    for moving, fixed in windows:
        for block in range(moving.shape[0]):
            scale = jnp.broadcast_to(fixed[block, 12][:, 0:1], (per_dev, points))
            for k in range(3):
                src[number, 3 + k] = scale * pushed[row : row + per_dev]
                row += per_dev
            number += 1


def pairs_kernel(stage, first, last, groups, per_dev, n_near, *refs):
    if first and stage == 0:
        (neighbours, near), refs = refs[:2], refs[2:]
    else:
        listed, refs = refs[0], refs[1:]
    (stiffness, own, own_s), refs = refs[:3], refs[3:]
    if stage == 0:
        windows = [(own, own_s)]
        (operator, out_tgt, feats, sums, out_layer), refs = refs[:5], refs[5:]
        centres = out_tgt.at[1]
        if first:
            held, lists, refs = refs[:2], refs[2:5], refs[5:]
    elif stage == 1:
        windows, (tgt, feats, sums_in, sums), refs = [refs[:2], refs[2:4]], refs[4:8], refs[8:]
        centres = tgt.at[1]
    else:
        windows, (tgt, feats, sums_in, layered), refs = [refs[:2]], refs[2:6], refs[6:]
        centres = tgt.at[1]
        outs, refs = refs[: 3 if last else 1], refs[3 if last else 1 :]
    if not first:
        pairs = listed
    elif stage == 0:
        pairs = lists[0]
    else:
        pairs, refs = refs[0], refs[1:]
    if first:
        meta, sems = refs[-2:]
    src = refs[0]
    if stage == 2:
        sums = refs[1]
    points = src.shape[-1]
    each = windows[0][0].shape[0]
    blocks = each * len(windows)
    dummy = 2 * blocks
    copies = []
    if first:
        for side, (moving, fixed) in enumerate(windows):
            cells = pl.ds(side * each, each)
            copies.append(pltpu.make_async_copy(
                fixed.at[:, 12, :, pl.ds(0, 128)], meta.at[cells], sems.at[side]))
    if first and stage == 0:
        loads = [
            pltpu.make_async_copy(array, copy, sems.at[1 + number])
            for number, (array, copy) in enumerate(zip((stiffness, operator), held))
        ]
        for load in loads:
            load.start()
    for copy in copies:
        copy.start()

    src[dummy] = jnp.zeros(src.shape[1:], f32)
    for side, (moving, fixed) in enumerate(windows):
        for block in range(each):
            number = side * each + block
            for k in range(3):
                src[number, k] = moving[block, k]
                src[blocks + number, k] = fixed[block, 9 + k]
                src[blocks + number, 3 + k] = moving[block, 3 + k]
    if stage:
        fill_forces(windows, stiffness, src)

    if stage == 0:
        for kind in range(2):
            for k in range(3):
                tile = (own[0, k], own_s[0, 9 + k])[kind]
                centre = jnp.mean(tile, axis=1, keepdims=True)
                out_tgt[1, kind, k] = jnp.broadcast_to(centre, tile.shape)
                out_tgt[0, kind, k] = tile - centre
        for kind in range(2):
            for local in range(per_dev):
                x = [out_tgt[0, kind, k, local : local + 1, :] for k in range(3)]
                feats[kind * per_dev + local] = target_features(x)
        sums[...] = jnp.zeros(sums.shape, f32)
    else:
        sums[...] = sums_in[...]
    for copy in copies:
        copy.wait()
    end = pairs.shape[0] - 1
    if not first:
        filled = pairs[end]
    elif stage == 0:
        counts = list_own(groups, per_dev, neighbours, near, meta, lists)
        for each_list, count in zip(lists, counts):
            each_list[end] = count
        filled = counts[0]
    else:

        def take(number, carry):
            pairs[number] = listed[number]
            return carry

        filled = listed[end]
        lax.fori_loop(0, filled, take, 0)
        filled = list_patches(groups, per_dev, blocks, n_near, meta, pairs, filled)
        pairs[end] = filled
    if stage == 0:
        if first:
            loads[0].wait()
            stiffness, operator = held
        fill_forces(windows, stiffness, src)
    pair_loop(filled, pairs, src, centres, feats, sums, per_dev, dummy)
    if stage == 0:
        if first:
            loads[1].wait()
        for k, tile in enumerate(layer(own[0, 3:6], operator)):
            out_layer[k] = tile
    if stage < 2:
        return

    for local in range(per_dev):
        slot = slice(local, local + 1)
        velocity = combine(sums[local], [tgt[0, 0, k, slot, :] for k in range(3)])
        wall_velocity = combine(sums[per_dev + local], [tgt[0, 1, k, slot, :] for k in range(3)])
        for k in range(3):
            position = own[0, k, slot, :] + time_step * velocity[k]
            density = own[0, 3 + k, slot, :]
            density = density - relax_factor * (
                wall_velocity[k] + 0.5 * density + layered[k, slot, :]
            )
            if last:
                outs[0][k, slot, :] = position
                outs[1][k, slot, :] = velocity[k]
                outs[2][k, slot, :] = density
            else:
                outs[0][k, slot, :] = position
                outs[0][3 + k, slot, :] = density


def cell_blocks(block):
    groups = lax.axis_size("cell")
    return [block] + [
        lax.ppermute(
            block, "cell", [(i, pair_partner(i, shift, groups)) for i in range(groups)]
        )
        for shift in range(1, groups)
    ]


def beside(window):
    count = lax.axis_size("seg")
    close = [(i, i ^ 1) for i in range(count) if i ^ 1 < count]
    other = [(i, i + 1 if i % 2 else i - 1) for i in range(count)]
    other = [(i, j) for i, j in other if 0 <= j < count]
    return lax.ppermute(window, "seg", close), lax.ppermute(window, "seg", other)


smem = pl.BlockSpec(memory_space=pltpu.SMEM)
vmem = pl.BlockSpec(memory_space=pltpu.VMEM)
anywhere = pl.BlockSpec(memory_space=pl.ANY)
hbm = pl.BlockSpec(memory_space=pltpu.HBM)


def in_hbm(array):
    return pltpu.with_memory_space_constraint(array, pltpu.HBM)


def pack(modulus, seg_count, near, arrays):
    _, per_dev, points = arrays[0].shape
    return pl.pallas_call(
        pack_kernel,
        out_shape=jax.ShapeDtypeStruct((13, per_dev, points), f32),
        in_specs=[anywhere] * 3 + [hbm] * 4,
        out_specs=vmem,
        scratch_shapes=[
            pltpu.SemaphoreType.DMA((7,)),
            pltpu.SMEM(modulus.shape, f32),
            pltpu.SMEM(seg_count.shape, jnp.int32),
            pltpu.SMEM(near.shape, jnp.int32),
        ],
        compiler_params=pltpu.CompilerParams(vmem_limit_bytes=4 * 1024 * 1024),
        name="pack",
    )(modulus, seg_count, near, *map(in_hbm, arrays))


def join(parts):
    return pl.pallas_call(
        join_kernel,
        out_shape=jax.ShapeDtypeStruct((len(parts), *parts[0].shape), f32),
        in_specs=[vmem] * len(parts),
        out_specs=vmem,
        compiler_params=pltpu.CompilerParams(vmem_limit_bytes=4 * 1024 * 1024),
        name="join",
    )(*parts)


def run_stage(stage, first, last, groups, per_dev, n_near, points, lists, entries, stiffness, own, arrays):
    blocks = (1, 2 * groups, groups)[stage]
    carried = [
        jax.ShapeDtypeStruct((2, 2, 3, per_dev, points), f32),
        jax.ShapeDtypeStruct((2 * per_dev, 48, points), bf16),
        jax.ShapeDtypeStruct((2 * per_dev, 24, points), f32),
    ]
    if stage == 0:
        shapes = carried + [jax.ShapeDtypeStruct((3, per_dev, points), f32)]
    elif stage == 1:
        shapes = carried[2:]
    elif last:
        shapes = [jax.ShapeDtypeStruct((3, per_dev, points), f32)] * 3
    else:
        shapes = [jax.ShapeDtypeStruct((6, per_dev, points), f32)]
    scratch = [pltpu.VMEM((2 * blocks + 1, 6, per_dev, points), f32)]
    if stage == 2:
        scratch.append(pltpu.VMEM(carried[2].shape, f32))
    out_specs = [vmem] * len(shapes)
    if first:
        count = 1 if stage else 3
        if stage == 0:
            shapes = shapes + [
                jax.ShapeDtypeStruct(array.shape, array.dtype) for array in (stiffness, arrays[0])
            ]
            out_specs = out_specs + [vmem] * 2
        shapes = shapes + [jax.ShapeDtypeStruct((entries + 4,), jnp.int32)] * count
        out_specs = out_specs + [smem] * count
        scratch += [
            pltpu.SMEM((blocks, per_dev, 128), f32),
            pltpu.SemaphoreType.DMA((3,)),
        ]
    load = first and stage == 0
    in_specs = [smem] * len(lists) + [hbm if load else vmem] + [vmem] * 2
    in_specs += [hbm if load else vmem] * len(arrays)
    if load:
        stiffness, arrays = in_hbm(stiffness), [in_hbm(array) for array in arrays]
    pair_count = (6, 2, 10)[stage]
    return pl.pallas_call(
        functools.partial(pairs_kernel, stage, first, last, groups, per_dev, n_near),
        out_shape=shapes,
        in_specs=in_specs,
        out_specs=out_specs,
        scratch_shapes=scratch,
        cost_estimate=pl.CostEstimate(
            flops=pair_count * 2 * points * points * 512, transcendentals=0,
            bytes_accessed=1 << 20,
        ),
        compiler_params=pltpu.CompilerParams(vmem_limit_bytes=16 * 1024 * 1024),
        name=("own_pairs", "segment_pairs", "outer_pairs")[stage],
    )(*lists, stiffness, *own, *arrays)


def body(
    positions, rest_shape, modulus, stiffness, wall_points, density,
    wall_operator, seg_count, neighbours, near_patches,
):
    per_dev, _, points = positions.shape
    groups = lax.axis_size("cell")
    near = near_patches.T
    turn = lambda array: jnp.transpose(array, (1, 0, 2))
    positions, rest_shape, wall_points, density = map(
        turn, (positions, rest_shape, wall_points, density)
    )

    fixed = pack(modulus, seg_count, near, (positions, rest_shape, wall_points, density))
    moving = fixed
    lists = [(neighbours, near)]
    n_near = near.shape[0]
    entries = neighbours.size + near.size + 3 * groups * near.size
    windows = ()
    for repeat in range(STEPS):
        first = repeat == 0
        last = repeat == STEPS - 1
        stage = functools.partial(
            run_stage, groups=groups, per_dev=per_dev, n_near=n_near, points=points, first=first,
            last=last, own=(moving[None], fixed[None]), entries=entries,
        )
        parts = cell_blocks(moving)
        tgt, feats, sums, layered, *more = stage(
            0, lists=lists[0], stiffness=stiffness, arrays=(wall_operator,)
        )
        if first:
            stiffness, wall_operator, *listed = more
            lists = [listed[:1], listed[1:2], listed[2:]]
        parts, sums = lax.optimization_barrier((parts, sums))
        window = join(parts)
        close, other = beside(window)
        if first:
            windows = (window, close, other)
        sums, *listed = stage(
            1, lists=lists[1], stiffness=stiffness,
            arrays=(window, windows[0], close, windows[1], tgt, feats, sums),
        )
        outs = stage(
            2, lists=lists[2], stiffness=stiffness,
            arrays=(other, windows[2], tgt, feats, sums, layered),
        )
        if first:
            lists = [lists[0], listed, outs[1:]]
        moving = outs[0]
    return tuple(map(turn, outs))


def solution(mesh):
    both = P(("seg", "cell"), None, None)
    placed = (
        both, both, P(("seg", "cell")), P(), both, both, P(), P("seg"),
        P(("seg", "cell"), None), P(("seg", "cell"), None),
    )
    return jax.shard_map(
        body, mesh=mesh, in_specs=placed, out_specs=(both, both, both), check_vma=False
    )
```

```python
import functools

import jax
import jax.numpy as jnp
from jax import lax
from jax.experimental import pallas as pl
from jax.experimental.pallas import tpu as pltpu
from jax.sharding import PartitionSpec as P

soften_square = 0.25
stokes_factor = 0.039788735772973836
relax_factor = 0.5
time_step = 0.5
own_most = 8
bf16 = jnp.bfloat16
f32 = jnp.float32
STEPS = 2


def row_places(points):
    return lax.broadcasted_iota(jnp.int32, (8, points), 0)


def tall(row):
    return jnp.broadcast_to(row, (8, row.shape[1]))


def parts_of(value):
    first = value.astype(bf16).astype(f32)
    rest = value - first
    second = rest.astype(bf16).astype(f32)
    third = (rest - second).astype(bf16).astype(f32)
    return first, second, third


def two_parts(value):
    high = value.astype(bf16)
    return high, (value - high.astype(f32)).astype(bf16)


def target_features(x):
    points = x[0].shape[1]
    place = row_places(points)
    square = x[0] * x[0] + x[1] * x[1] + x[2] * x[2]
    rows = jnp.where(place == 3, 1.0, 0.0)
    for number, row in ((0, x[0]), (1, x[1]), (2, x[2]), (4, square)):
        rows = jnp.where(place == number, tall(row), rows)
    high, middle, low = parts_of(rows)
    return jnp.concatenate([high, middle, high, low, high, middle], axis=0).astype(bf16)


def source_rows(y, f):
    place = row_places(y[0].shape[1])
    low_half = place < 4
    lane = place & 3
    square = tall(y[0] * y[0] + y[1] * y[1] + y[2] * y[2])
    along = tall(-(y[0] * f[0] + y[1] * f[1] + y[2] * f[2]))
    y = [tall(row) for row in y]
    f = [tall(row) for row in f]
    points_one = jnp.where(lane == 0, y[0], jnp.where(lane == 1, y[1], jnp.where(lane == 2, y[2], 1.0)))
    source = jnp.where(
        place < 3, -2 * points_one,
        jnp.where(place == 3, square + soften_square, jnp.where(place == 4, 1.0, 0.0)),
    )
    high, middle, low = parts_of(source)
    wide = jnp.concatenate([high, high, middle, high, low, middle], axis=0).astype(bf16)
    one = jnp.where(low_half, f[0], f[1]) * points_one
    two = jnp.where(low_half, f[2], along) * points_one
    three = jnp.where(lane == 0, f[0], jnp.where(lane == 1, f[1], f[2])) * square
    moments = jnp.concatenate(two_parts(jnp.concatenate([one, two, three], axis=0)), axis=0)
    return wide.T, moments


def sums_of_pairs(fetch, count):
    held = []

    def distance(unit):
        pair, half = divmod(unit, 2)
        if half == 0:
            y, f, features = fetch(pair)
            held.append((*source_rows(y, f), features))
        wide, _, features = held[pair]
        rows = wide.shape[0] // 2
        return jnp.dot(wide[half * rows : (half + 1) * rows], features, preferred_element_type=f32)

    def moment_sums(unit, distance):
        pair, half = divmod(unit, 2)
        inverse = lax.rsqrt(distance)
        cubed = (inverse * inverse * inverse).astype(bf16)
        moments = held[pair][1]
        rows = moments.shape[1] // 2
        return jnp.dot(
            moments[:, half * rows : (half + 1) * rows], cubed, preferred_element_type=f32
        )

    ready = [distance(0), distance(1)]
    out = []
    for unit in range(2 * count):
        if unit + 2 < 2 * count:
            ready.append(distance(unit + 2))
        sums = moment_sums(unit, ready[unit])
        if unit % 2 == 0:
            first = sums
        else:
            sums = first + sums
            out.append(sums[0:24] + sums[24:48])
    return out


def combine(sums, x):
    cross = [[sums[4 * m + k : 4 * m + k + 1] for k in range(3)] for m in range(3)]
    total = [sums[4 * m + 3 : 4 * m + 4] for m in range(3)]
    square = x[0] * x[0] + x[1] * x[1] + x[2] * x[2] + soften_square
    weight = x[0] * total[0] + x[1] * total[1] + x[2] * total[2] + sums[15:16]
    out = []
    for k in range(3):
        moment = x[0] * cross[0][k] + x[1] * cross[1][k] + x[2] * cross[2][k] + sums[12 + k : 13 + k]
        turned = x[0] * cross[k][0] + x[1] * cross[k][1] + x[2] * cross[k][2]
        direct = square * total[k] + sums[16 + k : 17 + k] - 2 * turned
        out.append(stokes_factor * (direct + x[k] * weight - moment))
    return out


def pack_kernel(*refs):
    modulus, count, near, positions, rest_shape, wall_points, density, out, sems = refs[:9]
    held = refs[9:]
    per_dev = positions.shape[1]
    copies = [
        pltpu.make_async_copy(array, target, sems.at[number])
        for number, (array, target) in enumerate(zip((modulus, count, near), held))
    ]
    for number, array in enumerate((positions, density, rest_shape, wall_points)):
        copies.append(pltpu.make_async_copy(array, out.at[pl.ds(3 * number, 3)], sems.at[3 + number]))
    for copy in copies:
        copy.start()
    for copy in copies:
        copy.wait()
    modulus, count, near = held
    shape = out.shape[1:]
    row = lax.broadcasted_iota(jnp.int32, shape, 0)
    lane = lax.broadcasted_iota(jnp.int32, shape, 1)
    table = jnp.zeros(shape, f32)
    first = lax.axis_index("cell") * per_dev
    for local in range(per_dev):
        alive = first + local < count[0]
        entries = [jnp.where(alive, modulus[local], 0.0)]
        entries += [jnp.where(alive, near[w, local] + 1, 0).astype(f32) for w in range(near.shape[0])]
        for number, entry in enumerate(entries):
            table = jnp.where(jnp.logical_and(row == local, lane == number), entry, table)
    out[12] = table


def join_kernel(count, *refs):
    parts, outs = refs[:count], refs[count:]
    for number, part in enumerate(parts):
        outs[0][number] = part[...]
        if len(outs) > 1 and number:
            outs[1][number - 1] = part[...]


def encode(target, block, local):
    return (target * 256 + block) * 16 + local


def pair_loop(filled, pairs, src, centres, feats, sums, per_dev):
    def some(first, count):
        targets = []

        def fetch(part):
            code = pairs[first + part]
            local = code & 15
            block = (code >> 4) & 255
            target = code >> 12
            targets.append(target)
            kind = lax.div(target, per_dev)
            slot = lax.rem(target, per_dev)
            y = [
                src[block, k, pl.ds(local, 1), :] - centres[kind, k, pl.ds(slot, 1), :]
                for k in range(3)
            ]
            f = [src[block, 3 + k, pl.ds(local, 1), :] for k in range(3)]
            return y, f, feats[target]

        found = sums_of_pairs(fetch, count)
        for target, value in zip(targets, found):
            sums[target] += value

    done = 0
    for count in (8, 4):
        steps = lax.div(filled - done + (1 if count == 4 else 0), count)

        def whole(step, carry, count=count, done=done):
            some(done + step * count, count)
            return carry

        lax.fori_loop(0, steps, whole, 0)
        done = done + steps * count

    @pl.when(done < filled)
    def _():
        some(done, 2)


def pair_partner(index, shift, groups):
    if groups & (groups - 1) == 0:
        return index ^ shift
    return (index + shift) % groups


def slot_of(member, other, groups):
    if groups & (groups - 1) == 0:
        return member ^ other
    return lax.rem(member - other + groups, groups)


def list_own(groups, per_dev, neighbours, near, meta, lists):
    n_list = neighbours.shape[1]
    n_near = near.shape[0]
    segment = lax.axis_index("seg")
    member = lax.axis_index("cell")
    seg_cells = groups * per_dev
    start = (segment - 1) * seg_cells
    close_side = 2 - 2 * lax.rem(segment, 2)
    filled = [jnp.int32(0)] * 3
    for local in range(per_dev):
        alive = meta[0, local, 0] != 0.0
        for n in range(n_list + n_near):
            wall = n >= n_list
            relative = (near[n - n_list, local] if wall else neighbours[local, n]) - start
            side = lax.div(relative, seg_cells)
            inside = lax.rem(relative, seg_cells)
            turn = slot_of(member, lax.div(inside, per_dev), groups)
            middle = side == 1
            close = side == close_side
            early = jnp.logical_and(jnp.logical_and(middle, turn == 0), filled[0] < own_most)
            inner = jnp.logical_or(middle, close)
            where = (
                early,
                jnp.logical_and(inner, jnp.logical_not(early)),
                jnp.logical_not(inner),
            )
            blocks = (0, turn + jnp.where(middle, 0, groups), turn)
            for stage, count in enumerate((1, 2 * groups, groups)):
                block = blocks[stage] + (count if wall else 0)
                lists[stage][filled[stage]] = encode(local, block, lax.rem(inside, per_dev))
                here = jnp.logical_and(alive, where[stage])
                filled[stage] = filled[stage] + here.astype(jnp.int32)
    return filled


def list_patches(groups, per_dev, blocks, n_near, meta, pairs, filled):
    seg_cells = groups * per_dev
    first = lax.axis_index("seg") * seg_cells + lax.axis_index("cell") * per_dev + 1

    def scan(block, filled):
        for local in range(per_dev):
            for w in range(n_near):
                patch = meta[block, local, 1 + w].astype(jnp.int32) - first
                mine = jnp.logical_and(patch >= 0, patch < per_dev)
                pairs[filled] = encode(per_dev + patch, block, local)
                filled = filled + mine.astype(jnp.int32)
        return filled

    return lax.fori_loop(0, blocks, scan, filled)


def layer(density, operator):
    _, per_dev, points = density.shape
    rows = jnp.concatenate([density[k] for k in range(3)] + [jnp.zeros((per_dev, points), f32)], axis=0)
    high, low = two_parts(rows)
    operator_high, operator_low = two_parts(operator[...])
    turned = functools.partial(
        lax.dot_general, dimension_numbers=(((1,), (1,)), ((), ())), preferred_element_type=f32
    )
    count = rows.shape[0]
    main = turned(jnp.concatenate([high, low], axis=0), operator_high)
    total = main[:count] + main[count:] + turned(high, operator_low)
    return [total[k * per_dev : (k + 1) * per_dev] for k in range(3)]


def fill_forces(held, stiffness, src):
    tiles = []
    for moving, at, fixed, fixed_at in held:
        for k in range(3):
            tiles.append(moving[at, k] - fixed[fixed_at, 6 + k])
    per_dev, points = tiles[0].shape
    rows = len(tiles) * per_dev
    if rows % 16:
        tiles.append(jnp.zeros((16 - rows % 16, points), f32))
    offset = jnp.concatenate(tiles, axis=0).astype(bf16)
    pushed = lax.dot_general(
        offset, stiffness[...], (((1,), (1,)), ((), ())), preferred_element_type=f32
    )
    row = 0
    for number, (_, _, fixed, fixed_at) in enumerate(held):
        scale = jnp.broadcast_to(fixed[fixed_at, 12][:, 0:1], (per_dev, points))
        for k in range(3):
            src[number, 3 + k] = scale * pushed[row : row + per_dev]
            row += per_dev


def pairs_kernel(stage, first, last, groups, per_dev, n_near, *refs):
    if first and stage == 0:
        (neighbours, near), refs = refs[:2], refs[2:]
    else:
        listed, refs = refs[0], refs[1:]
    (stiffness, own, own_s), refs = refs[:3], refs[3:]
    if stage == 0:
        moving, fixed = [own], [own_s]
        (operator, out_tgt, feats, sums, out_layer), refs = refs[:5], refs[5:]
        centres = out_tgt.at[1]
        if first:
            loaded, lists, refs = refs[:2], refs[2:5], refs[5:]
    elif stage == 1:
        moving, fixed, refs = refs[:2], refs[2:4], refs[4:]
        (tgt, feats, sums_in, sums), refs = refs[:4], refs[4:]
        centres = tgt.at[1]
    else:
        count = 2 if first else 1
        moving, fixed, refs = refs[:count], refs[count : count + 2], refs[count + 2 :]
        (tgt, feats, sums_in, layered), refs = refs[:4], refs[4:]
        centres = tgt.at[1]
        outs, refs = refs[: 3 if last else 1], refs[3 if last else 1 :]
    if not first:
        pairs = listed
    elif stage == 0:
        pairs = lists[0]
    else:
        pairs, refs = refs[0], refs[1:]
    if first:
        meta, sems = refs[-2:]
    src = refs[0]
    if stage == 2:
        sums = refs[1]
    points = src.shape[-1]
    held = [
        (*pair, *fixed_pair)
        for pair, fixed_pair in zip(
            [(ref, at) for ref in moving for at in range(ref.shape[0])],
            [(ref, at) for ref in fixed for at in range(ref.shape[0])],
        )
    ]
    blocks = len(held)
    dummy = 2 * blocks
    copies = []
    if first:
        start = 0
        for number, ref in enumerate(fixed):
            cells = pl.ds(start, ref.shape[0])
            copies.append(pltpu.make_async_copy(
                ref.at[:, 12, :, pl.ds(0, 128)], meta.at[cells], sems.at[number]))
            start += ref.shape[0]
    if first and stage == 0:
        loads = [
            pltpu.make_async_copy(array, copy, sems.at[1 + number])
            for number, (array, copy) in enumerate(zip((stiffness, operator), loaded))
        ]
        for load in loads:
            load.start()
    for copy in copies:
        copy.start()

    src[dummy] = jnp.zeros(src.shape[1:], f32)
    for number, (ref, at, fixed_ref, fixed_at) in enumerate(held):
        for k in range(3):
            src[number, k] = ref[at, k]
            src[blocks + number, k] = fixed_ref[fixed_at, 9 + k]
            src[blocks + number, 3 + k] = ref[at, 3 + k]
    if stage:
        fill_forces(held, stiffness, src)

    if stage == 0:
        for kind in range(2):
            for k in range(3):
                tile = (own[0, k], own_s[0, 9 + k])[kind]
                centre = jnp.mean(tile, axis=1, keepdims=True)
                out_tgt[1, kind, k] = jnp.broadcast_to(centre, tile.shape)
                out_tgt[0, kind, k] = tile - centre
        for kind in range(2):
            for local in range(per_dev):
                x = [out_tgt[0, kind, k, local : local + 1, :] for k in range(3)]
                feats[kind * per_dev + local] = target_features(x)
        sums[...] = jnp.zeros(sums.shape, f32)
    else:
        sums[...] = sums_in[...]
    for copy in copies:
        copy.wait()
    end = pairs.shape[0] - 1
    if not first:
        filled = pairs[end]
    elif stage == 0:
        counts = list_own(groups, per_dev, neighbours, near, meta, lists)
        for each_list, count in zip(lists, counts):
            each_list[end] = count
        filled = counts[0]
    else:

        def take(number, carry):
            pairs[number] = listed[number]
            return carry

        filled = listed[end]
        lax.fori_loop(0, filled, take, 0)
        filled = list_patches(groups, per_dev, blocks, n_near, meta, pairs, filled)
        pairs[end] = filled
    if stage == 0:
        if first:
            loads[0].wait()
            stiffness, operator = loaded
        fill_forces(held, stiffness, src)
    if first:
        for extra in range(2):
            pairs[filled + extra] = encode(0, dummy, 0)
    pair_loop(filled, pairs, src, centres, feats, sums, per_dev)
    if stage == 0:
        if first:
            loads[1].wait()
        for k, tile in enumerate(layer(own[0, 3:6], operator)):
            out_layer[k] = tile
    if stage < 2:
        return

    for local in range(per_dev):
        slot = slice(local, local + 1)
        velocity = combine(sums[local], [tgt[0, 0, k, slot, :] for k in range(3)])
        wall_velocity = combine(sums[per_dev + local], [tgt[0, 1, k, slot, :] for k in range(3)])
        for k in range(3):
            position = own[0, k, slot, :] + time_step * velocity[k]
            density = own[0, 3 + k, slot, :]
            density = density - relax_factor * (
                wall_velocity[k] + 0.5 * density + layered[k, slot, :]
            )
            if last:
                outs[0][k, slot, :] = position
                outs[1][k, slot, :] = velocity[k]
                outs[2][k, slot, :] = density
            else:
                outs[0][k, slot, :] = position
                outs[0][3 + k, slot, :] = density


def cell_blocks(block):
    groups = lax.axis_size("cell")
    return [block] + [
        lax.ppermute(
            block, "cell", [(i, pair_partner(i, shift, groups)) for i in range(groups)]
        )
        for shift in range(1, groups)
    ]


def paired(count):
    return [(i, i ^ 1) for i in range(count) if i ^ 1 < count]


def paired_next(count):
    pairs = [(i, i + 1 if i % 2 else i - 1) for i in range(count)]
    return [(i, j) for i, j in pairs if 0 <= j < count]


smem = pl.BlockSpec(memory_space=pltpu.SMEM)
vmem = pl.BlockSpec(memory_space=pltpu.VMEM)
anywhere = pl.BlockSpec(memory_space=pl.ANY)
hbm = pl.BlockSpec(memory_space=pltpu.HBM)


def in_hbm(array):
    return pltpu.with_memory_space_constraint(array, pltpu.HBM)


def pack(modulus, seg_count, near, arrays):
    _, per_dev, points = arrays[0].shape
    return pl.pallas_call(
        pack_kernel,
        out_shape=jax.ShapeDtypeStruct((13, per_dev, points), f32),
        in_specs=[anywhere] * 3 + [hbm] * 4,
        out_specs=vmem,
        scratch_shapes=[
            pltpu.SemaphoreType.DMA((7,)),
            pltpu.SMEM(modulus.shape, f32),
            pltpu.SMEM(seg_count.shape, jnp.int32),
            pltpu.SMEM(near.shape, jnp.int32),
        ],
        compiler_params=pltpu.CompilerParams(vmem_limit_bytes=4 * 1024 * 1024),
        name="pack",
    )(in_hbm(modulus), seg_count, in_hbm(near), *map(in_hbm, arrays))


def join(parts, twice):
    shapes = [
        jax.ShapeDtypeStruct((len(parts) - less, *parts[0].shape), f32) for less in range(2 if twice else 1)
    ]
    return pl.pallas_call(
        functools.partial(join_kernel, len(parts)),
        out_shape=shapes,
        in_specs=[vmem] * len(parts),
        out_specs=[vmem] * len(shapes),
        compiler_params=pltpu.CompilerParams(vmem_limit_bytes=4 * 1024 * 1024),
        name="join",
    )(*parts)


def run_stage(stage, first, last, groups, per_dev, n_near, points, lists, entries, stiffness, own, arrays):
    blocks = (1, 2 * groups, groups)[stage]
    carried = [
        jax.ShapeDtypeStruct((2, 2, 3, per_dev, points), f32),
        jax.ShapeDtypeStruct((2 * per_dev, 48, points), bf16),
        jax.ShapeDtypeStruct((2 * per_dev, 24, points), f32),
    ]
    if stage == 0:
        shapes = carried + [jax.ShapeDtypeStruct((3, per_dev, points), f32)]
    elif stage == 1:
        shapes = carried[2:]
    elif last:
        shapes = [jax.ShapeDtypeStruct((3, per_dev, points), f32)] * 3
    else:
        shapes = [jax.ShapeDtypeStruct((6, per_dev, points), f32)]
    scratch = [pltpu.VMEM((2 * blocks + 1, 6, per_dev, points), f32)]
    if stage == 2:
        scratch.append(pltpu.VMEM(carried[2].shape, f32))
    out_specs = [vmem] * len(shapes)
    if first:
        count = 1 if stage else 3
        if stage == 0:
            shapes = shapes + [
                jax.ShapeDtypeStruct(array.shape, array.dtype) for array in (stiffness, arrays[0])
            ]
            out_specs = out_specs + [vmem] * 2
        shapes = shapes + [jax.ShapeDtypeStruct((entries + 4,), jnp.int32)] * count
        out_specs = out_specs + [smem] * count
        scratch += [
            pltpu.SMEM((blocks, per_dev, 128), f32),
            pltpu.SemaphoreType.DMA((3,)),
        ]
    load = first and stage == 0
    in_specs = [smem] * len(lists) + [hbm if load else vmem] + [vmem] * 2
    in_specs += [hbm if load else vmem] * len(arrays)
    if load:
        stiffness, arrays = in_hbm(stiffness), [in_hbm(array) for array in arrays]
    pair_count = (6, 2, 10)[stage]
    return pl.pallas_call(
        functools.partial(pairs_kernel, stage, first, last, groups, per_dev, n_near),
        out_shape=shapes,
        in_specs=in_specs,
        out_specs=out_specs,
        scratch_shapes=scratch,
        cost_estimate=pl.CostEstimate(
            flops=pair_count * 2 * points * points * 512, transcendentals=0,
            bytes_accessed=1 << 20,
        ),
        compiler_params=pltpu.CompilerParams(vmem_limit_bytes=16 * 1024 * 1024),
        name=("own_pairs", "segment_pairs", "outer_pairs")[stage],
    )(*lists, stiffness, *own, *arrays)


def body(
    positions, rest_shape, modulus, stiffness, wall_points, density,
    wall_operator, seg_count, neighbours, near_patches,
):
    per_dev, _, points = positions.shape
    groups = lax.axis_size("cell")
    near = near_patches.T
    turn = lambda array: jnp.transpose(array, (1, 0, 2))
    positions, rest_shape, wall_points, density = map(
        turn, (positions, rest_shape, wall_points, density)
    )

    fixed = pack(modulus, seg_count, near, (positions, rest_shape, wall_points, density))
    moving = fixed
    lists = [(neighbours, near)]
    n_near = near.shape[0]
    entries = neighbours.size + near.size + 3 * groups * near.size
    segments = lax.axis_size("seg")
    for repeat in range(STEPS):
        first = repeat == 0
        last = repeat == STEPS - 1
        stage = functools.partial(
            run_stage, groups=groups, per_dev=per_dev, n_near=n_near, points=points, first=first,
            last=last, own=(moving[None], fixed[None]), entries=entries,
        )
        parts = cell_blocks(moving)
        if first:
            far = lax.ppermute(moving, "seg", paired_next(segments))
            parts.append(far)
        tgt, feats, sums, layered, *more = stage(
            0, lists=lists[0], stiffness=stiffness, arrays=(wall_operator,)
        )
        if first:
            stiffness, wall_operator, *listed = more
            lists = [listed[:1], listed[1:2], listed[2:]]
        parts, sums = lax.optimization_barrier((parts, sums))
        if first:
            far = parts.pop()
        window, *rest = join(parts, first)
        close = lax.ppermute(window, "seg", paired(segments))
        far_rest = lax.ppermute(rest[0] if first else window, "seg", paired_next(segments))
        if first:
            fixed_near, fixed_far = (window, close), (far[None], far_rest)
            moving_far = fixed_far
        else:
            moving_far = (far_rest,)
        sums, *listed = stage(
            1, lists=lists[1], stiffness=stiffness,
            arrays=(window, close, *fixed_near, tgt, feats, sums),
        )
        outs = stage(
            2, lists=lists[2], stiffness=stiffness,
            arrays=(*moving_far, *fixed_far, tgt, feats, sums, layered),
        )
        if first:
            lists = [lists[0], listed, outs[1:]]
        moving = outs[0]
    return tuple(map(turn, outs))


def solution(mesh):
    both = P(("seg", "cell"), None, None)
    placed = (
        both, both, P(("seg", "cell")), P(), both, both, P(), P("seg"),
        P(("seg", "cell"), None), P(("seg", "cell"), None),
    )
    return jax.shard_map(
        body, mesh=mesh, in_specs=placed, out_specs=(both, both, both), check_vma=False
    )
```

```python
import functools

import jax
import jax.numpy as jnp
from jax import lax
from jax.experimental import pallas as pl
from jax.experimental.pallas import tpu as pltpu
from jax.sharding import PartitionSpec as P

soften_square = 0.25
stokes_factor = 0.039788735772973836
relax_factor = 0.5
time_step = 0.5
own_most = 4
bf16 = jnp.bfloat16
f32 = jnp.float32
STEPS = 2


def row_places(points):
    return lax.broadcasted_iota(jnp.int32, (8, points), 0)


def tall(row):
    return jnp.broadcast_to(row, (8, row.shape[1]))


def parts_of(value):
    first = value.astype(bf16).astype(f32)
    rest = value - first
    second = rest.astype(bf16).astype(f32)
    third = (rest - second).astype(bf16).astype(f32)
    return first, second, third


def two_parts(value):
    high = value.astype(bf16)
    return high, (value - high.astype(f32)).astype(bf16)


def target_features(x):
    points = x[0].shape[1]
    place = row_places(points)
    square = x[0] * x[0] + x[1] * x[1] + x[2] * x[2]
    rows = jnp.where(place == 3, 1.0, 0.0)
    for number, row in ((0, x[0]), (1, x[1]), (2, x[2]), (4, square)):
        rows = jnp.where(place == number, tall(row), rows)
    high, middle, low = parts_of(rows)
    return jnp.concatenate([high, middle, high, low, high, middle], axis=0).astype(bf16)


def source_rows(y, f):
    place = row_places(y[0].shape[1])
    low_half = place < 4
    lane = place & 3
    square = tall(y[0] * y[0] + y[1] * y[1] + y[2] * y[2])
    along = tall(-(y[0] * f[0] + y[1] * f[1] + y[2] * f[2]))
    y = [tall(row) for row in y]
    f = [tall(row) for row in f]
    points_one = jnp.where(lane == 0, y[0], jnp.where(lane == 1, y[1], jnp.where(lane == 2, y[2], 1.0)))
    source = jnp.where(
        place < 3, -2 * points_one,
        jnp.where(place == 3, square + soften_square, jnp.where(place == 4, 1.0, 0.0)),
    )
    high, middle, low = parts_of(source)
    wide = jnp.concatenate([high, high, middle, high, low, middle], axis=0).astype(bf16)
    one = jnp.where(low_half, f[0], f[1]) * points_one
    two = jnp.where(low_half, f[2], along) * points_one
    three = jnp.where(lane == 0, f[0], jnp.where(lane == 1, f[1], f[2])) * square
    moments = jnp.concatenate(two_parts(jnp.concatenate([one, two, three], axis=0)), axis=0)
    return wide.T, moments


def sums_of_pairs(fetch, count):
    held = []

    def distance(unit):
        pair, half = divmod(unit, 2)
        if half == 0:
            y, f, features = fetch(pair)
            held.append((*source_rows(y, f), features))
        wide, _, features = held[pair]
        rows = wide.shape[0] // 2
        return jnp.dot(wide[half * rows : (half + 1) * rows], features, preferred_element_type=f32)

    def moment_sums(unit, distance):
        pair, half = divmod(unit, 2)
        inverse = lax.rsqrt(distance)
        cubed = (inverse * inverse * inverse).astype(bf16)
        moments = held[pair][1]
        rows = moments.shape[1] // 2
        return jnp.dot(
            moments[:, half * rows : (half + 1) * rows], cubed, preferred_element_type=f32
        )

    ready = [distance(0), distance(1)]
    out = []
    for unit in range(2 * count):
        if unit + 2 < 2 * count:
            ready.append(distance(unit + 2))
        sums = moment_sums(unit, ready[unit])
        if unit % 2 == 0:
            first = sums
        else:
            sums = first + sums
            out.append(sums[0:24] + sums[24:48])
    return out


def combine(sums, x):
    cross = [[sums[4 * m + k : 4 * m + k + 1] for k in range(3)] for m in range(3)]
    total = [sums[4 * m + 3 : 4 * m + 4] for m in range(3)]
    square = x[0] * x[0] + x[1] * x[1] + x[2] * x[2] + soften_square
    weight = x[0] * total[0] + x[1] * total[1] + x[2] * total[2] + sums[15:16]
    out = []
    for k in range(3):
        moment = x[0] * cross[0][k] + x[1] * cross[1][k] + x[2] * cross[2][k] + sums[12 + k : 13 + k]
        turned = x[0] * cross[k][0] + x[1] * cross[k][1] + x[2] * cross[k][2]
        direct = square * total[k] + sums[16 + k : 17 + k] - 2 * turned
        out.append(stokes_factor * (direct + x[k] * weight - moment))
    return out


def pack_kernel(*refs):
    modulus, count, near, positions, rest_shape, wall_points, density, out, sems = refs[:9]
    held = refs[9:]
    per_dev = positions.shape[1]
    copies = [
        pltpu.make_async_copy(array, target, sems.at[number])
        for number, (array, target) in enumerate(zip((modulus, count, near), held))
    ]
    for number, array in enumerate((positions, density, rest_shape, wall_points)):
        copies.append(pltpu.make_async_copy(array, out.at[pl.ds(3 * number, 3)], sems.at[3 + number]))
    for copy in copies:
        copy.start()
    for copy in copies:
        copy.wait()
    modulus, count, near = held
    shape = out.shape[1:]
    row = lax.broadcasted_iota(jnp.int32, shape, 0)
    lane = lax.broadcasted_iota(jnp.int32, shape, 1)
    table = jnp.zeros(shape, f32)
    first = lax.axis_index("cell") * per_dev
    for local in range(per_dev):
        alive = first + local < count[0]
        entries = [jnp.where(alive, modulus[local], 0.0)]
        entries += [jnp.where(alive, near[w, local] + 1, 0).astype(f32) for w in range(near.shape[0])]
        for number, entry in enumerate(entries):
            table = jnp.where(jnp.logical_and(row == local, lane == number), entry, table)
    out[12] = table


def join_kernel(count, *refs):
    parts, outs = refs[:count], refs[count:]
    for number, part in enumerate(parts):
        outs[0][number] = part[...]
        if len(outs) > 1 and number:
            outs[1][number - 1] = part[...]


def encode(target, block, local):
    return (target * 256 + block) * 16 + local


def pair_loop(filled, pairs, src, centres, feats, sums, per_dev):
    def some(first, count):
        targets = []

        def fetch(part):
            code = pairs[first + part]
            local = code & 15
            block = (code >> 4) & 255
            target = code >> 12
            targets.append(target)
            kind = lax.div(target, per_dev)
            slot = lax.rem(target, per_dev)
            y = [
                src[block, k, pl.ds(local, 1), :] - centres[kind, k, pl.ds(slot, 1), :]
                for k in range(3)
            ]
            f = [src[block, 3 + k, pl.ds(local, 1), :] for k in range(3)]
            return y, f, feats[target]

        found = sums_of_pairs(fetch, count)
        for target, value in zip(targets, found):
            sums[target] += value

    done = 0
    for count in (8, 4):
        steps = lax.div(filled - done + (1 if count == 4 else 0), count)

        def whole(step, carry, count=count, done=done):
            some(done + step * count, count)
            return carry

        lax.fori_loop(0, steps, whole, 0)
        done = done + steps * count

    @pl.when(done < filled)
    def _():
        some(done, 2)


def pair_partner(index, shift, groups):
    if groups & (groups - 1) == 0:
        return index ^ shift
    return (index + shift) % groups


def slot_of(member, other, groups):
    if groups & (groups - 1) == 0:
        return member ^ other
    return lax.rem(member - other + groups, groups)


def list_own(groups, per_dev, neighbours, near, meta, lists):
    n_list = neighbours.shape[1]
    n_near = near.shape[0]
    segment = lax.axis_index("seg")
    member = lax.axis_index("cell")
    seg_cells = groups * per_dev
    start = (segment - 1) * seg_cells
    close_side = 2 - 2 * lax.rem(segment, 2)
    filled = [jnp.int32(0)] * 3
    for local in range(per_dev):
        alive = meta[0, local, 0] != 0.0
        for n in range(n_list + n_near):
            wall = n >= n_list
            relative = (near[n - n_list, local] if wall else neighbours[local, n]) - start
            side = lax.div(relative, seg_cells)
            inside = lax.rem(relative, seg_cells)
            turn = slot_of(member, lax.div(inside, per_dev), groups)
            middle = side == 1
            close = side == close_side
            early = jnp.logical_and(jnp.logical_and(middle, turn == 0), filled[0] < own_most)
            inner = jnp.logical_or(middle, close)
            where = (
                early,
                jnp.logical_and(inner, jnp.logical_not(early)),
                jnp.logical_not(inner),
            )
            blocks = (0, turn + jnp.where(middle, 0, groups), turn)
            for stage, count in enumerate((1, 2 * groups, groups)):
                block = blocks[stage] + (count if wall else 0)
                lists[stage][filled[stage]] = encode(local, block, lax.rem(inside, per_dev))
                here = jnp.logical_and(alive, where[stage])
                filled[stage] = filled[stage] + here.astype(jnp.int32)
    return filled


def list_patches(groups, per_dev, blocks, n_near, meta, pairs, filled):
    seg_cells = groups * per_dev
    first = lax.axis_index("seg") * seg_cells + lax.axis_index("cell") * per_dev + 1

    def scan(block, filled):
        for local in range(per_dev):
            for w in range(n_near):
                patch = meta[block, local, 1 + w].astype(jnp.int32) - first
                mine = jnp.logical_and(patch >= 0, patch < per_dev)
                pairs[filled] = encode(per_dev + patch, block, local)
                filled = filled + mine.astype(jnp.int32)
        return filled

    return lax.fori_loop(0, blocks, scan, filled)


def layer(density, operator):
    _, per_dev, points = density.shape
    rows = jnp.concatenate([density[k] for k in range(3)] + [jnp.zeros((per_dev, points), f32)], axis=0)
    high, low = two_parts(rows)
    operator_high, operator_low = two_parts(operator[...])
    turned = functools.partial(
        lax.dot_general, dimension_numbers=(((1,), (1,)), ((), ())), preferred_element_type=f32
    )
    count = rows.shape[0]
    main = turned(jnp.concatenate([high, low], axis=0), operator_high)
    total = main[:count] + main[count:] + turned(high, operator_low)
    return [total[k * per_dev : (k + 1) * per_dev] for k in range(3)]


def fill_forces(held, stiffness, src):
    tiles = []
    for moving, at, fixed, fixed_at in held:
        for k in range(3):
            tiles.append(moving[at, k] - fixed[fixed_at, 6 + k])
    per_dev, points = tiles[0].shape
    rows = len(tiles) * per_dev
    if rows % 16:
        tiles.append(jnp.zeros((16 - rows % 16, points), f32))
    offset = jnp.concatenate(tiles, axis=0).astype(bf16)
    pushed = lax.dot_general(
        offset, stiffness[...], (((1,), (1,)), ((), ())), preferred_element_type=f32
    )
    row = 0
    for number, (_, _, fixed, fixed_at) in enumerate(held):
        scale = jnp.broadcast_to(fixed[fixed_at, 12][:, 0:1], (per_dev, points))
        for k in range(3):
            src[number, 3 + k] = scale * pushed[row : row + per_dev]
            row += per_dev


def pairs_kernel(stage, first, last, groups, per_dev, n_near, *refs):
    count = 2 if first and stage == 0 else 1
    given, refs = refs[:count], refs[count:]
    (stiffness, own, own_s), refs = refs[:3], refs[3:]
    if stage == 0:
        moving, fixed = [own], [own_s]
        (operator, out_tgt, feats, sums, out_layer), refs = refs[:5], refs[5:]
        centres = out_tgt.at[1]
        if first:
            loaded, refs = refs[:2], refs[2:]
    elif stage == 1:
        moving, fixed, refs = refs[:2], refs[2:4], refs[4:]
        (tgt, feats, sums_in, sums), refs = refs[:4], refs[4:]
        centres = tgt.at[1]
    else:
        moving, fixed, refs = refs[:1], refs[1:2], refs[2:]
        (tgt, feats, sums_in, layered), refs = refs[:4], refs[4:]
        centres = tgt.at[1]
        outs, refs = refs[: 3 if last else 1], refs[3 if last else 1 :]
    if first:
        count = 3 if stage == 0 else 1
        out_lists, refs = refs[:count], refs[count:]
    src, refs = refs[0], refs[1:]
    if stage == 2:
        sums, refs = refs[0], refs[1:]
    if first:
        lists, refs = refs[:count], refs[count:]
        meta, refs = refs[0], refs[1:]
    else:
        lists, refs = refs[:1], refs[1:]
    if first and stage == 0:
        (neighbours, near), refs = refs[:2], refs[2:]
        taken = neighbours, near
    else:
        taken = lists
    (sems,) = refs
    pairs = lists[0]
    points = src.shape[-1]
    held = [
        (*pair, *fixed_pair)
        for pair, fixed_pair in zip(
            [(ref, at) for ref in moving for at in range(ref.shape[0])],
            [(ref, at) for ref in fixed for at in range(ref.shape[0])],
        )
    ]
    blocks = len(held)
    dummy = 2 * blocks
    copies = [
        pltpu.make_async_copy(array, copy, sems.at[4 + number])
        for number, (array, copy) in enumerate(zip(given, taken))
    ]
    if first:
        start = 0
        for number, ref in enumerate(fixed):
            cells = pl.ds(start, ref.shape[0])
            copies.append(pltpu.make_async_copy(
                ref.at[:, 12, :, pl.ds(0, 128)], meta.at[cells], sems.at[number]))
            start += ref.shape[0]
    for copy in copies:
        copy.start()
    if first and stage == 0:
        loads = [
            pltpu.make_async_copy(array, copy, sems.at[2 + number])
            for number, (array, copy) in enumerate(zip((stiffness, operator), loaded))
        ]
        for load in loads:
            load.start()

    src[dummy] = jnp.zeros(src.shape[1:], f32)
    for number, (ref, at, fixed_ref, fixed_at) in enumerate(held):
        for k in range(3):
            src[number, k] = ref[at, k]
            src[blocks + number, k] = fixed_ref[fixed_at, 9 + k]
            src[blocks + number, 3 + k] = ref[at, 3 + k]
    if stage:
        fill_forces(held, stiffness, src)

    if stage == 0:
        for kind in range(2):
            for k in range(3):
                tile = (own[0, k], own_s[0, 9 + k])[kind]
                centre = jnp.mean(tile, axis=1, keepdims=True)
                out_tgt[1, kind, k] = jnp.broadcast_to(centre, tile.shape)
                out_tgt[0, kind, k] = tile - centre
        for kind in range(2):
            for local in range(per_dev):
                x = [out_tgt[0, kind, k, local : local + 1, :] for k in range(3)]
                feats[kind * per_dev + local] = target_features(x)
        sums[...] = jnp.zeros(sums.shape, f32)
    else:
        sums[...] = sums_in[...]
    for copy in copies:
        copy.wait()
    end = pairs.shape[0] - 1
    filled = None
    if first and stage == 0:
        counts = list_own(groups, per_dev, neighbours, near, meta, lists)
        for each_list, count in zip(lists, counts):
            each_list[end] = count
        filled = counts[0]
    elif first:
        filled = list_patches(groups, per_dev, blocks, n_near, meta, pairs, pairs[end])
        pairs[end] = filled
    else:
        filled = pairs[end]
    keeps = []
    if first:
        for extra in range(2):
            pairs[filled + extra] = encode(0, dummy, 0)
        keeps = [
            pltpu.make_async_copy(each_list, out, sems.at[6 + number])
            for number, (each_list, out) in enumerate(zip(lists, out_lists))
        ]
        for keep in keeps:
            keep.start()
    if stage == 0:
        if first:
            loads[0].wait()
            stiffness, operator = loaded
        fill_forces(held, stiffness, src)
    pair_loop(filled, pairs, src, centres, feats, sums, per_dev)
    if stage == 0:
        if first:
            loads[1].wait()
        for k, tile in enumerate(layer(own[0, 3:6], operator)):
            out_layer[k] = tile
    for keep in keeps:
        keep.wait()
    if stage < 2:
        return

    for local in range(per_dev):
        slot = slice(local, local + 1)
        velocity = combine(sums[local], [tgt[0, 0, k, slot, :] for k in range(3)])
        wall_velocity = combine(sums[per_dev + local], [tgt[0, 1, k, slot, :] for k in range(3)])
        for k in range(3):
            position = own[0, k, slot, :] + time_step * velocity[k]
            density = own[0, 3 + k, slot, :]
            density = density - relax_factor * (
                wall_velocity[k] + 0.5 * density + layered[k, slot, :]
            )
            if last:
                outs[0][k, slot, :] = position
                outs[1][k, slot, :] = velocity[k]
                outs[2][k, slot, :] = density
            else:
                outs[0][k, slot, :] = position
                outs[0][3 + k, slot, :] = density


def cell_blocks(block):
    groups = lax.axis_size("cell")
    return [block] + [
        lax.ppermute(
            block, "cell", [(i, pair_partner(i, shift, groups)) for i in range(groups)]
        )
        for shift in range(1, groups)
    ]


def paired(count):
    return [(i, i ^ 1) for i in range(count) if i ^ 1 < count]


def paired_next(count):
    pairs = [(i, i + 1 if i % 2 else i - 1) for i in range(count)]
    return [(i, j) for i, j in pairs if 0 <= j < count]


vmem = pl.BlockSpec(memory_space=pltpu.VMEM)
anywhere = pl.BlockSpec(memory_space=pl.ANY)
hbm = pl.BlockSpec(memory_space=pltpu.HBM)


def in_hbm(array):
    return pltpu.with_memory_space_constraint(array, pltpu.HBM)


def pack(modulus, seg_count, near, arrays):
    _, per_dev, points = arrays[0].shape
    return pl.pallas_call(
        pack_kernel,
        out_shape=jax.ShapeDtypeStruct((13, per_dev, points), f32),
        in_specs=[anywhere] * 3 + [hbm] * 4,
        out_specs=vmem,
        scratch_shapes=[
            pltpu.SemaphoreType.DMA((7,)),
            pltpu.SMEM(modulus.shape, f32),
            pltpu.SMEM(seg_count.shape, jnp.int32),
            pltpu.SMEM(near.shape, jnp.int32),
        ],
        compiler_params=pltpu.CompilerParams(vmem_limit_bytes=4 * 1024 * 1024),
        name="pack",
    )(in_hbm(modulus), seg_count, in_hbm(near), *map(in_hbm, arrays))


def join(parts, twice):
    shapes = [
        jax.ShapeDtypeStruct((len(parts) - less, *parts[0].shape), f32) for less in range(2 if twice else 1)
    ]
    return pl.pallas_call(
        functools.partial(join_kernel, len(parts)),
        out_shape=shapes,
        in_specs=[vmem] * len(parts),
        out_specs=[vmem] * len(shapes),
        compiler_params=pltpu.CompilerParams(vmem_limit_bytes=4 * 1024 * 1024),
        name="join",
    )(*parts)


def run_stage(stage, first, last, groups, per_dev, n_near, points, lists, entries, stiffness, own, arrays):
    blocks = (1, 2 * groups, groups)[stage]
    carried = [
        jax.ShapeDtypeStruct((2, 2, 3, per_dev, points), f32),
        jax.ShapeDtypeStruct((2 * per_dev, 48, points), bf16),
        jax.ShapeDtypeStruct((2 * per_dev, 24, points), f32),
    ]
    if stage == 0:
        shapes = carried + [jax.ShapeDtypeStruct((3, per_dev, points), f32)]
    elif stage == 1:
        shapes = carried[2:]
    elif last:
        shapes = [jax.ShapeDtypeStruct((3, per_dev, points), f32)] * 3
    else:
        shapes = [jax.ShapeDtypeStruct((6, per_dev, points), f32)]
    scratch = [pltpu.VMEM((2 * blocks + 1, 6, per_dev, points), f32)]
    if stage == 2:
        scratch.append(pltpu.VMEM(carried[2].shape, f32))
    size = -(-(entries + 4) // 128) * 128
    scratch += [pltpu.SMEM((size,), jnp.int32)] * (3 if first and stage == 0 else 1)
    if first:
        if stage == 0:
            shapes = shapes + [
                jax.ShapeDtypeStruct(array.shape, array.dtype) for array in (stiffness, arrays[0])
            ]
        shapes = shapes + [jax.ShapeDtypeStruct((size,), jnp.int32)] * (1 if stage else 3)
        scratch.append(pltpu.SMEM((blocks, per_dev, 128), f32))
        if stage == 0:
            scratch += [pltpu.SMEM(array.shape, jnp.int32) for array in lists]
    scratch.append(pltpu.SemaphoreType.DMA((9,)))
    load = first and stage == 0
    in_specs = [anywhere] * len(lists) + [hbm if load else vmem] + [vmem] * 2
    in_specs += [hbm if load else vmem] * len(arrays)
    if load:
        stiffness, arrays = in_hbm(stiffness), [in_hbm(array) for array in arrays]
    pair_count = (6, 2, 10)[stage]
    return pl.pallas_call(
        functools.partial(pairs_kernel, stage, first, last, groups, per_dev, n_near),
        out_shape=shapes,
        in_specs=in_specs,
        out_specs=[vmem] * len(shapes),
        scratch_shapes=scratch,
        cost_estimate=pl.CostEstimate(
            flops=pair_count * 2 * points * points * 512, transcendentals=0,
            bytes_accessed=1 << 20,
        ),
        compiler_params=pltpu.CompilerParams(vmem_limit_bytes=16 * 1024 * 1024),
        name=("own_pairs", "segment_pairs", "outer_pairs")[stage],
    )(*lists, stiffness, *own, *arrays)


def body(
    positions, rest_shape, modulus, stiffness, wall_points, density,
    wall_operator, seg_count, neighbours, near_patches,
):
    per_dev, _, points = positions.shape
    groups = lax.axis_size("cell")
    near = near_patches.T
    turn = lambda array: jnp.transpose(array, (1, 0, 2))
    positions, rest_shape, wall_points, density = map(
        turn, (positions, rest_shape, wall_points, density)
    )

    fixed = pack(modulus, seg_count, near, (positions, rest_shape, wall_points, density))
    moving = fixed
    lists = [(neighbours, near)]
    n_near = near.shape[0]
    entries = neighbours.size + near.size + 3 * groups * near.size
    segments = lax.axis_size("seg")
    for repeat in range(STEPS):
        first = repeat == 0
        last = repeat == STEPS - 1
        stage = functools.partial(
            run_stage, groups=groups, per_dev=per_dev, n_near=n_near, points=points, first=first,
            last=last, own=(moving[None], fixed[None]), entries=entries,
        )
        parts = cell_blocks(moving)
        tgt, feats, sums, layered, *more = stage(
            0, lists=lists[0], stiffness=stiffness, arrays=(wall_operator,)
        )
        if first:
            stiffness, wall_operator, *listed = more
            lists = [listed[:1], listed[1:2], listed[2:]]
        parts, sums = lax.optimization_barrier((parts, sums))
        window, *rest = join(parts, False)
        close = lax.ppermute(window, "seg", paired(segments))
        far_rest = lax.ppermute(window, "seg", paired_next(segments))
        if first:
            fixed_near, fixed_far = (window, close), (far_rest,)
        moving_far = (far_rest,)
        sums, *listed = stage(
            1, lists=lists[1], stiffness=stiffness,
            arrays=(window, close, *fixed_near, tgt, feats, sums),
        )
        outs = stage(
            2, lists=lists[2], stiffness=stiffness,
            arrays=(*moving_far, *fixed_far, tgt, feats, sums, layered),
        )
        if first:
            lists = [lists[0], listed, outs[1:]]
        moving = outs[0]
    return tuple(map(turn, outs))


def solution(mesh):
    both = P(("seg", "cell"), None, None)
    placed = (
        both, both, P(("seg", "cell")), P(), both, both, P(), P("seg"),
        P(("seg", "cell"), None), P(("seg", "cell"), None),
    )
    return jax.shard_map(
        body, mesh=mesh, in_specs=placed, out_specs=(both, both, both), check_vma=False
    )
```

```python
import functools

import jax
import jax.numpy as jnp
from jax import lax
from jax.experimental import pallas as pl
from jax.experimental.pallas import tpu as pltpu
from jax.sharding import PartitionSpec as P

soften_square = 0.25
stokes_factor = 0.039788735772973836
relax_factor = 0.5
time_step = 0.5
own_most = 4
bf16 = jnp.bfloat16
f32 = jnp.float32
STEPS = 2


def row_places(points):
    return lax.broadcasted_iota(jnp.int32, (8, points), 0)


def tall(row):
    return jnp.broadcast_to(row, (8, row.shape[1]))


def parts_of(value):
    first = value.astype(bf16).astype(f32)
    rest = value - first
    second = rest.astype(bf16).astype(f32)
    third = (rest - second).astype(bf16).astype(f32)
    return first, second, third


def two_parts(value):
    high = value.astype(bf16)
    return high, (value - high.astype(f32)).astype(bf16)


def target_features(x):
    points = x[0].shape[1]
    place = row_places(points)
    square = x[0] * x[0] + x[1] * x[1] + x[2] * x[2]
    rows = jnp.where(place == 3, 1.0, 0.0)
    for number, row in ((0, x[0]), (1, x[1]), (2, x[2]), (4, square)):
        rows = jnp.where(place == number, tall(row), rows)
    high, middle, low = parts_of(rows)
    return jnp.concatenate([high, middle, high, low, high, middle], axis=0).astype(bf16)


def source_rows(y, f):
    place = row_places(y[0].shape[1])
    low_half = place < 4
    lane = place & 3
    square = tall(y[0] * y[0] + y[1] * y[1] + y[2] * y[2])
    along = tall(-(y[0] * f[0] + y[1] * f[1] + y[2] * f[2]))
    y = [tall(row) for row in y]
    f = [tall(row) for row in f]
    points_one = jnp.where(lane == 0, y[0], jnp.where(lane == 1, y[1], jnp.where(lane == 2, y[2], 1.0)))
    source = jnp.where(
        place < 3, -2 * points_one,
        jnp.where(place == 3, square + soften_square, jnp.where(place == 4, 1.0, 0.0)),
    )
    high, middle, low = parts_of(source)
    wide = jnp.concatenate([high, high, middle, high, low, middle], axis=0).astype(bf16)
    one = jnp.where(low_half, f[0], f[1]) * points_one
    two = jnp.where(low_half, f[2], along) * points_one
    three = jnp.where(lane == 0, f[0], jnp.where(lane == 1, f[1], f[2])) * square
    moments = jnp.concatenate(two_parts(jnp.concatenate([one, two, three], axis=0)), axis=0)
    return wide.T, moments


def sums_of_pairs(fetch, count, precise):
    held = []

    def distance(unit):
        pair, half = divmod(unit, 2)
        if half == 0:
            y, f, features = fetch(pair)
            held.append((*source_rows(y, f), features))
        wide, _, features = held[pair]
        rows = wide.shape[0] // 2
        return jnp.dot(wide[half * rows : (half + 1) * rows], features, preferred_element_type=f32)

    def moment_sums(unit, distance):
        pair, half = divmod(unit, 2)
        inverse = lax.rsqrt(jnp.maximum(distance, soften_square))
        cubed = inverse * inverse * inverse
        moments = held[pair][1]
        rows = moments.shape[1] // 2
        moments = moments[:, half * rows : (half + 1) * rows]
        high, low = two_parts(cubed) if precise else (cubed.astype(bf16), None)
        sums = jnp.dot(moments, high, preferred_element_type=f32)
        sums = sums[0:24] + sums[24:48]
        if precise:
            sums = sums + jnp.dot(moments[0:24], low, preferred_element_type=f32)
        return sums

    ready = [distance(0), distance(1)]
    out = []
    for unit in range(2 * count):
        if unit + 2 < 2 * count:
            ready.append(distance(unit + 2))
        sums = moment_sums(unit, ready[unit])
        if unit % 2 == 0:
            first = sums
        else:
            out.append(first + sums)
    return out


def combine(sums, x):
    cross = [[sums[4 * m + k : 4 * m + k + 1] for k in range(3)] for m in range(3)]
    total = [sums[4 * m + 3 : 4 * m + 4] for m in range(3)]
    square = x[0] * x[0] + x[1] * x[1] + x[2] * x[2] + soften_square
    weight = x[0] * total[0] + x[1] * total[1] + x[2] * total[2] + sums[15:16]
    out = []
    for k in range(3):
        moment = x[0] * cross[0][k] + x[1] * cross[1][k] + x[2] * cross[2][k] + sums[12 + k : 13 + k]
        turned = x[0] * cross[k][0] + x[1] * cross[k][1] + x[2] * cross[k][2]
        direct = square * total[k] + sums[16 + k : 17 + k] - 2 * turned
        out.append(stokes_factor * (direct + x[k] * weight - moment))
    return out


def pack_kernel(*refs):
    modulus, count, near, positions, rest_shape, wall_points, density, out, sems = refs[:9]
    held = refs[9:]
    per_dev = positions.shape[1]
    copies = [
        pltpu.make_async_copy(array, target, sems.at[number])
        for number, (array, target) in enumerate(zip((modulus, count, near), held))
    ]
    for number, array in enumerate((positions, density, rest_shape, wall_points)):
        copies.append(pltpu.make_async_copy(array, out.at[pl.ds(3 * number, 3)], sems.at[3 + number]))
    for copy in copies:
        copy.start()
    for copy in copies:
        copy.wait()
    modulus, count, near = held
    shape = out.shape[1:]
    row = lax.broadcasted_iota(jnp.int32, shape, 0)
    lane = lax.broadcasted_iota(jnp.int32, shape, 1)
    table = jnp.zeros(shape, f32)
    first = lax.axis_index("cell") * per_dev
    for local in range(per_dev):
        alive = first + local < count[0]
        entries = [jnp.where(alive, modulus[local], 0.0)]
        entries += [jnp.where(alive, near[w, local] + 1, 0).astype(f32) for w in range(near.shape[0])]
        for number, entry in enumerate(entries):
            table = jnp.where(jnp.logical_and(row == local, lane == number), entry, table)
    out[12] = table


def join_kernel(count, *refs):
    parts, outs = refs[:count], refs[count:]
    for number, part in enumerate(parts):
        outs[0][number] = part[...]
        if len(outs) > 1 and number:
            outs[1][number - 1] = part[...]


def encode(target, block, local):
    return (target * 256 + block) * 16 + local


def pair_loop(filled, pairs, src, centres, feats, sums, per_dev, precise):
    def some(first, count):
        targets = []

        def fetch(part):
            code = pairs[first + part]
            local = code & 15
            block = (code >> 4) & 255
            target = code >> 12
            targets.append(target)
            kind = lax.div(target, per_dev)
            slot = lax.rem(target, per_dev)
            y = [
                src[block, k, pl.ds(local, 1), :] - centres[kind, k, pl.ds(slot, 1), :]
                for k in range(3)
            ]
            f = [src[block, 3 + k, pl.ds(local, 1), :] for k in range(3)]
            return y, f, feats[target]

        found = sums_of_pairs(fetch, count, precise)
        for target, value in zip(targets, found):
            sums[target] += value

    done = 0
    for count in (8, 4):
        steps = lax.div(filled - done + (1 if count == 4 else 0), count)

        def whole(step, carry, count=count, done=done):
            some(done + step * count, count)
            return carry

        lax.fori_loop(0, steps, whole, 0)
        done = done + steps * count

    @pl.when(done < filled)
    def _():
        some(done, 2)


def pair_partner(index, shift, groups):
    if groups & (groups - 1) == 0:
        return index ^ shift
    return (index + shift) % groups


def slot_of(member, other, groups):
    if groups & (groups - 1) == 0:
        return member ^ other
    return lax.rem(member - other + groups, groups)


def list_own(groups, per_dev, neighbours, near, meta, lists):
    n_list = neighbours.shape[1]
    n_near = near.shape[0]
    segment = lax.axis_index("seg")
    member = lax.axis_index("cell")
    seg_cells = groups * per_dev
    start = (segment - 1) * seg_cells
    close_side = 2 - 2 * lax.rem(segment, 2)
    filled = [jnp.int32(0)] * 3
    for local in range(per_dev):
        alive = meta[0, local, 0] != 0.0
        for n in range(n_list + n_near):
            wall = n >= n_list
            relative = (near[n - n_list, local] if wall else neighbours[local, n]) - start
            side = lax.div(relative, seg_cells)
            inside = lax.rem(relative, seg_cells)
            turn = slot_of(member, lax.div(inside, per_dev), groups)
            middle = side == 1
            close = side == close_side
            early = jnp.logical_and(jnp.logical_and(middle, turn == 0), filled[0] < own_most)
            inner = jnp.logical_or(middle, close)
            where = (
                early,
                jnp.logical_and(inner, jnp.logical_not(early)),
                jnp.logical_not(inner),
            )
            blocks = (0, turn + jnp.where(middle, 0, groups), turn)
            for stage, count in enumerate((1, 2 * groups, groups)):
                block = blocks[stage] + (count if wall else 0)
                lists[stage][filled[stage]] = encode(local, block, lax.rem(inside, per_dev))
                here = jnp.logical_and(alive, where[stage])
                filled[stage] = filled[stage] + here.astype(jnp.int32)
    return filled


def list_patches(groups, per_dev, blocks, n_near, meta, pairs, filled):
    seg_cells = groups * per_dev
    first = lax.axis_index("seg") * seg_cells + lax.axis_index("cell") * per_dev + 1

    def scan(block, filled):
        for local in range(per_dev):
            for w in range(n_near):
                patch = meta[block, local, 1 + w].astype(jnp.int32) - first
                mine = jnp.logical_and(patch >= 0, patch < per_dev)
                pairs[filled] = encode(per_dev + patch, block, local)
                filled = filled + mine.astype(jnp.int32)
        return filled

    return lax.fori_loop(0, blocks, scan, filled)


def layer(density, operator):
    _, per_dev, points = density.shape
    rows = jnp.concatenate([density[k] for k in range(3)] + [jnp.zeros((per_dev, points), f32)], axis=0)
    high, low = two_parts(rows)
    operator_high, operator_low = two_parts(operator[...])
    turned = functools.partial(
        lax.dot_general, dimension_numbers=(((1,), (1,)), ((), ())), preferred_element_type=f32
    )
    count = rows.shape[0]
    main = turned(jnp.concatenate([high, low], axis=0), operator_high)
    total = main[:count] + main[count:] + turned(high, operator_low)
    return [total[k * per_dev : (k + 1) * per_dev] for k in range(3)]


def fill_forces(held, stiffness, src):
    tiles = []
    for moving, at, fixed, fixed_at in held:
        for k in range(3):
            tiles.append(moving[at, k] - fixed[fixed_at, 6 + k])
    per_dev, points = tiles[0].shape
    rows = len(tiles) * per_dev
    if rows % 16:
        tiles.append(jnp.zeros((16 - rows % 16, points), f32))
    offset = jnp.concatenate(tiles, axis=0).astype(bf16)
    pushed = lax.dot_general(
        offset, stiffness[...], (((1,), (1,)), ((), ())), preferred_element_type=f32
    )
    row = 0
    for number, (_, _, fixed, fixed_at) in enumerate(held):
        scale = jnp.broadcast_to(fixed[fixed_at, 12][:, 0:1], (per_dev, points))
        for k in range(3):
            src[number, 3 + k] = scale * pushed[row : row + per_dev]
            row += per_dev


def pairs_kernel(stage, first, last, groups, per_dev, n_near, *refs):
    count = 2 if first and stage == 0 else 1
    given, refs = refs[:count], refs[count:]
    (stiffness, own, own_s), refs = refs[:3], refs[3:]
    if stage == 0:
        moving, fixed = [own], [own_s]
        (operator, out_tgt, feats, sums, out_layer), refs = refs[:5], refs[5:]
        centres = out_tgt.at[1]
        if first:
            loaded, refs = refs[:2], refs[2:]
    elif stage == 1:
        moving, fixed, refs = refs[:2], refs[2:4], refs[4:]
        (tgt, feats, sums_in, sums), refs = refs[:4], refs[4:]
        centres = tgt.at[1]
    else:
        moving, fixed, refs = refs[:1], refs[1:2], refs[2:]
        (tgt, feats, sums_in, layered), refs = refs[:4], refs[4:]
        centres = tgt.at[1]
        outs, refs = refs[: 3 if last else 1], refs[3 if last else 1 :]
    if first:
        count = 3 if stage == 0 else 1
        out_lists, refs = refs[:count], refs[count:]
    src, refs = refs[0], refs[1:]
    if stage == 2:
        sums, refs = refs[0], refs[1:]
    if first:
        lists, refs = refs[:count], refs[count:]
        meta, refs = refs[0], refs[1:]
    else:
        lists, refs = refs[:1], refs[1:]
    if first and stage == 0:
        (neighbours, near), refs = refs[:2], refs[2:]
        taken = neighbours, near
    else:
        taken = lists
    (sems,) = refs
    pairs = lists[0]
    points = src.shape[-1]
    held = [
        (*pair, *fixed_pair)
        for pair, fixed_pair in zip(
            [(ref, at) for ref in moving for at in range(ref.shape[0])],
            [(ref, at) for ref in fixed for at in range(ref.shape[0])],
        )
    ]
    blocks = len(held)
    dummy = 2 * blocks
    copies = [
        pltpu.make_async_copy(array, copy, sems.at[4 + number])
        for number, (array, copy) in enumerate(zip(given, taken))
    ]
    if first:
        start = 0
        for number, ref in enumerate(fixed):
            cells = pl.ds(start, ref.shape[0])
            copies.append(pltpu.make_async_copy(
                ref.at[:, 12, :, pl.ds(0, 128)], meta.at[cells], sems.at[number]))
            start += ref.shape[0]
    for copy in copies:
        copy.start()
    if first and stage == 0:
        loads = [
            pltpu.make_async_copy(array, copy, sems.at[2 + number])
            for number, (array, copy) in enumerate(zip((stiffness, operator), loaded))
        ]
        for load in loads:
            load.start()

    src[dummy] = jnp.zeros(src.shape[1:], f32)
    for number, (ref, at, fixed_ref, fixed_at) in enumerate(held):
        for k in range(3):
            src[number, k] = ref[at, k]
            src[blocks + number, k] = fixed_ref[fixed_at, 9 + k]
            src[blocks + number, 3 + k] = ref[at, 3 + k]
    if stage:
        fill_forces(held, stiffness, src)

    if stage == 0:
        for kind in range(2):
            for k in range(3):
                tile = (own[0, k], own_s[0, 9 + k])[kind]
                centre = jnp.mean(tile, axis=1, keepdims=True)
                out_tgt[1, kind, k] = jnp.broadcast_to(centre, tile.shape)
                out_tgt[0, kind, k] = tile - centre
        for kind in range(2):
            for local in range(per_dev):
                x = [out_tgt[0, kind, k, local : local + 1, :] for k in range(3)]
                feats[kind * per_dev + local] = target_features(x)
        sums[...] = jnp.zeros(sums.shape, f32)
    else:
        sums[...] = sums_in[...]
    for copy in copies:
        copy.wait()
    end = pairs.shape[0] - 1
    filled = None
    if first and stage == 0:
        counts = list_own(groups, per_dev, neighbours, near, meta, lists)
        for each_list, count in zip(lists, counts):
            each_list[end] = count
        filled = counts[0]
    elif first:
        filled = list_patches(groups, per_dev, blocks, n_near, meta, pairs, pairs[end])
        pairs[end] = filled
    else:
        filled = pairs[end]
    keeps = []
    if first:
        for extra in range(2):
            pairs[filled + extra] = encode(0, dummy, 0)
        keeps = [
            pltpu.make_async_copy(each_list, out, sems.at[6 + number])
            for number, (each_list, out) in enumerate(zip(lists, out_lists))
        ]
        for keep in keeps:
            keep.start()
    if stage == 0:
        if first:
            loads[0].wait()
            stiffness, operator = loaded
        fill_forces(held, stiffness, src)
    pair_loop(filled, pairs, src, centres, feats, sums, per_dev, not last)
    if stage == 0:
        if first:
            loads[1].wait()
        for k, tile in enumerate(layer(own[0, 3:6], operator)):
            out_layer[k] = tile
    for keep in keeps:
        keep.wait()
    if stage < 2:
        return

    for local in range(per_dev):
        slot = slice(local, local + 1)
        velocity = combine(sums[local], [tgt[0, 0, k, slot, :] for k in range(3)])
        wall_velocity = combine(sums[per_dev + local], [tgt[0, 1, k, slot, :] for k in range(3)])
        for k in range(3):
            position = own[0, k, slot, :] + time_step * velocity[k]
            density = own[0, 3 + k, slot, :]
            density = density - relax_factor * (
                wall_velocity[k] + 0.5 * density + layered[k, slot, :]
            )
            if last:
                outs[0][k, slot, :] = position
                outs[1][k, slot, :] = velocity[k]
                outs[2][k, slot, :] = density
            else:
                outs[0][k, slot, :] = position
                outs[0][3 + k, slot, :] = density


def cell_blocks(block):
    groups = lax.axis_size("cell")
    return [block] + [
        lax.ppermute(
            block, "cell", [(i, pair_partner(i, shift, groups)) for i in range(groups)]
        )
        for shift in range(1, groups)
    ]


def paired(count):
    return [(i, i ^ 1) for i in range(count) if i ^ 1 < count]


def paired_next(count):
    pairs = [(i, i + 1 if i % 2 else i - 1) for i in range(count)]
    return [(i, j) for i, j in pairs if 0 <= j < count]


vmem = pl.BlockSpec(memory_space=pltpu.VMEM)
anywhere = pl.BlockSpec(memory_space=pl.ANY)
hbm = pl.BlockSpec(memory_space=pltpu.HBM)


def in_hbm(array):
    return pltpu.with_memory_space_constraint(array, pltpu.HBM)


def pack(modulus, seg_count, near, arrays):
    _, per_dev, points = arrays[0].shape
    return pl.pallas_call(
        pack_kernel,
        out_shape=jax.ShapeDtypeStruct((13, per_dev, points), f32),
        in_specs=[anywhere] * 3 + [hbm] * 4,
        out_specs=vmem,
        scratch_shapes=[
            pltpu.SemaphoreType.DMA((7,)),
            pltpu.SMEM(modulus.shape, f32),
            pltpu.SMEM(seg_count.shape, jnp.int32),
            pltpu.SMEM(near.shape, jnp.int32),
        ],
        compiler_params=pltpu.CompilerParams(vmem_limit_bytes=4 * 1024 * 1024),
        name="pack",
    )(in_hbm(modulus), seg_count, in_hbm(near), *map(in_hbm, arrays))


def join(parts, twice):
    shapes = [
        jax.ShapeDtypeStruct((len(parts) - less, *parts[0].shape), f32) for less in range(2 if twice else 1)
    ]
    return pl.pallas_call(
        functools.partial(join_kernel, len(parts)),
        out_shape=shapes,
        in_specs=[vmem] * len(parts),
        out_specs=[vmem] * len(shapes),
        compiler_params=pltpu.CompilerParams(vmem_limit_bytes=4 * 1024 * 1024),
        name="join",
    )(*parts)


def run_stage(stage, first, last, groups, per_dev, n_near, points, lists, entries, stiffness, own, arrays):
    blocks = (1, 2 * groups, groups)[stage]
    carried = [
        jax.ShapeDtypeStruct((2, 2, 3, per_dev, points), f32),
        jax.ShapeDtypeStruct((2 * per_dev, 48, points), bf16),
        jax.ShapeDtypeStruct((2 * per_dev, 24, points), f32),
    ]
    if stage == 0:
        shapes = carried + [jax.ShapeDtypeStruct((3, per_dev, points), f32)]
    elif stage == 1:
        shapes = carried[2:]
    elif last:
        shapes = [jax.ShapeDtypeStruct((3, per_dev, points), f32)] * 3
    else:
        shapes = [jax.ShapeDtypeStruct((6, per_dev, points), f32)]
    scratch = [pltpu.VMEM((2 * blocks + 1, 6, per_dev, points), f32)]
    if stage == 2:
        scratch.append(pltpu.VMEM(carried[2].shape, f32))
    size = -(-(entries + 4) // 128) * 128
    scratch += [pltpu.SMEM((size,), jnp.int32)] * (3 if first and stage == 0 else 1)
    if first:
        if stage == 0:
            shapes = shapes + [
                jax.ShapeDtypeStruct(array.shape, array.dtype) for array in (stiffness, arrays[0])
            ]
        shapes = shapes + [jax.ShapeDtypeStruct((size,), jnp.int32)] * (1 if stage else 3)
        scratch.append(pltpu.SMEM((blocks, per_dev, 128), f32))
        if stage == 0:
            scratch += [pltpu.SMEM(array.shape, jnp.int32) for array in lists]
    scratch.append(pltpu.SemaphoreType.DMA((9,)))
    load = first and stage == 0
    in_specs = [anywhere] * len(lists) + [hbm if load else vmem] + [vmem] * 2
    in_specs += [hbm if load else vmem] * len(arrays)
    if load:
        stiffness, arrays = in_hbm(stiffness), [in_hbm(array) for array in arrays]
    pair_count = (6, 2, 10)[stage]
    return pl.pallas_call(
        functools.partial(pairs_kernel, stage, first, last, groups, per_dev, n_near),
        out_shape=shapes,
        in_specs=in_specs,
        out_specs=[vmem] * len(shapes),
        scratch_shapes=scratch,
        cost_estimate=pl.CostEstimate(
            flops=pair_count * 2 * points * points * 512, transcendentals=0,
            bytes_accessed=1 << 20,
        ),
        compiler_params=pltpu.CompilerParams(vmem_limit_bytes=16 * 1024 * 1024),
        name=("own_pairs", "segment_pairs", "outer_pairs")[stage],
    )(*lists, stiffness, *own, *arrays)


def body(
    positions, rest_shape, modulus, stiffness, wall_points, density,
    wall_operator, seg_count, neighbours, near_patches,
):
    per_dev, _, points = positions.shape
    groups = lax.axis_size("cell")
    near = near_patches.T
    turn = lambda array: jnp.transpose(array, (1, 0, 2))
    positions, rest_shape, wall_points, density = map(
        turn, (positions, rest_shape, wall_points, density)
    )

    fixed = pack(modulus, seg_count, near, (positions, rest_shape, wall_points, density))
    moving = fixed
    lists = [(neighbours, near)]
    n_near = near.shape[0]
    entries = neighbours.size + near.size + 3 * groups * near.size
    segments = lax.axis_size("seg")
    for repeat in range(STEPS):
        first = repeat == 0
        last = repeat == STEPS - 1
        stage = functools.partial(
            run_stage, groups=groups, per_dev=per_dev, n_near=n_near, points=points, first=first,
            last=last, own=(moving[None], fixed[None]), entries=entries,
        )
        parts = cell_blocks(moving)
        tgt, feats, sums, layered, *more = stage(
            0, lists=lists[0], stiffness=stiffness, arrays=(wall_operator,)
        )
        if first:
            stiffness, wall_operator, *listed = more
            lists = [listed[:1], listed[1:2], listed[2:]]
        parts, sums = lax.optimization_barrier((parts, sums))
        window, *rest = join(parts, False)
        close = lax.ppermute(window, "seg", paired(segments))
        far_rest = lax.ppermute(window, "seg", paired_next(segments))
        if first:
            fixed_near, fixed_far = (window, close), (far_rest,)
        moving_far = (far_rest,)
        sums, *listed = stage(
            1, lists=lists[1], stiffness=stiffness,
            arrays=(window, close, *fixed_near, tgt, feats, sums),
        )
        outs = stage(
            2, lists=lists[2], stiffness=stiffness,
            arrays=(*moving_far, *fixed_far, tgt, feats, sums, layered),
        )
        if first:
            lists = [lists[0], listed, outs[1:]]
        moving = outs[0]
    return tuple(map(turn, outs))


def solution(mesh):
    both = P(("seg", "cell"), None, None)
    placed = (
        both, both, P(("seg", "cell")), P(), both, both, P(), P("seg"),
        P(("seg", "cell"), None), P(("seg", "cell"), None),
    )
    return jax.shard_map(
        body, mesh=mesh, in_specs=placed, out_specs=(both, both, both), check_vma=False
    )
```
